32 devices in a mesh: groups: 2 (over y), replica: 4 (over z), sx: 4 (over x, core).
Axes of the slice: x: 2, y: 2, z: 4, core: 2. Of those that a mesh axis runs over, the one named last changes fastest.
Arguments:
- coords: float32 [3, 8, 4096], P(None, ('groups', 'replica'), 'sx'), parts along dimension 1, may hold values from 0 to 1
- widths: float32 [8, 4096], P(('groups', 'replica'), 'sx'), parts along dimension 0, may hold values from 1 to 2
- amplitudes: float32 [8, 4096], P(('groups', 'replica'), 'sx'), parts along dimension 0, may hold values from 1 to 4
- live_blocks: int32 [8, 4], P(('groups', 'replica'), 'sx'), parts along dimension 0, may hold values from 1 to 8, as said below
- target_map: float32 [192, 64, 480], P(('groups', 'sx')), parts along dimension 0, may hold values from -2 to 2
Outputs:
- mean_density: float32 [192, 64, 480], P(('groups', 'sx'), 'replica'), parts along dimension 0
- forces: float32 [3, 8, 4096], P(None, ('groups', 'replica'), 'sx'), parts along dimension 1
The draws below stay inside these ranges and needn't reach their ends.
There are 2 independent parts, one for each index of `groups`. The reference program is written for one: setup_inputs(seed, part) draws one part's arguments, and reference() takes and returns one part's arrays. A program takes and returns all parts, laid end to end along the dimension named above; each array names one. Nothing has to cross between parts.
Inputs may be any that keep to these rules, and one draw needn't show every extreme that they name: `live_blocks`: blocks past the count hold padding slots. Some member's brick has all 8 blocks in use in every draw.
All inputs are finite; a program needn't handle non-finite values.
Results may differ from the reference program's by a relative error of at most 0.0044.
Values may be sent and summed in bfloat16 or wider, within the bound.
No kernel may reach another device: no remote copies, remote signals or barrier semaphores. Data moves between devices by JAX's collectives and lax.ppermute only.
A program may use at most 64 MiB of HBM per device.

```python
import math
import jax
import jax.numpy as jnp
from jax import lax

CX = 24
NZ = 64
NY = 480
REACH = 6
BLOCK = 128
BLOCKS = 8
ATOMS_DEV = 1024
SLOTS = 4096
REPLICAS = 4
NX = 96
SPAN = 36
N_REPLICA = 4
N_SX = 4


def draw_live_blocks(key, part):
    key = jax.random.fold_in(key, 7)
    first_key, second_key, third_key = jax.random.split(key, 3)
    bricks = NX // CX
    grid_shape = (REPLICAS, bricks)
    first_draw = jax.random.randint(first_key, grid_shape, 0, BLOCKS)
    second_draw = jax.random.randint(second_key, grid_shape, 0, BLOCKS)
    counts = 1 + first_draw * second_draw // (BLOCKS - 1)
    chosen = jax.random.randint(third_key, (), 0, REPLICAS * bricks)
    flat_index = jnp.arange(REPLICAS * bricks).reshape(grid_shape)
    return jnp.where(flat_index == chosen, BLOCKS, counts).astype(jnp.int32)


def block_scale(own_key, dims, pieces, least, high):
    level = 1.0
    for dim, blocks in pieces:
        draws = jax.random.uniform(jax.random.fold_in(jax.random.fold_in(own_key, 6), dim), (blocks,), jnp.float32, least / len(pieces), high / len(pieces))
        level = level * jnp.repeat(jnp.exp(draws), dims[dim] // blocks).reshape((-1,) + (1,) * (len(dims) - 1 - dim))
    return level


def gaussian(stream_key, shape, deviation, reach, shards=(), kind=jnp.bfloat16):
    array = jax.random.normal(stream_key, shape, jnp.float32) * deviation
    if len(shards) > 0:
        array = block_scale(stream_key, shape, shards, -0.22, 0.18) * array
    return jnp.clip(array, min=-reach, max=reach).astype(kind)


def setup_inputs(seed: int = 0, part: int = 0) -> dict:
    key_of = jax.random.split(jax.random.key(seed), 6)
    own_keys = jax.random.split(jax.random.fold_in(key_of[5], part), 6)
    coords = jnp.clip(1.0 * jax.random.uniform(own_keys[0], (3, REPLICAS, SLOTS), jnp.float32) ** block_scale(own_keys[0], (3, REPLICAS, SLOTS), ((1, 4), (2, 4)), -0.2, 0.2), 0.0, 1.0)
    widths = jnp.clip(jnp.exp(math.log(2.0) - 0.6931472 * jax.random.uniform(own_keys[1], (REPLICAS, SLOTS), jnp.float32) ** block_scale(own_keys[1], (REPLICAS, SLOTS), ((0, 4), (1, 4)), -0.2, 0.2)), 1.0, 2.0)
    amplitudes = jnp.clip(jnp.exp(math.log(4.0) - 1.3862944 * jax.random.uniform(own_keys[2], (REPLICAS, SLOTS), jnp.float32) ** block_scale(own_keys[2], (REPLICAS, SLOTS), ((0, 4), (1, 4)), -0.2, 0.2)), 1.0, 4.0)
    live_blocks = draw_live_blocks(jax.random.fold_in(jax.random.fold_in(key_of[5], part), 71), part)
    target_map = gaussian(own_keys[4], (NX, NZ, NY), 0.3, 2.0, ((0, 4),), jnp.float32)
    return {"coords": coords, "widths": widths, "amplitudes": amplitudes, "live_blocks": live_blocks, "target_map": target_map}


noise_floor = 0.05


def atom_tables(fraction, radius, amplitude, alive_mask, anchor, total_x):
    pos_x = anchor + CX * fraction[0]
    pos_y = NY * fraction[1]
    pos_z = NZ * fraction[2]
    inv_var = 1.0 / (radius * radius)
    cells_x = anchor - REACH + jnp.arange(SPAN).astype(jnp.float32)
    inside = ((cells_x >= 0.0) & (cells_x < total_x)).astype(jnp.float32)
    off_x = cells_x[None, :] - pos_x[:, None]
    off_y = jnp.arange(NY).astype(jnp.float32)[None, :] - pos_y[:, None]
    off_z = jnp.arange(NZ).astype(jnp.float32)[None, :] - pos_z[:, None]
    scale = inv_var[:, None]
    gauss_x = jnp.exp(-0.5 * off_x * off_x * scale) * inside[None, :]
    gauss_y = jnp.exp(-0.5 * off_y * off_y * scale)
    gauss_z = jnp.exp(-0.5 * off_z * off_z * scale)
    weight = amplitude * alive_mask
    return (weight, gauss_x, gauss_x * off_x * scale, gauss_y, gauss_y * off_y * scale,
            gauss_z, gauss_z * off_z * scale)


def splat_window(weight, gauss_x, gauss_z, gauss_y):
    left_table = (weight[:, None, None] * gauss_x[:, :, None] * gauss_z[:, None, :]).astype(jnp.bfloat16)
    left_table = left_table.reshape(weight.shape[0], SPAN * NZ)
    return lax.dot_general(left_table, gauss_y.astype(jnp.bfloat16), (((0,), (0,)), ((), ())),
                           preferred_element_type=jnp.float32)


def pull_forces(grad_field, weight, gauss_x, slope_x, gauss_y, slope_y, gauss_z, slope_z):
    contract = (((1,), (1,)), ((), ()))
    pulled = lax.dot_general(grad_field, gauss_y.astype(jnp.bfloat16), contract,
                             preferred_element_type=jnp.float32).reshape(SPAN, NZ, -1)
    slanted = lax.dot_general(grad_field, slope_y.astype(jnp.bfloat16), contract,
                              preferred_element_type=jnp.float32).reshape(SPAN, NZ, -1)
    highest = lax.Precision.HIGHEST
    force_x = weight * jnp.einsum('xza,ax,az->a', pulled, slope_x, gauss_z, precision=highest)
    force_y = weight * jnp.einsum('xza,ax,az->a', slanted, gauss_x, gauss_z, precision=highest)
    force_z = weight * jnp.einsum('xza,ax,az->a', pulled, gauss_x, slope_z, precision=highest)
    return jnp.stack([force_x, force_y, force_z])


def moments(first, second, target, members):
    ens_mean = first / members
    spread = second / members - ens_mean * ens_mean
    noise_var = noise_floor + spread / members
    residual = target - ens_mean
    drive_term = -residual / (noise_var * members)
    gain_term = (1.0 / noise_var - residual * residual / (noise_var * noise_var)) / (members * members)
    return ens_mean, drive_term - gain_term * ens_mean, gain_term


def brick_tables(fraction, radius, amplitude, live_count, brick_index, total_x):
    lower = brick_index * ATOMS_DEV
    upper = lower + ATOMS_DEV
    slot_block = (jnp.arange(ATOMS_DEV) // BLOCK).astype(jnp.int32)
    alive_mask = (slot_block < live_count[brick_index]).astype(jnp.float32)
    anchor = jnp.asarray(brick_index * CX).astype(jnp.float32)
    return atom_tables(fraction[:, lower:upper], radius[lower:upper], amplitude[lower:upper],
                       alive_mask, anchor, total_x)


def replica_density(fraction, radius, amplitude, live_count):
    total_x = CX * N_SX
    padded = jnp.zeros((total_x + 2 * REACH, NZ, NY), jnp.float32)
    for brick_index in range(N_SX):
        tables = brick_tables(fraction, radius, amplitude, live_count, brick_index, total_x)
        window = splat_window(tables[0], tables[1], tables[5], tables[3]).reshape(SPAN, NZ, NY)
        padded = padded.at[brick_index * CX:brick_index * CX + SPAN].add(window)
    return padded[REACH:REACH + total_x]


def replica_forces(fraction, radius, amplitude, live_count, density, offset_term, gain_term):
    total_x = CX * N_SX
    gradient = (offset_term + gain_term * density).astype(jnp.bfloat16)
    padded = jnp.pad(gradient, ((REACH, REACH), (0, 0), (0, 0)))
    results = []
    for brick_index in range(N_SX):
        tables = brick_tables(fraction, radius, amplitude, live_count, brick_index, total_x)
        grad_field = padded[brick_index * CX:brick_index * CX + SPAN].reshape(SPAN * NZ, NY)
        results.append(pull_forces(grad_field, *tables))
    return jnp.concatenate(results, 1)


def reference(coords, widths, amplitudes, live_blocks, target_map):
    moved = jnp.transpose(coords, (1, 0, 2))
    density = lax.map(lambda member_data: replica_density(*member_data),
                      (moved, widths, amplitudes, live_blocks))
    first = jnp.sum(density, 0)
    second = jnp.sum(density * density, 0)
    ens_mean, offset_term, gain_term = moments(first, second, target_map, N_REPLICA)
    forces = lax.map(lambda member_data: replica_forces(*member_data, offset_term, gain_term),
                     (moved, widths, amplitudes, live_blocks, density))
    return ens_mean, jnp.transpose(forces, (1, 0, 2))
```

```python
import functools
import math

import jax
import jax.numpy as jnp
from jax import lax
from jax.experimental import pallas as pl
from jax.experimental.pallas import tpu as pltpu
from jax.sharding import PartitionSpec as P

CX = 24
NZ = 64
NY = 480
REACH = 6
BLOCK = 128
ATOMS_DEV = 1024
SPAN = CX + 2 * REACH
LAP = 2 * REACH
CHUNK = 2 * BLOCK
LANES = 512
FIELDS = 8
HALF_LOG2E = 0.5 * math.log2(math.e)

noise_floor = 0.05


def refine_kernel(
    members, zp, zs, sliced, place_ref, atoms_ref, below_ref, above_ref, target_ref,
    mean_ref, forces_ref, rho, grad, wanted, gy, pulled, rows, sem,
):
    z_first = place_ref[0] * zs
    brick = place_ref[1]
    last_plane = place_ref[2]

    if sliced:
        source = target_ref.at[:, pl.ds(pl.multiple_of(z_first, 8), zp), :]
    else:
        source = target_ref
    fetch = pltpu.make_async_copy(source, wanted.at[pl.ds(REACH, CX)], sem)
    fetch.start()
    wanted[0:REACH] = below_ref[...]
    wanted[REACH + CX :] = above_ref[...]
    rho[...] = jnp.zeros_like(rho)
    grad[...] = jnp.zeros_like(grad)
    gy[NY:, :] = jnp.zeros((LANES - NY, 2 * CHUNK), jnp.bfloat16)
    forces_ref[...] = jnp.zeros_like(forces_ref)

    step = lax.broadcasted_iota(jnp.int32, (16, CHUNK), 0).astype(jnp.float32)
    step_z = lax.broadcasted_iota(jnp.int32, (zp, CHUNK), 0)
    own_z = (step_z < zs).astype(jnp.float32)
    cell_z = (step_z + z_first).astype(jnp.float32)

    def chunks_of(member, side):
        count = jnp.max(atoms_ref[member, side, 5:6, 0:BLOCK]).astype(jnp.int32)
        return (count + 1) // 2

    def fields(member, side, chunk):
        cols = pl.ds(pl.multiple_of(chunk * CHUNK, CHUNK), CHUNK)
        data = atoms_ref[member, side, :, cols]
        inv = 1.0 / data[3:4]
        q = inv * inv
        return data[0:1], data[1:2], data[2:3], q, q * -HALF_LOG2E, data[4:5], cols

    def table_y(frac, power, q, slopes):
        base = step - NY * frac
        for k in range(NY // 16):
            off = base + float(16 * k)
            value = jnp.exp2(off * off * power)
            gy[16 * k : 16 * k + 16, 0:CHUNK] = value.astype(jnp.bfloat16)
            if slopes:
                gy[16 * k : 16 * k + 16, CHUNK:] = (value * (off * q)).astype(jnp.bfloat16)

    def table_x(frac, power, shift, lower, count):
        cell = lax.broadcasted_iota(jnp.int32, (count, CHUNK), 0) + lower
        plane = cell + (brick * CX - REACH)
        inside = ((plane >= 0) & (plane < last_plane)).astype(jnp.float32)
        off = cell.astype(jnp.float32) - (CX * frac + shift)
        return jnp.exp2(off * off * power) * inside, off

    def table_z(frac, power):
        off = cell_z - NZ * frac
        return jnp.exp2(off * off * power) * own_z, off

    def splat(side, shift, lower, count):
        def one_member(member, carry):
            def one_chunk(chunk, inner):
                frac_x, frac_y, frac_z, q, power, weight, cols = fields(member, side, chunk)
                gx, _ = table_x(frac_x, power, shift, lower, count)
                gz, _ = table_z(frac_z, power)
                table_y(frac_y, power, q, False)
                left = (weight * gx)[:, None, :] * gz[None, :, :]
                left = left.reshape(count * zp, CHUNK).astype(jnp.bfloat16)
                add = lax.dot_general(
                    left, gy[:, 0:CHUNK], (((1,), (1,)), ((), ())),
                    preferred_element_type=jnp.float32,
                )
                rho[member, lower * zp : (lower + count) * zp, :] += add
                return inner

            return lax.fori_loop(0, chunks_of(member, side), one_chunk, carry)

        lax.fori_loop(0, members, one_member, 0)

    splat(1, REACH, 0, SPAN)
    splat(0, REACH - CX, 0, LAP)
    splat(2, REACH + CX, CX, LAP)

    fetch.wait()

    group = max(1, 16 // zp)

    def gradient(t, carry):
        at = pl.ds(pl.multiple_of(t * group * zp, 16), group * zp)
        planes = pl.ds(t * group, group)
        fields_here = [rho[m, at, 0:NY] for m in range(members)]
        first = functools.reduce(jnp.add, fields_here)
        second = functools.reduce(jnp.add, [f * f for f in fields_here])
        mean = first * (1.0 / members)
        spread = second * (1.0 / members) - mean * mean
        inv = 1.0 / (noise_floor + spread * (1.0 / members))
        pull = (wanted[planes].reshape(group * zp, NY) - mean) * inv
        gain = (inv - pull * pull) * (1.0 / (members * members))
        offset = pull * (-1.0 / members) - gain * mean
        for m in range(members):
            grad[m, at, 0:NY] = (offset + gain * fields_here[m]).astype(jnp.bfloat16)

        @pl.when((t * group >= REACH) & (t * group < REACH + CX))
        def _():
            mean_ref[pl.ds(t * group - REACH, group)] = mean.reshape(group, zp, NY)

        return carry

    lax.fori_loop(0, SPAN // group, gradient, 0)

    def pull_member(member, carry):
        def one_chunk(chunk, inner):
            frac_x, frac_y, frac_z, q, power, weight, cols = fields(member, 1, chunk)
            gx, off_x = table_x(frac_x, power, REACH, 0, SPAN)
            gz, off_z = table_z(frac_z, power)
            rows[0:SPAN] = gx
            rows[SPAN : 2 * SPAN] = gx * off_x * q
            table_y(frac_y, power, q, True)
            pulled[...] = jnp.dot(grad[member], gy[...], preferred_element_type=jnp.float32)
            sum_x = jnp.zeros((zp, CHUNK), jnp.float32)
            sum_y = jnp.zeros((zp, CHUNK), jnp.float32)
            sum_z = jnp.zeros((zp, CHUNK), jnp.float32)
            for t in range(SPAN):
                plain = pulled[t * zp : (t + 1) * zp, 0:CHUNK]
                slanted = pulled[t * zp : (t + 1) * zp, CHUNK:]
                here = rows[t : t + 1]
                sum_x += rows[SPAN + t : SPAN + t + 1] * plain
                sum_y += here * slanted
                sum_z += here * plain
            force_x = weight * jnp.sum(sum_x * gz, 0, keepdims=True)
            force_y = weight * jnp.sum(sum_y * gz, 0, keepdims=True)
            force_z = weight * jnp.sum(sum_z * (gz * off_z * q), 0, keepdims=True)
            forces_ref[member, 0:1, cols] = force_x
            forces_ref[member, 1:2, cols] = force_y
            forces_ref[member, 2:3, cols] = force_z
            return inner

        return lax.fori_loop(0, chunks_of(member, 1), one_chunk, carry)

    lax.fori_loop(0, members, pull_member, 0)


def shards(coords, widths, amplitudes, live_blocks, target_map):
    members = lax.axis_size("replica")
    bricks = lax.axis_size("sx")
    rank = lax.axis_index("replica")
    zs = NZ // members
    zp = max(zs, 8)
    sliced = zs % 8 == 0
    up = [(i, i + 1) for i in range(bricks - 1)]
    down = [(i + 1, i) for i in range(bricks - 1)]

    live = live_blocks[0, 0]
    alive = (jnp.arange(ATOMS_DEV) // BLOCK < live).astype(jnp.float32)
    own = jnp.concatenate(
        [
            coords[:, 0, :],
            widths,
            amplitudes * alive[None, :],
            jnp.broadcast_to(live.astype(jnp.float32), (FIELDS - 5, ATOMS_DEV)),
        ],
        0,
    )
    shifts = [[(i, (i + k) % members) for i in range(members)] for k in range(members)]
    if members <= 4:
        everyone = jnp.stack([own] + [lax.ppermute(own, "replica", p) for p in shifts[1:]])
    else:
        everyone = lax.all_gather(own, "replica")
    low = lax.ppermute(everyone, "sx", up)
    high = lax.ppermute(everyone, "sx", down)
    atoms = jnp.stack([low, everyone, high], 1)

    def share(block):
        part = lax.dynamic_slice_in_dim(block, rank * zs, zs, 1)
        return jnp.pad(part, ((0, 0), (0, zp - zs), (0, 0)))

    below = lax.ppermute(share(target_map[CX - REACH :]), "sx", up)
    above = lax.ppermute(share(target_map[:REACH]), "sx", down)
    target = target_map if sliced else share(target_map)
    place = jnp.stack([rank, lax.axis_index("sx"), CX * bricks]).astype(jnp.int32)

    vmem = pl.BlockSpec(memory_space=pltpu.VMEM)
    mean, partial = pl.pallas_call(
        functools.partial(refine_kernel, members, zp, zs, sliced),
        out_shape=(
            jax.ShapeDtypeStruct((CX, zp, NY), jnp.float32),
            jax.ShapeDtypeStruct((members, FIELDS, ATOMS_DEV), jnp.float32),
        ),
        in_specs=[pl.BlockSpec(memory_space=pltpu.SMEM), vmem, vmem, vmem, pl.BlockSpec(memory_space=pl.ANY)],
        out_specs=(vmem, vmem),
        scratch_shapes=[
            pltpu.VMEM((members, SPAN * zp, LANES), jnp.float32),
            pltpu.VMEM((members, SPAN * zp, LANES), jnp.bfloat16),
            pltpu.VMEM((SPAN, zp, NY), jnp.float32),
            pltpu.VMEM((LANES, 2 * CHUNK), jnp.bfloat16),
            pltpu.VMEM((SPAN * zp, 2 * CHUNK), jnp.float32),
            pltpu.VMEM((2 * SPAN, CHUNK), jnp.float32),
            pltpu.SemaphoreType.DMA,
        ],
        compiler_params=pltpu.CompilerParams(vmem_limit_bytes=60 * 1024 * 1024),
        name="refine",
    )(place, atoms, below, above, target)

    partial = partial[:, :3]
    if members <= 4:
        forces = partial[0]
        for k in range(1, members):
            back = [(target_rank, source) for source, target_rank in shifts[k]]
            forces = forces + lax.ppermute(partial[k], "replica", back)
    else:
        forces = lax.psum_scatter(partial, "replica", scatter_dimension=0)
    return mean[:, :zs], forces[:, None, :]


def solution(mesh):
    placed = (
        P(None, ("groups", "replica"), "sx"),
        P(("groups", "replica"), "sx"),
        P(("groups", "replica"), "sx"),
        P(("groups", "replica"), "sx"),
        P(("groups", "sx"), None, None),
    )
    return jax.shard_map(
        shards,
        mesh=mesh,
        in_specs=placed,
        out_specs=(P(("groups", "sx"), "replica", None), P(None, ("groups", "replica"), "sx")),
        check_vma=False,
    )
```

```python
import functools
import math

import jax
import jax.numpy as jnp
from jax import lax
from jax.experimental import pallas as pl
from jax.experimental.pallas import tpu as pltpu
from jax.sharding import PartitionSpec as P

CX = 24
NZ = 64
NY = 480
REACH = 6
BLOCK = 128
BLOCKS = 8
ATOMS_DEV = 1024
SPAN = CX + 2 * REACH
LAP = 2 * REACH
LANES = 512
FIELDS = 5
HALF_LOG2E = 0.5 * math.log2(math.e)
STASH_LIMIT = 4

noise_floor = 0.05


def pack_kernel(
    zs, sliced, coords_ref, widths_ref, amplitudes_ref, live_ref, target_ref,
    own_ref, first_ref, second_ref, sems,
):
    odd = lax.rem(lax.axis_index("sx"), 2)
    planes = (CX - REACH) * (1 - odd), (CX - REACH) * odd
    copies = []
    for k, (plane, out) in enumerate(zip(planes, (first_ref, second_ref))):
        if sliced:
            z_first = pl.multiple_of(lax.axis_index("replica") * zs, 8)
            source = target_ref.at[pl.ds(plane, REACH), pl.ds(z_first, zs), :]
        else:
            source = target_ref.at[pl.ds(plane, REACH)]
        copies.append(pltpu.make_async_copy(source, out, sems.at[k]))
        copies[-1].start()
    block = lax.broadcasted_iota(jnp.int32, (BLOCKS, BLOCK), 0)
    own_ref[0:3] = coords_ref[...]
    own_ref[3] = widths_ref[...]
    own_ref[4] = jnp.where(block < live_ref[0, 0], amplitudes_ref[...], 0.0)
    for copy in copies:
        copy.wait()


def refine_kernel(
    members, zp, zs, sliced, stash, atoms_ref, near_ref, far_ref, near_target, far_target,
    target_ref, mean_ref, *rest,
):
    outs = rest[: len(rest) - 13]
    (rho, grad, wanted, mean_vmem, gy, gy_side, left, left_side, pulled, rows, forces, order, sems) = rest[
        len(outs) :
    ]
    rank = lax.axis_index("replica")
    brick = lax.axis_index("sx")
    last_plane = CX * lax.axis_size("sx")
    odd = lax.rem(brick, 2)
    slots = members * BLOCKS

    if sliced:
        z_first = rank * zs
        source = target_ref.at[:, pl.ds(pl.multiple_of(z_first, 8), zs), :]
    else:
        z_first = rank * zs
        source = target_ref
    fetches = [
        pltpu.make_async_copy(source, wanted.at[pl.ds(REACH, CX)], sems.at[0]),
        pltpu.make_async_copy(
            near_target, wanted.at[pl.ds((REACH + CX) * (1 - odd), REACH)], sems.at[1]
        ),
        pltpu.make_async_copy(far_target, wanted.at[pl.ds((REACH + CX) * odd, REACH)], sems.at[2]),
    ]
    for fetch in fetches:
        fetch.start()

    block_number = (lax.broadcasted_iota(jnp.int32, (BLOCKS, BLOCK), 0) + 1).astype(jnp.float32)

    def live_of(ref, member):
        return jnp.max(jnp.where(ref[member, 4] != 0.0, block_number, 0.0)).astype(jnp.int32)

    def listed(ref, start, base, filled):
        def one_member(member, count):
            def one(block, inner):
                order[inner] = base + member * BLOCKS + block
                return inner + 1

            return lax.fori_loop(start, live_of(ref, member), one, count)

        return lax.fori_loop(0, members, one_member, filled, unroll=members <= 4)

    def first_block(member, carry):
        order[member] = member * BLOCKS
        return carry

    lax.fori_loop(0, members, first_block, 0)
    own_count = listed(atoms_ref, 1, 0, members)
    side_first = slots
    side_near = listed(near_ref, 0, 0, side_first)
    side_count = listed(far_ref, 0, slots, side_near) - side_first

    forces[...] = jnp.zeros_like(forces)
    grad[:, :, NY - 96 :] = jnp.zeros((members, SPAN * zp, LANES - NY + 96), jnp.bfloat16)
    for k in range(gy.shape[0]):
        gy[k, NY:, :] = jnp.zeros((LANES - NY, 2 * BLOCK), jnp.bfloat16)
    for k in range(2):
        gy_side[k, NY:, :] = jnp.zeros((LANES - NY, BLOCK), jnp.bfloat16)

    step = lax.broadcasted_iota(jnp.int32, (16, BLOCK), 0).astype(jnp.float32)
    step_z = lax.broadcasted_iota(jnp.int32, (zp, BLOCK), 0)
    own_z = (step_z < zs).astype(jnp.float32)
    cell_z = (step_z + z_first).astype(jnp.float32)

    def fields(ref, member, block):
        data = [ref[member, f, pl.ds(block, 1), :] for f in range(FIELDS)]
        inv = 1.0 / data[3]
        q = inv * inv
        return data[0], data[1], data[2], q, q * -HALF_LOG2E, data[4]

    def table_y(out, frac, power, q, slopes):
        base = step - NY * frac
        for k in range(NY // 16):
            off = base + float(16 * k)
            value = jnp.exp2(off * off * power)
            out[16 * k : 16 * k + 16, 0:BLOCK] = value.astype(jnp.bfloat16)
            if slopes:
                out[16 * k : 16 * k + 16, BLOCK:] = (value * (off * q)).astype(jnp.bfloat16)

    def table_x(frac, power, shift, lower, count, edges):
        cell = lax.broadcasted_iota(jnp.int32, (count, BLOCK), 0) + lower
        off = cell.astype(jnp.float32) - (CX * frac + shift)
        value = jnp.exp2(off * off * power)
        if edges:
            plane = cell + (brick * CX - REACH)
            value = jnp.where((plane >= 0) & (plane < last_plane), value, 0.0)
        return value, off

    def table_z(frac, power):
        off = cell_z - NZ * frac
        value = jnp.exp2(off * off * power)
        return (value if zs == zp else value * own_z), off

    def fill_left(out, scaled, gz, count, part):
        rows[part, 0:count] = scaled
        group = max(1, 16 // zp)
        for t in range(0, count, group):
            pieces = [rows[part, t + i : t + i + 1] * gz for i in range(group)]
            piece = pieces[0] if group == 1 else jnp.concatenate(pieces, 0)
            out[t * zp : (t + group) * zp] = piece.astype(jnp.bfloat16)

    def matmul_t(a, b):
        return lax.dot_general(a, b, (((1,), (1,)), ((), ())), preferred_element_type=jnp.float32)

    def own_splat(unit, slot, part, keep, fresh):
        code = order[unit]
        member, block = code // BLOCKS, lax.rem(code, BLOCKS)
        frac_x, frac_y, frac_z, q, power, weight = fields(atoms_ref, member, block)
        gx, _ = table_x(frac_x, power, REACH, 0, SPAN, True)
        gz, _ = table_z(frac_z, power)
        table_y(gy.at[slot], frac_y, power, q, stash)
        fill_left(left.at[part], weight * keep * gx, gz, SPAN, part)
        add = matmul_t(left[part], gy[slot, :, 0:BLOCK])
        return member, add

    def start_members(pair, carry):
        for part in range(2):
            unit = 2 * pair + part
            member, add = own_splat(unit, unit if stash else part, part, 1.0, True)
            rho[member] = add
        return carry

    lax.fori_loop(0, members // 2, start_members, 0)

    def more_blocks(pair, carry):
        done = []
        for part in range(2):
            unit = members + 2 * pair + part
            keep = jnp.where(unit < own_count, 1.0, 0.0)
            at = jnp.minimum(unit, own_count - 1)
            done.append(own_splat(at, at if stash else part, part, keep, False))
        for member, add in done:
            rho[member] += add
        return carry

    lax.fori_loop(0, (own_count - members + 1) // 2, more_blocks, 0)

    def side_blocks(ref, base, above):
        lower = CX * above
        shift = REACH - CX + 2 * CX * above

        def one_pair(pair, carry):
            done = []
            for part in range(2):
                unit = 2 * pair + part
                keep = jnp.where(unit < base[1], 1.0, 0.0)
                code = order[side_first + jnp.minimum(unit, base[1] - 1)] - base[2]
                member, block = code // BLOCKS, lax.rem(code, BLOCKS)
                frac_x, frac_y, frac_z, q, power, weight = fields(ref, member, block)
                gx, _ = table_x(
                    frac_x, power, shift.astype(jnp.float32), lower, LAP, False
                )
                gz, _ = table_z(frac_z, power)
                table_y(gy_side.at[part], frac_y, power, q, False)
                fill_left(left_side.at[part], weight * keep * gx, gz, LAP, part)
                done.append((member, matmul_t(left_side[part], gy_side[part])))
            for member, add in done:
                at = pl.ds(pl.multiple_of(lower * zp, 16), LAP * zp)
                rho[member, at, :] += add
            return carry

        lax.fori_loop(base[0] // 2, (base[1] + 1) // 2, one_pair, 0)

    near_count = side_near - side_first
    side_blocks(near_ref, (0, near_count, 0), 1 - odd)
    side_first = side_near
    side_blocks(far_ref, (0, side_count - near_count, slots), odd)

    for fetch in fetches:
        fetch.wait()

    group = max(1, 16 // zp)

    def gradient(t, carry):
        at = pl.ds(pl.multiple_of(t * group * zp, 16), group * zp)
        planes = pl.ds(t * group, group)
        here = [rho[m, at, 0:NY] for m in range(members)]
        first = functools.reduce(jnp.add, here)
        second = functools.reduce(jnp.add, [f * f for f in here])
        mean = first * (1.0 / members)
        spread = second * (1.0 / members) - mean * mean
        inv = 1.0 / (noise_floor + spread * (1.0 / members))
        pull = (wanted[planes].reshape(group * zp, NY) - mean) * inv
        gain = (inv - pull * pull) * (1.0 / (members * members))
        offset = pull * (-1.0 / members) - gain * mean
        for m in range(members):
            grad[m, at, 0:NY] = (offset + gain * here[m]).astype(jnp.bfloat16)
        mean_vmem[planes] = mean.reshape(group, zp, NY)
        return carry

    lax.fori_loop(0, SPAN // group, gradient, 0)
    give = pltpu.make_async_copy(mean_vmem.at[pl.ds(REACH, CX)], mean_ref, sems.at[3])
    give.start()

    def pull_pair(pair, carry):
        for part in range(2):
            unit = jnp.minimum(2 * pair + part, own_count - 1)
            code = order[unit]
            member, block = code // BLOCKS, lax.rem(code, BLOCKS)
            frac_x, frac_y, frac_z, q, power, weight = fields(atoms_ref, member, block)
            gx, off_x = table_x(frac_x, power, REACH, 0, SPAN, True)
            gz, off_z = table_z(frac_z, power)
            rows[part, 0:SPAN] = gx
            rows[part, SPAN : 2 * SPAN] = gx * off_x * q
            slot = unit if stash else part
            if not stash:
                table_y(gy.at[slot], frac_y, power, q, True)
            pulled[part] = jnp.dot(grad[member], gy[slot], preferred_element_type=jnp.float32)
            sum_x = jnp.zeros((zp, BLOCK), jnp.float32)
            sum_y = jnp.zeros((zp, BLOCK), jnp.float32)
            sum_z = jnp.zeros((zp, BLOCK), jnp.float32)
            for t in range(SPAN):
                plain = pulled[part, t * zp : (t + 1) * zp, 0:BLOCK]
                slanted = pulled[part, t * zp : (t + 1) * zp, BLOCK:]
                here = rows[part, t : t + 1]
                sum_x += rows[part, SPAN + t : SPAN + t + 1] * plain
                sum_y += here * slanted
                sum_z += here * plain
            at = pl.ds(block, 1)
            forces[member, 0, at] = weight * jnp.sum(sum_x * gz, 0, keepdims=True)
            forces[member, 1, at] = weight * jnp.sum(sum_y * gz, 0, keepdims=True)
            forces[member, 2, at] = weight * jnp.sum(sum_z * (gz * off_z * q), 0, keepdims=True)
        return carry

    lax.fori_loop(0, (own_count + 1) // 2, pull_pair, 0)
    if len(outs) == 1:
        outs[0][...] = forces[...]
    else:
        for m, out in enumerate(outs):
            out[...] = forces[m]
    give.wait()


def shards(coords, widths, amplitudes, live_blocks, target_map):
    members = lax.axis_size("replica")
    bricks = lax.axis_size("sx")
    rank = lax.axis_index("replica")
    zs = NZ // members
    zp = max(zs, 8)
    sliced = zs % 8 == 0
    few = members <= 4 and members & (members - 1) == 0
    stash = members <= STASH_LIMIT
    blocks = (BLOCKS, BLOCK)
    vmem = pl.BlockSpec(memory_space=pltpu.VMEM)
    smem = pl.BlockSpec(memory_space=pltpu.SMEM)
    anywhere = pl.BlockSpec(memory_space=pl.ANY)

    target = target_map
    if not sliced:
        part = lax.dynamic_slice_in_dim(target_map, rank * zs, zs, 1)
        target = jnp.pad(part, ((0, 0), (0, zp - zs), (0, 0)))
    edge = jax.ShapeDtypeStruct((REACH, zp, NY), jnp.float32)
    own, near_edge, far_edge = pl.pallas_call(
        functools.partial(pack_kernel, zs, sliced),
        out_shape=(jax.ShapeDtypeStruct((FIELDS,) + blocks, jnp.float32), edge, edge),
        in_specs=[vmem, vmem, vmem, smem, anywhere],
        out_specs=(vmem, vmem, vmem),
        scratch_shapes=[pltpu.SemaphoreType.DMA((2,))],
        name="pack",
    )(coords.reshape((3,) + blocks), widths.reshape(blocks), amplitudes.reshape(blocks), live_blocks, target)

    def swap(block, pairs):
        return lax.ppermute(block, "sx", pairs + [(b, a) for a, b in pairs])

    near_pairs = [(i, i + 1) for i in range(0, bricks - 1, 2)]
    far_pairs = [(i, i + 1) for i in range(1, bricks - 1, 2)]

    def across(block, k):
        return lax.ppermute(block, "replica", [(i, i ^ k) for i in range(members)])

    if few:
        everyone = jnp.stack([own] + [across(own, k) for k in range(1, members)])
    else:
        everyone = lax.all_gather(own, "replica")
    near_target, far_target = swap(near_edge, near_pairs), swap(far_edge, far_pairs)
    far, near = swap(everyone, far_pairs), swap(everyone, near_pairs)

    force_shapes = (
        [jax.ShapeDtypeStruct((3,) + blocks, jnp.float32)] * members
        if few
        else [jax.ShapeDtypeStruct((members, 3) + blocks, jnp.float32)]
    )
    slots = members * BLOCKS if stash else 2
    mean, *partial = pl.pallas_call(
        functools.partial(refine_kernel, members, zp, zs, sliced, stash),
        out_shape=[jax.ShapeDtypeStruct((CX, zp, NY), jnp.float32)] + force_shapes,
        in_specs=[vmem, vmem, vmem, anywhere, anywhere, anywhere],
        out_specs=[anywhere] + [vmem] * len(force_shapes),
        scratch_shapes=[
            pltpu.VMEM((members, SPAN * zp, LANES), jnp.float32),
            pltpu.VMEM((members, SPAN * zp, LANES), jnp.bfloat16),
            pltpu.VMEM((SPAN, zp, NY), jnp.float32),
            pltpu.VMEM((SPAN, zp, NY), jnp.float32),
            pltpu.VMEM((slots, LANES, 2 * BLOCK), jnp.bfloat16),
            pltpu.VMEM((2, LANES, BLOCK), jnp.bfloat16),
            pltpu.VMEM((2, SPAN * zp, BLOCK), jnp.bfloat16),
            pltpu.VMEM((2, LAP * zp, BLOCK), jnp.bfloat16),
            pltpu.VMEM((2, SPAN * zp, 2 * BLOCK), jnp.float32),
            pltpu.VMEM((2, 2 * SPAN, BLOCK), jnp.float32),
            pltpu.VMEM((members, 3) + blocks, jnp.float32),
            pltpu.SMEM((3 * members * BLOCKS + 1,), jnp.int32),
            pltpu.SemaphoreType.DMA((4,)),
        ],
        compiler_params=pltpu.CompilerParams(vmem_limit_bytes=44 * 1024 * 1024),
        name="refine",
    )(everyone, near, far, near_target, far_target, target)

    if few:
        forces = partial[0]
        for k in range(1, members):
            forces = forces + across(partial[k], k)
    else:
        forces = lax.psum_scatter(partial[0], "replica", scatter_dimension=0)
    return mean[:, :zs], forces.reshape(3, 1, ATOMS_DEV)


def solution(mesh):
    placed = (
        P(None, ("groups", "replica"), "sx"),
        P(("groups", "replica"), "sx"),
        P(("groups", "replica"), "sx"),
        P(("groups", "replica"), "sx"),
        P(("groups", "sx"), None, None),
    )
    return jax.shard_map(
        shards,
        mesh=mesh,
        in_specs=placed,
        out_specs=(P(("groups", "sx"), "replica", None), P(None, ("groups", "replica"), "sx")),
        check_vma=False,
    )
```

```python
import functools
import math

import jax
import jax.numpy as jnp
from jax import lax
from jax.experimental import pallas as pl
from jax.experimental.pallas import tpu as pltpu
from jax.sharding import PartitionSpec as P

CX = 24
NZ = 64
NY = 480
REACH = 6
BLOCK = 128
BLOCKS = 8
ATOMS_DEV = 1024
SPAN = CX + 2 * REACH
LAP = 2 * REACH
LANES = 512
FIELDS = 5
HALF_LOG2E = 0.5 * math.log2(math.e)
STASH_LIMIT = 4

noise_floor = 0.05


def live_of(ref, member):
    number = (lax.broadcasted_iota(jnp.int32, (BLOCKS, BLOCK), 0) + 1).astype(jnp.float32)
    return jnp.max(jnp.where(ref[member, 4] != 0.0, number, 0.0)).astype(jnp.int32)


def listed(out, count, first, stride, base, live):
    for block in range(first, BLOCKS, stride):
        out[count] = base + block
        count = count + jnp.where(block < live, 1, 0)
    return count


class Tables:
    def __init__(self, zp, zs, atoms_ref):
        self.zp, self.zs, self.atoms_ref = zp, zs, atoms_ref
        self.brick = lax.axis_index("sx")
        self.last_plane = CX * lax.axis_size("sx")
        self.step = lax.broadcasted_iota(jnp.int32, (16, BLOCK), 0).astype(jnp.float32)
        step_z = lax.broadcasted_iota(jnp.int32, (zp, BLOCK), 0)
        self.own_z = (step_z < zs).astype(jnp.float32)
        self.cell_z = (step_z + lax.axis_index("replica") * zs).astype(jnp.float32)

    def fields(self, data):
        frac_x, frac_y, frac_z, width, weight = data
        inv = 1.0 / width
        q = inv * inv
        return frac_x, frac_y, frac_z, q, q * -HALF_LOG2E, weight

    def own_fields(self, member, block):
        return self.fields([self.atoms_ref[member, f, pl.ds(block, 1), :] for f in range(FIELDS)])

    def y(self, out, slopes, frac, power, q):
        base = self.step - NY * frac
        for k in range(NY // 16):
            off = base + float(16 * k)
            value = jnp.exp2(off * off * power)
            out[16 * k : 16 * k + 16, :] = value.astype(jnp.bfloat16)
            if slopes is not None:
                slopes[16 * k : 16 * k + 16, :] = (value * (off * q)).astype(jnp.bfloat16)

    def x(self, frac, power, shift, lower, count, edges):
        cell = lax.broadcasted_iota(jnp.int32, (count, BLOCK), 0) + lower
        off = cell.astype(jnp.float32) - (CX * frac + shift)
        value = jnp.exp2(off * off * power)
        if edges:
            plane = cell + (self.brick * CX - REACH)
            value = jnp.where((plane >= 0) & (plane < self.last_plane), value, 0.0)
        return value, off

    def z(self, frac, power):
        off = self.cell_z - NZ * frac
        value = jnp.exp2(off * off * power)
        return (value if self.zs == self.zp else value * self.own_z), off


def zero_tails(*tables):
    for table in tables:
        table[:, NY:, :] = jnp.zeros((table.shape[0], LANES - NY, BLOCK), jnp.bfloat16)


def splat_kernel(members, zp, zs, stash, atoms_ref, near_ref, far_ref, rho, *rest):
    if stash:
        gy, slope, gy_side, sides, left, left_side, rows, more_list, side_list = rest
    else:
        gy, gy_side, sides, left, left_side, rows, more_list, side_list = rest
        slope = None
    odd = lax.rem(lax.axis_index("sx"), 2)

    def list_member(member, counts):
        own, near, far = (live_of(ref, member) for ref in (atoms_ref, near_ref, far_ref))
        base = member * BLOCKS
        sides[0, member] = near_ref[member]
        sides[1, member] = far_ref[member]
        side_count = listed(side_list, counts[1], 0, 1, base, near)
        return (
            listed(more_list, counts[0], 2, 2, base, own),
            listed(side_list, side_count, 0, 1, members * BLOCKS + base, far),
        )

    more_count, side_count = lax.fori_loop(
        0, members, list_member, (jnp.int32(0),) * 2, unroll=members <= 4
    )
    zero_tails(gy, gy_side)
    if stash:
        zero_tails(slope)
    tables = Tables(zp, zs, atoms_ref)

    def fill_left(out, scaled, gz, count, here):
        here[0:count] = scaled
        group = max(1, 16 // zp)
        for t in range(0, count, group):
            pieces = [here[t + i : t + i + 1] * gz for i in range(group)]
            piece = pieces[0] if group == 1 else jnp.concatenate(pieces, 0)
            out[t * zp : (t + group) * zp] = piece.astype(jnp.bfloat16)

    def matmul_t(a, b):
        return lax.dot_general(a, b, (((1,), (1,)), ((), ())), preferred_element_type=jnp.float32)

    def own_splat(member, block, part):
        at = [member * BLOCKS + block + half if stash else 2 * part + half for half in range(2)]
        for half in range(2):
            spot = 2 * part + half
            frac_x, frac_y, frac_z, q, power, weight = tables.own_fields(member, block + half)
            gx, _ = tables.x(frac_x, power, REACH, 0, SPAN, True)
            gz, _ = tables.z(frac_z, power)
            tables.y(gy.at[at[half]], slope.at[at[half]] if stash else None, frac_y, power, q)
            fill_left(left.at[spot], weight * gx, gz, SPAN, rows.at[spot])
        return matmul_t(
            jnp.concatenate([left[2 * part], left[2 * part + 1]], 1),
            jnp.concatenate([gy[at[0]], gy[at[1]]], 1),
        )

    def start_members(pair, carry):
        for part in range(2):
            rho[2 * pair + part] = own_splat(2 * pair + part, 0, part)
        return carry

    lax.fori_loop(0, members // 2, start_members, 0)

    def more_blocks(unit, carry):
        code = more_list[unit]
        member, block = code // BLOCKS, lax.rem(code, BLOCKS)
        rho[member] += own_splat(member, block, 0)
        return carry

    lax.fori_loop(0, more_count, more_blocks, 0)

    side_group = gy_side.shape[0]

    def side_blocks(step_at, carry):
        done = []
        for part in range(side_group):
            unit = side_group * step_at + part
            code = side_list[jnp.minimum(unit, side_count - 1)]
            side, member = code // (members * BLOCKS), lax.rem(code // BLOCKS, members)
            above = jnp.where(side == 0, 1 - odd, odd)
            block = pl.ds(lax.rem(code, BLOCKS), 1)
            keep = jnp.where(unit < side_count, 1.0, 0.0)
            lower = CX * above
            shift = (REACH - CX + 2 * CX * above).astype(jnp.float32)
            frac_x, frac_y, frac_z, q, power, weight = tables.fields(
                [sides[side, member, f, block, :] for f in range(FIELDS)]
            )
            gx, _ = tables.x(frac_x, power, shift, lower, LAP, False)
            gz, _ = tables.z(frac_z, power)
            tables.y(gy_side.at[part], None, frac_y, power, q)
            fill_left(left_side.at[part], weight * keep * gx, gz, LAP, rows.at[part])
            at = pl.ds(pl.multiple_of(lower * zp, 16), LAP * zp)
            done.append((member, at, matmul_t(left_side[part], gy_side[part])))
        for member, at, add in done:
            rho[member, at, :] += add
        return carry

    lax.fori_loop(0, (side_count + side_group - 1) // side_group, side_blocks, 0)


def pull_kernel(
    members, zp, zs, sliced, stash, atoms_ref, near_target, far_target, target_ref, rho, *rest
):
    if stash:
        gy, slope, *rest = rest
        mean_ref, *outs, grad, wanted, mean_vmem, pulled, rows, forces, pull_list, sems = rest
    else:
        mean_ref, *outs, grad, wanted, mean_vmem, pulled, rows, forces, pull_list, sems, gy, slope = rest
    odd = lax.rem(lax.axis_index("sx"), 2)
    if sliced:
        z_first = pl.multiple_of(lax.axis_index("replica") * zs, 8)
        source = target_ref.at[:, pl.ds(z_first, zs), :]
    else:
        source = target_ref
    fetches = [
        pltpu.make_async_copy(source, wanted.at[pl.ds(REACH, CX)], sems.at[0]),
        pltpu.make_async_copy(
            near_target, wanted.at[pl.ds((REACH + CX) * (1 - odd), REACH)], sems.at[1]
        ),
        pltpu.make_async_copy(far_target, wanted.at[pl.ds((REACH + CX) * odd, REACH)], sems.at[2]),
    ]
    for fetch in fetches:
        fetch.start()

    def list_member(member, count):
        return listed(pull_list, count, 0, 1, member * BLOCKS, live_of(atoms_ref, member))

    pull_count = lax.fori_loop(0, members, list_member, jnp.int32(0), unroll=members <= 4)
    forces[...] = jnp.zeros_like(forces)
    grad[:, :, NY - 96 :] = jnp.zeros((members, SPAN * zp, LANES - NY + 96), jnp.bfloat16)
    if not stash:
        zero_tails(gy, slope)
    tables = Tables(zp, zs, atoms_ref)

    for fetch in fetches:
        fetch.wait()

    group = max(1, 16 // zp)

    def gradient(t, carry):
        at = pl.ds(pl.multiple_of(t * group * zp, 16), group * zp)
        planes = pl.ds(t * group, group)
        here = [rho[m, at, 0:NY] for m in range(members)]
        first = functools.reduce(jnp.add, here)
        second = functools.reduce(jnp.add, [f * f for f in here])
        mean = first * (1.0 / members)
        spread = second * (1.0 / members) - mean * mean
        noise = noise_floor + spread * (1.0 / members)
        guess = pl.reciprocal(noise, approx=True)
        inv = guess * (2.0 - noise * guess)
        pull = (wanted[planes].reshape(group * zp, NY) - mean) * inv
        gain = (inv - pull * pull) * (1.0 / (members * members))
        offset = pull * (-1.0 / members) - gain * mean
        for m in range(members):
            grad[m, at, 0:NY] = (offset + gain * here[m]).astype(jnp.bfloat16)
        mean_vmem[planes] = mean.reshape(group, zp, NY)
        return carry

    lax.fori_loop(0, SPAN // group, gradient, 0)
    give = pltpu.make_async_copy(mean_vmem.at[pl.ds(REACH, CX)], mean_ref, sems.at[3])
    give.start()

    def pull_pair(pair, carry):
        for part in range(2):
            code = pull_list[jnp.minimum(2 * pair + part, pull_count - 1)]
            member, block = code // BLOCKS, lax.rem(code, BLOCKS)
            frac_x, frac_y, frac_z, q, power, weight = tables.own_fields(member, block)
            gx, off_x = tables.x(frac_x, power, REACH, 0, SPAN, True)
            gz, off_z = tables.z(frac_z, power)
            rows[part, 0:SPAN] = gx
            rows[part, SPAN : 2 * SPAN] = gx * off_x * q
            slot = code if stash else part
            if not stash:
                tables.y(gy.at[slot], slope.at[slot], frac_y, power, q)
            pulled[part] = jnp.dot(
                grad[member], jnp.concatenate([gy[slot], slope[slot]], 1),
                preferred_element_type=jnp.float32,
            )
            sum_x = jnp.zeros((zp, BLOCK), jnp.float32)
            sum_y = jnp.zeros((zp, BLOCK), jnp.float32)
            sum_z = jnp.zeros((zp, BLOCK), jnp.float32)
            for t in range(SPAN):
                plain = pulled[part, t * zp : (t + 1) * zp, 0:BLOCK]
                slanted = pulled[part, t * zp : (t + 1) * zp, BLOCK:]
                here = rows[part, t : t + 1]
                sum_x += rows[part, SPAN + t : SPAN + t + 1] * plain
                sum_y += here * slanted
                sum_z += here * plain
            at = pl.ds(block, 1)
            forces[member, 0, at] = weight * jnp.sum(sum_x * gz, 0, keepdims=True)
            forces[member, 1, at] = weight * jnp.sum(sum_y * gz, 0, keepdims=True)
            forces[member, 2, at] = weight * jnp.sum(sum_z * (gz * off_z * q), 0, keepdims=True)
        return carry

    lax.fori_loop(0, (pull_count + 1) // 2, pull_pair, 0)
    if len(outs) == 1:
        outs[0][...] = forces[...]
    else:
        for m, out in enumerate(outs):
            out[...] = forces[m]
    give.wait()


def shards(coords, widths, amplitudes, live_blocks, target_map):
    members = lax.axis_size("replica")
    bricks = lax.axis_size("sx")
    rank = lax.axis_index("replica")
    zs = NZ // members
    zp = max(zs, 8)
    sliced = zs % 8 == 0
    few = members <= 4 and members & (members - 1) == 0
    stash = members <= STASH_LIMIT
    blocks = (BLOCKS, BLOCK)
    vmem = pl.BlockSpec(memory_space=pltpu.VMEM)
    anywhere = pl.BlockSpec(memory_space=pl.ANY)

    target = target_map
    if not sliced:
        part = lax.dynamic_slice_in_dim(target_map, rank * zs, zs, 1)
        target = jnp.pad(part, ((0, 0), (0, zp - zs), (0, 0)))
    alive = lax.broadcasted_iota(jnp.int32, (1,) + blocks, 1) < live_blocks[0, 0]
    weights = jnp.where(alive, amplitudes.reshape((1,) + blocks), 0.0)
    own = jnp.concatenate([coords.reshape((3,) + blocks), widths.reshape((1,) + blocks), weights])

    odd = lax.rem(lax.axis_index("sx"), 2)

    def edge(plane):
        z_first = rank * zs if sliced else 0
        return lax.dynamic_slice(target, (plane, z_first, 0), (REACH, zp, NY))

    near_edge, far_edge = edge((CX - REACH) * (1 - odd)), edge((CX - REACH) * odd)

    def swap(block, pairs):
        return lax.ppermute(block, "sx", pairs + [(b, a) for a, b in pairs])

    near_pairs = [(i, i + 1) for i in range(0, bricks - 1, 2)]
    far_pairs = [(i, i + 1) for i in range(1, bricks - 1, 2)]

    def across(block, k):
        return lax.ppermute(block, "replica", [(i, i ^ k) for i in range(members)])

    if few:
        everyone = jnp.stack([own] + [across(own, k) for k in range(1, members)])
    else:
        everyone = lax.all_gather(own, "replica")
    far, near = swap(everyone, far_pairs), swap(everyone, near_pairs)
    near_edge, far_edge, _ = lax.optimization_barrier((near_edge, far_edge, everyone))
    far_target, near_target = swap(far_edge, far_pairs), swap(near_edge, near_pairs)

    force_shapes = (
        [jax.ShapeDtypeStruct((3,) + blocks, jnp.float32)] * members
        if few
        else [jax.ShapeDtypeStruct((members, 3) + blocks, jnp.float32)]
    )
    table = ((members * BLOCKS if stash else 4), LANES, BLOCK)
    tables = [jax.ShapeDtypeStruct(table, jnp.bfloat16)] * 2 if stash else []
    splat = pl.pallas_call(
        functools.partial(splat_kernel, members, zp, zs, stash),
        out_shape=[jax.ShapeDtypeStruct((members, SPAN * zp, LANES), jnp.float32)] + tables,
        in_specs=[vmem] * 3,
        out_specs=[vmem] * (1 + len(tables)),
        scratch_shapes=([] if stash else [pltpu.VMEM(table, jnp.bfloat16)])
        + [
            pltpu.VMEM((4, LANES, BLOCK), jnp.bfloat16),
            pltpu.VMEM((2, members, FIELDS) + blocks, jnp.float32),
            pltpu.VMEM((4, SPAN * zp, BLOCK), jnp.bfloat16),
            pltpu.VMEM((4, LAP * zp, BLOCK), jnp.bfloat16),
            pltpu.VMEM((4, SPAN, BLOCK), jnp.float32),
            pltpu.SMEM((members * BLOCKS + 1,), jnp.int32),
            pltpu.SMEM((2 * members * BLOCKS + 1,), jnp.int32),
        ],
        compiler_params=pltpu.CompilerParams(vmem_limit_bytes=24 * 1024 * 1024),
        cost_estimate=pl.CostEstimate(flops=6_000_000_000, bytes_accessed=14_000_000, transcendentals=0),
        name="splat",
    )(everyone, near, far)
    mean, *partial = pl.pallas_call(
        functools.partial(pull_kernel, members, zp, zs, sliced, stash),
        out_shape=[jax.ShapeDtypeStruct((CX, zp, NY), jnp.float32)] + force_shapes,
        in_specs=[vmem, anywhere, anywhere, anywhere] + [vmem] * len(splat),
        out_specs=[anywhere] + [vmem] * len(force_shapes),
        scratch_shapes=[
            pltpu.VMEM((members, SPAN * zp, LANES), jnp.bfloat16),
            pltpu.VMEM((SPAN, zp, NY), jnp.float32),
            pltpu.VMEM((SPAN, zp, NY), jnp.float32),
            pltpu.VMEM((2, SPAN * zp, 2 * BLOCK), jnp.float32),
            pltpu.VMEM((2, 2 * SPAN, BLOCK), jnp.float32),
            pltpu.VMEM((members, 3) + blocks, jnp.float32),
            pltpu.SMEM((members * BLOCKS + 1,), jnp.int32),
            pltpu.SemaphoreType.DMA((4,)),
        ]
        + ([] if stash else [pltpu.VMEM(table, jnp.bfloat16)] * 2),
        compiler_params=pltpu.CompilerParams(vmem_limit_bytes=(24 if stash else 40) * 1024 * 1024),
        cost_estimate=pl.CostEstimate(flops=6_000_000_000, bytes_accessed=14_000_000, transcendentals=0),
        name="pull",
    )(everyone, near_target, far_target, target, *splat)

    if few:
        forces = partial[0]
        for k in range(1, members):
            forces = forces + across(partial[k], k)
    else:
        forces = lax.psum_scatter(partial[0], "replica", scatter_dimension=0)
    return mean[:, :zs], forces.reshape(3, 1, ATOMS_DEV)


def solution(mesh):
    placed = (
        P(None, ("groups", "replica"), "sx"),
        P(("groups", "replica"), "sx"),
        P(("groups", "replica"), "sx"),
        P(("groups", "replica"), "sx"),
        P(("groups", "sx"), None, None),
    )
    return jax.shard_map(
        shards,
        mesh=mesh,
        in_specs=placed,
        out_specs=(P(("groups", "sx"), "replica", None), P(None, ("groups", "replica"), "sx")),
        check_vma=False,
    )
```

```python
import functools
import math

import jax
import jax.numpy as jnp
from jax import lax
from jax.experimental import pallas as pl
from jax.experimental.pallas import tpu as pltpu
from jax.sharding import PartitionSpec as P

CX = 24
NZ = 64
NY = 480
REACH = 6
BLOCK = 128
BLOCKS = 8
ATOMS_DEV = 1024
SPAN = CX + 2 * REACH
LAP = 2 * REACH
LANES = 512
FIELDS = 5
HALF_LOG2E = 0.5 * math.log2(math.e)
STASH_LIMIT = 4

noise_floor = 0.05


def pack_kernel(coords_ref, widths_ref, amplitudes_ref, live_ref, own_ref, sems):
    copies = [
        pltpu.make_async_copy(coords_ref, own_ref.at[pl.ds(0, 3)], sems.at[0]),
        pltpu.make_async_copy(widths_ref, own_ref.at[3], sems.at[1]),
        pltpu.make_async_copy(amplitudes_ref, own_ref.at[4], sems.at[2]),
    ]
    for copy in copies:
        copy.start()
    for copy in copies:
        copy.wait()
    block = lax.broadcasted_iota(jnp.int32, (BLOCKS, BLOCK), 0)
    own_ref[4] = jnp.where(block < live_ref[0, 0], own_ref[4], 0.0)


def live_of(ref, member):
    number = (lax.broadcasted_iota(jnp.int32, (BLOCKS, BLOCK), 0) + 1).astype(jnp.float32)
    return jnp.max(jnp.where(ref[member, 4] != 0.0, number, 0.0)).astype(jnp.int32)


def listed(out, count, first, stride, base, live):
    for block in range(first, BLOCKS, stride):
        out[count] = base + block
        count = count + jnp.where(block < live, 1, 0)
    return count


class Tables:
    def __init__(self, zp, zs, atoms_ref):
        self.zp, self.zs, self.atoms_ref = zp, zs, atoms_ref
        self.brick = lax.axis_index("sx")
        self.last_plane = CX * lax.axis_size("sx")
        self.step = lax.broadcasted_iota(jnp.int32, (16, BLOCK), 0).astype(jnp.float32)
        step_z = lax.broadcasted_iota(jnp.int32, (zp, BLOCK), 0)
        self.own_z = (step_z < zs).astype(jnp.float32)
        self.cell_z = (step_z + lax.axis_index("replica") * zs).astype(jnp.float32)

    def fields(self, data):
        frac_x, frac_y, frac_z, width, weight = data
        inv = 1.0 / width
        q = inv * inv
        return frac_x, frac_y, frac_z, q, q * -HALF_LOG2E, weight

    def own_fields(self, member, block):
        return self.fields([self.atoms_ref[member, f, pl.ds(block, 1), :] for f in range(FIELDS)])

    def y(self, out, slopes, frac, power, q):
        base = self.step - NY * frac
        for k in range(NY // 16):
            off = base + float(16 * k)
            value = jnp.exp2(off * off * power)
            out[16 * k : 16 * k + 16, :] = value.astype(jnp.bfloat16)
            if slopes is not None:
                slopes[16 * k : 16 * k + 16, :] = (value * (off * q)).astype(jnp.bfloat16)

    def x(self, frac, power, shift, lower, count, edges):
        cell = lax.broadcasted_iota(jnp.int32, (count, BLOCK), 0) + lower
        off = cell.astype(jnp.float32) - (CX * frac + shift)
        value = jnp.exp2(off * off * power)
        if edges:
            plane = cell + (self.brick * CX - REACH)
            value = jnp.where((plane >= 0) & (plane < self.last_plane), value, 0.0)
        return value, off

    def z(self, frac, power):
        off = self.cell_z - NZ * frac
        value = jnp.exp2(off * off * power)
        return (value if self.zs == self.zp else value * self.own_z), off


def zero_tails(*tables):
    for table in tables:
        table[:, NY:, :] = jnp.zeros((table.shape[0], LANES - NY, BLOCK), jnp.bfloat16)


def splat_kernel(
    members, zp, zs, sliced, stash, atoms_ref, near_ref, far_ref, target_ref, rho, wanted, *rest
):
    if stash:
        gy, slope, gy_side, sides, left, left_side, rows, more_list, side_list, sem = rest
    else:
        gy, gy_side, sides, left, left_side, rows, more_list, side_list, sem = rest
        slope = None
    odd = lax.rem(lax.axis_index("sx"), 2)
    if sliced:
        z_first = pl.multiple_of(lax.axis_index("replica") * zs, 8)
        source = target_ref.at[:, pl.ds(z_first, zs), :]
    else:
        source = target_ref
    fetch = pltpu.make_async_copy(source, wanted, sem)
    fetch.start()

    def list_member(member, counts):
        own, near, far = (live_of(ref, member) for ref in (atoms_ref, near_ref, far_ref))
        base = member * BLOCKS
        sides[0, member] = near_ref[member]
        sides[1, member] = far_ref[member]
        side_count = listed(side_list, counts[1], 0, 1, base, near)
        return (
            listed(more_list, counts[0], 2, 2, base, own),
            listed(side_list, side_count, 0, 1, members * BLOCKS + base, far),
        )

    more_count, side_count = lax.fori_loop(
        0, members, list_member, (jnp.int32(0),) * 2, unroll=members <= 4
    )
    zero_tails(gy, gy_side)
    if stash:
        zero_tails(slope)
    tables = Tables(zp, zs, atoms_ref)

    def fill_left(out, scaled, gz, count, here):
        here[0:count] = scaled
        group = max(1, 16 // zp)
        for t in range(0, count, group):
            pieces = [here[t + i : t + i + 1] * gz for i in range(group)]
            piece = pieces[0] if group == 1 else jnp.concatenate(pieces, 0)
            out[t * zp : (t + group) * zp] = piece.astype(jnp.bfloat16)

    def matmul_t(a, b):
        return lax.dot_general(a, b, (((1,), (1,)), ((), ())), preferred_element_type=jnp.float32)

    def own_splat(member, block, part):
        at = [member * BLOCKS + block + half if stash else 2 * part + half for half in range(2)]
        for half in range(2):
            spot = 2 * part + half
            frac_x, frac_y, frac_z, q, power, weight = tables.own_fields(member, block + half)
            gx, _ = tables.x(frac_x, power, REACH, 0, SPAN, True)
            gz, _ = tables.z(frac_z, power)
            tables.y(gy.at[at[half]], slope.at[at[half]] if stash else None, frac_y, power, q)
            fill_left(left.at[spot], weight * gx, gz, SPAN, rows.at[spot])
        return matmul_t(
            jnp.concatenate([left[2 * part], left[2 * part + 1]], 1),
            jnp.concatenate([gy[at[0]], gy[at[1]]], 1),
        )

    def start_members(step_at, carry):
        for part in range(start_group):
            member = start_group * step_at + part
            rho[member] = own_splat(member, 0, part)
        return carry

    start_group = min(members, 4)
    lax.fori_loop(0, members // start_group, start_members, 0)

    def more_pair(unit, part):
        code = more_list[unit]
        member, block = code // BLOCKS, lax.rem(code, BLOCKS)
        return member, slice(None), own_splat(member, block, part)

    side_group = gy_side.shape[0]

    def side_units(step_at):
        done = []
        for part in range(side_group):
            unit = side_group * step_at + part
            code = side_list[jnp.minimum(unit, side_count - 1)]
            side, member = code // (members * BLOCKS), lax.rem(code // BLOCKS, members)
            above = jnp.where(side == 0, 1 - odd, odd)
            block = pl.ds(lax.rem(code, BLOCKS), 1)
            keep = jnp.where(unit < side_count, 1.0, 0.0)
            lower = CX * above
            shift = (REACH - CX + 2 * CX * above).astype(jnp.float32)
            frac_x, frac_y, frac_z, q, power, weight = tables.fields(
                [sides[side, member, f, block, :] for f in range(FIELDS)]
            )
            gx, _ = tables.x(frac_x, power, shift, lower, LAP, False)
            gz, _ = tables.z(frac_z, power)
            tables.y(gy_side.at[part], None, frac_y, power, q)
            here = rows.at[rows.shape[0] - side_group + part]
            fill_left(left_side.at[part], weight * keep * gx, gz, LAP, here)
            at = pl.ds(pl.multiple_of(lower * zp, 16), LAP * zp)
            done.append((member, at, matmul_t(left_side[part], gy_side[part])))
        return done

    def add_up(done):
        for member, at, add in done:
            rho[member, at, :] += add

    def both(step_at, carry):
        add_up([more_pair(step_at, 0)] + side_units(step_at))
        return carry

    def more_alone(step_at, carry):
        add_up([more_pair(step_at, 0)])
        return carry

    def side_alone(step_at, carry):
        add_up(side_units(step_at))
        return carry

    side_steps = (side_count + side_group - 1) // side_group
    shared = jnp.minimum(more_count, side_steps)
    lax.fori_loop(0, shared, both, 0)
    lax.fori_loop(shared, more_count, more_alone, 0)
    lax.fori_loop(shared, side_steps, side_alone, 0)
    fetch.wait()


def pull_kernel(members, zp, zs, stash, atoms_ref, near_target, far_target, rho, wanted, *rest):
    if stash:
        gy, slope, *rest = rest
        mean_ref, *outs, grad, mean_vmem, pulled, rows, forces, pull_list, sem = rest
    else:
        mean_ref, *outs, grad, mean_vmem, pulled, rows, forces, pull_list, sem, gy, slope = rest
    odd = lax.rem(lax.axis_index("sx"), 2)

    def list_member(member, count):
        return listed(pull_list, count, 0, 1, member * BLOCKS, live_of(atoms_ref, member))

    pull_count = lax.fori_loop(0, members, list_member, jnp.int32(0), unroll=members <= 4)
    forces[...] = jnp.zeros_like(forces)
    grad[:, :, NY - 96 :] = jnp.zeros((members, SPAN * zp, LANES - NY + 96), jnp.bfloat16)
    if not stash:
        zero_tails(gy, slope)
    tables = Tables(zp, zs, atoms_ref)

    group = max(1, 16 // zp)

    def gradient(first_plane, goal, means, t, carry):
        at = pl.ds(pl.multiple_of((first_plane + t * group) * zp, 16), group * zp)
        planes = pl.ds(t * group, group)
        here = [rho[m, at, 0:NY] for m in range(members)]
        first = functools.reduce(jnp.add, here)
        second = functools.reduce(jnp.add, [f * f for f in here])
        mean = first * (1.0 / members)
        spread = second * (1.0 / members) - mean * mean
        noise = noise_floor + spread * (1.0 / members)
        guess = pl.reciprocal(noise, approx=True)
        inv = guess * (2.0 - noise * guess)
        pull = (goal[planes].reshape(group * zp, NY) - mean) * inv
        gain = (inv - pull * pull) * (1.0 / (members * members))
        offset = pull * (-1.0 / members) - gain * mean
        for m in range(members):
            grad[m, at, 0:NY] = (offset + gain * here[m]).astype(jnp.bfloat16)
        if means is not None:
            means[planes] = mean.reshape(group, zp, NY)
        return carry

    for first_plane, goal, means in (
        (REACH, wanted, mean_vmem),
        ((REACH + CX) * (1 - odd), near_target, None),
        ((REACH + CX) * odd, far_target, None),
    ):
        steps = goal.shape[0] // group
        lax.fori_loop(0, steps, functools.partial(gradient, first_plane, goal, means), 0)
    give = pltpu.make_async_copy(mean_vmem, mean_ref, sem)
    give.start()

    pull_group = pulled.shape[0]

    def pull_units(first_unit, units):
        for part in range(units):
            code = pull_list[jnp.minimum(first_unit + part, pull_count - 1)]
            member, block = code // BLOCKS, lax.rem(code, BLOCKS)
            frac_x, frac_y, frac_z, q, power, weight = tables.own_fields(member, block)
            gx, off_x = tables.x(frac_x, power, REACH, 0, SPAN, True)
            gz, off_z = tables.z(frac_z, power)
            rows[part, 0:SPAN] = gx
            rows[part, SPAN : 2 * SPAN] = gx * off_x * q
            slot = code if stash else part
            if not stash:
                tables.y(gy.at[slot], slope.at[slot], frac_y, power, q)
            pulled[part] = jnp.dot(
                grad[member], jnp.concatenate([gy[slot], slope[slot]], 1),
                preferred_element_type=jnp.float32,
            )
            sum_x = jnp.zeros((zp, BLOCK), jnp.float32)
            sum_y = jnp.zeros((zp, BLOCK), jnp.float32)
            sum_z = jnp.zeros((zp, BLOCK), jnp.float32)
            for t in range(SPAN):
                plain = pulled[part, t * zp : (t + 1) * zp, 0:BLOCK]
                slanted = pulled[part, t * zp : (t + 1) * zp, BLOCK:]
                here = rows[part, t : t + 1]
                sum_x += rows[part, SPAN + t : SPAN + t + 1] * plain
                sum_y += here * slanted
                sum_z += here * plain
            at = pl.ds(block, 1)
            forces[member, 0, at] = weight * jnp.sum(sum_x * gz, 0, keepdims=True)
            forces[member, 1, at] = weight * jnp.sum(sum_y * gz, 0, keepdims=True)
            forces[member, 2, at] = weight * jnp.sum(sum_z * (gz * off_z * q), 0, keepdims=True)

    def pull_many(step_at, carry):
        pull_units(pull_group * step_at, pull_group)
        return carry

    def pull_two(step_at, carry):
        pull_units(2 * step_at, 2)
        return carry

    whole = pull_count // pull_group
    lax.fori_loop(0, whole, pull_many, 0)
    lax.fori_loop(whole * (pull_group // 2), (pull_count + 1) // 2, pull_two, 0)
    if len(outs) == 1:
        outs[0][...] = forces[...]
    else:
        for k, out in enumerate(outs):
            out[...] = forces[k * members // 2 : (k + 1) * members // 2]
    give.wait()


def shards(coords, widths, amplitudes, live_blocks, target_map):
    members = lax.axis_size("replica")
    bricks = lax.axis_size("sx")
    rank = lax.axis_index("replica")
    zs = NZ // members
    zp = max(zs, 8)
    sliced = zs % 8 == 0
    few = members <= 4 and members & (members - 1) == 0
    stash = members <= STASH_LIMIT
    blocks = (BLOCKS, BLOCK)
    vmem = pl.BlockSpec(memory_space=pltpu.VMEM)
    anywhere = pl.BlockSpec(memory_space=pl.ANY)

    target = target_map
    if not sliced:
        part = lax.dynamic_slice_in_dim(target_map, rank * zs, zs, 1)
        target = jnp.pad(part, ((0, 0), (0, zp - zs), (0, 0)))
    hbm = pl.BlockSpec(memory_space=pltpu.HBM)
    own = pl.pallas_call(
        pack_kernel,
        out_shape=jax.ShapeDtypeStruct((FIELDS,) + blocks, jnp.float32),
        in_specs=[hbm] * 3 + [pl.BlockSpec(memory_space=pltpu.SMEM)],
        out_specs=vmem,
        scratch_shapes=[pltpu.SemaphoreType.DMA((3,))],
        compiler_params=pltpu.CompilerParams(vmem_limit_bytes=4 * 1024 * 1024),
        name="pack",
    )(
        *(
            pltpu.with_memory_space_constraint(x, pltpu.HBM)
            for x in (coords.reshape((3,) + blocks), widths.reshape(blocks), amplitudes.reshape(blocks))
        ),
        live_blocks,
    )

    odd = lax.rem(lax.axis_index("sx"), 2)

    def edge(plane):
        z_first = rank * zs if sliced else 0
        return lax.dynamic_slice(target, (plane, z_first, 0), (REACH, zp, NY))

    near_edge, far_edge = edge((CX - REACH) * (1 - odd)), edge((CX - REACH) * odd)

    def swap(block, pairs):
        return lax.ppermute(block, "sx", pairs + [(b, a) for a, b in pairs])

    near_pairs = [(i, i + 1) for i in range(0, bricks - 1, 2)]
    far_pairs = [(i, i + 1) for i in range(1, bricks - 1, 2)]

    def across(block, k):
        return lax.ppermute(block, "replica", [(i, i ^ k) for i in range(members)])

    if few:
        everyone = own[None]
        while everyone.shape[0] < members:
            everyone = jnp.concatenate([everyone, across(everyone, everyone.shape[0])])
            everyone, near_edge, far_edge = lax.optimization_barrier((everyone, near_edge, far_edge))
    else:
        everyone = lax.all_gather(own, "replica")
    far, near = swap(everyone, far_pairs), swap(everyone, near_pairs)
    near_edge, far_edge, _ = lax.optimization_barrier((near_edge, far_edge, everyone))
    far_target, near_target = swap(far_edge, far_pairs), swap(near_edge, near_pairs)

    force_shapes = (
        [jax.ShapeDtypeStruct((members // 2, 3) + blocks, jnp.float32)] * 2
        if few
        else [jax.ShapeDtypeStruct((members, 3) + blocks, jnp.float32)]
    )
    table = ((members * BLOCKS if stash else 8), LANES, BLOCK)
    tables = [jax.ShapeDtypeStruct(table, jnp.bfloat16)] * 2 if stash else []
    splat = pl.pallas_call(
        functools.partial(splat_kernel, members, zp, zs, sliced, stash),
        out_shape=[
            jax.ShapeDtypeStruct((members, SPAN * zp, LANES), jnp.float32),
            jax.ShapeDtypeStruct((CX, zp, NY), jnp.float32),
        ]
        + tables,
        in_specs=[vmem] * 3 + [hbm],
        out_specs=[vmem] * (2 + len(tables)),
        scratch_shapes=([] if stash else [pltpu.VMEM(table, jnp.bfloat16)])
        + [
            pltpu.VMEM((4, LANES, BLOCK), jnp.bfloat16),
            pltpu.VMEM((2, members, FIELDS) + blocks, jnp.float32),
            pltpu.VMEM((8, SPAN * zp, BLOCK), jnp.bfloat16),
            pltpu.VMEM((4, LAP * zp, BLOCK), jnp.bfloat16),
            pltpu.VMEM((12, SPAN, BLOCK), jnp.float32),
            pltpu.SMEM((members * BLOCKS + 1,), jnp.int32),
            pltpu.SMEM((2 * members * BLOCKS + 1,), jnp.int32),
            pltpu.SemaphoreType.DMA,
        ],
        compiler_params=pltpu.CompilerParams(vmem_limit_bytes=24 * 1024 * 1024),
        cost_estimate=pl.CostEstimate(flops=6_000_000_000, bytes_accessed=14_000_000, transcendentals=0),
        name="splat",
    )(everyone, near, far, pltpu.with_memory_space_constraint(target, pltpu.HBM))
    mean, *partial = pl.pallas_call(
        functools.partial(pull_kernel, members, zp, zs, stash),
        out_shape=[jax.ShapeDtypeStruct((CX, zp, NY), jnp.float32)] + force_shapes,
        in_specs=[vmem] * (3 + len(splat)),
        out_specs=[anywhere] + [vmem] * len(force_shapes),
        scratch_shapes=[
            pltpu.VMEM((members, SPAN * zp, LANES), jnp.bfloat16),
            pltpu.VMEM((CX, zp, NY), jnp.float32),
            pltpu.VMEM((4, SPAN * zp, 2 * BLOCK), jnp.float32),
            pltpu.VMEM((4, 2 * SPAN, BLOCK), jnp.float32),
            pltpu.VMEM((members, 3) + blocks, jnp.float32),
            pltpu.SMEM((members * BLOCKS + 1,), jnp.int32),
            pltpu.SemaphoreType.DMA,
        ]
        + ([] if stash else [pltpu.VMEM(table, jnp.bfloat16)] * 2),
        compiler_params=pltpu.CompilerParams(vmem_limit_bytes=(24 if stash else 40) * 1024 * 1024),
        cost_estimate=pl.CostEstimate(flops=6_000_000_000, bytes_accessed=14_000_000, transcendentals=0),
        name="pull",
    )(everyone, near_target, far_target, *splat)

    if few:
        k = members // 2
        forces = partial[0] + across(partial[1], k)
        while k > 1:
            k //= 2
            forces = forces[:k] + across(forces[k:], k)
    else:
        forces = lax.psum_scatter(partial[0], "replica", scatter_dimension=0)
    return mean[:, :zs], forces.reshape(3, 1, ATOMS_DEV)


def solution(mesh):
    placed = (
        P(None, ("groups", "replica"), "sx"),
        P(("groups", "replica"), "sx"),
        P(("groups", "replica"), "sx"),
        P(("groups", "replica"), "sx"),
        P(("groups", "sx"), None, None),
    )
    return jax.shard_map(
        shards,
        mesh=mesh,
        in_specs=placed,
        out_specs=(P(("groups", "sx"), "replica", None), P(None, ("groups", "replica"), "sx")),
        check_vma=False,
    )
```

```python
import functools
import math

import jax
import jax.numpy as jnp
from jax import lax
from jax.experimental import pallas as pl
from jax.experimental.pallas import tpu as pltpu
from jax.sharding import PartitionSpec as P

CX = 24
NZ = 64
NY = 480
REACH = 6
BLOCK = 128
BLOCKS = 8
ATOMS_DEV = 1024
SPAN = CX + 2 * REACH
LAP = 2 * REACH
LANES = 512
FIELDS = 5
HALF_LOG2E = 0.5 * math.log2(math.e)
STASH_LIMIT = 4

noise_floor = 0.05


def pack_kernel(coords_ref, widths_ref, amplitudes_ref, live_ref, own_ref, sems):
    copies = [
        pltpu.make_async_copy(coords_ref, own_ref.at[pl.ds(0, 3)], sems.at[0]),
        pltpu.make_async_copy(widths_ref, own_ref.at[3], sems.at[1]),
        pltpu.make_async_copy(amplitudes_ref, own_ref.at[4], sems.at[2]),
    ]
    for copy in copies:
        copy.start()
    for copy in copies:
        copy.wait()
    block = lax.broadcasted_iota(jnp.int32, (BLOCKS, BLOCK), 0)
    own_ref[4] = jnp.where(block < live_ref[0, 0], own_ref[4], 0.0)


def live_of(ref, member):
    number = (lax.broadcasted_iota(jnp.int32, (BLOCKS, BLOCK), 0) + 1).astype(jnp.float32)
    return jnp.max(jnp.where(ref[member, 4] != 0.0, number, 0.0)).astype(jnp.int32)


def split(code):
    return lax.shift_right_logical(code, 3), code & 7


def listed(out, count, first, stride, base, live):
    for block in range(first, BLOCKS, stride):
        out[count] = base + block
        count = count + jnp.where(block < live, 1, 0)
    return count


class Tables:
    def __init__(self, zp, zs, atoms_ref):
        self.zp, self.zs, self.atoms_ref = zp, zs, atoms_ref
        self.brick = lax.axis_index("sx")
        self.last_plane = CX * lax.axis_size("sx")
        self.step = lax.broadcasted_iota(jnp.int32, (16, BLOCK), 0).astype(jnp.float32)
        step_z = lax.broadcasted_iota(jnp.int32, (zp, BLOCK), 0)
        self.own_z = (step_z < zs).astype(jnp.float32)
        self.cell_z = (step_z + lax.axis_index("replica") * zs).astype(jnp.float32)

    def fields(self, data):
        frac_x, frac_y, frac_z, width, weight = data
        inv = 1.0 / width
        q = inv * inv
        return frac_x, frac_y, frac_z, q, q * -HALF_LOG2E, weight

    def own_fields(self, member, block):
        return self.fields([self.atoms_ref[member, f, pl.ds(block, 1), :] for f in range(FIELDS)])

    def y(self, out, slopes, frac, power, q):
        base = self.step - NY * frac
        for k in range(NY // 16):
            off = base + float(16 * k)
            value = jnp.exp2(off * off * power)
            out[16 * k : 16 * k + 16, :] = value.astype(jnp.bfloat16)
            if slopes is not None:
                slopes[16 * k : 16 * k + 16, :] = (value * (off * q)).astype(jnp.bfloat16)

    def x(self, frac, power, shift, lower, count, edges):
        cell = lax.broadcasted_iota(jnp.int32, (count, BLOCK), 0) + lower
        off = cell.astype(jnp.float32) - (CX * frac + shift)
        value = jnp.exp2(off * off * power)
        if edges:
            plane = cell + (self.brick * CX - REACH)
            value = jnp.where((plane >= 0) & (plane < self.last_plane), value, 0.0)
        return value, off

    def z(self, frac, power):
        off = self.cell_z - NZ * frac
        value = jnp.exp2(off * off * power)
        return (value if self.zs == self.zp else value * self.own_z), off


def zero_tails(*tables):
    for table in tables:
        table[:, NY:, :] = jnp.zeros((table.shape[0], LANES - NY, BLOCK), jnp.bfloat16)


def splat_kernel(
    members, zp, zs, sliced, stash, atoms_ref, near_ref, far_ref, target_ref, rho, wanted, *rest
):
    if stash:
        gy, slope, gy_side, sides, left, left_side, rows, more_list, side_list, sem = rest
    else:
        gy, gy_side, sides, left, left_side, rows, more_list, side_list, sem = rest
        slope = None
    odd = lax.rem(lax.axis_index("sx"), 2)
    if sliced:
        z_first = pl.multiple_of(lax.axis_index("replica") * zs, 8)
        source = target_ref.at[:, pl.ds(z_first, zs), :]
    else:
        source = target_ref
    fetch = pltpu.make_async_copy(source, wanted, sem)
    fetch.start()

    def list_member(member, counts):
        own, near, far = (live_of(ref, member) for ref in (atoms_ref, near_ref, far_ref))
        base = member * BLOCKS
        sides[member] = near_ref[member]
        sides[members + member] = far_ref[member]
        side_count = listed(side_list, counts[1], 0, 1, base, near)
        return (
            listed(more_list, counts[0], 2, 2, base, own),
            listed(side_list, side_count, 0, 1, members * BLOCKS + base, far),
        )

    more_count, side_count = lax.fori_loop(
        0, members, list_member, (jnp.int32(0),) * 2, unroll=members <= 4
    )
    zero_tails(gy, gy_side)
    if stash:
        zero_tails(slope)
    tables = Tables(zp, zs, atoms_ref)

    def fill_left(out, scaled, gz, count, here):
        here[0:count] = scaled
        group = max(1, 16 // zp)
        for t in range(0, count, group):
            pieces = [here[t + i : t + i + 1] * gz for i in range(group)]
            piece = pieces[0] if group == 1 else jnp.concatenate(pieces, 0)
            out[t * zp : (t + group) * zp] = piece.astype(jnp.bfloat16)

    def matmul_t(a, b):
        return lax.dot_general(a, b, (((1,), (1,)), ((), ())), preferred_element_type=jnp.float32)

    def own_splat(member, block, part):
        at = [member * BLOCKS + block + half if stash else 2 * part + half for half in range(2)]
        for half in range(2):
            spot = 2 * part + half
            frac_x, frac_y, frac_z, q, power, weight = tables.own_fields(member, block + half)
            gx, _ = tables.x(frac_x, power, REACH, 0, SPAN, True)
            gz, _ = tables.z(frac_z, power)
            tables.y(gy.at[at[half]], slope.at[at[half]] if stash else None, frac_y, power, q)
            fill_left(left.at[spot], weight * gx, gz, SPAN, rows.at[spot])
        return matmul_t(
            jnp.concatenate([left[2 * part], left[2 * part + 1]], 1),
            jnp.concatenate([gy[at[0]], gy[at[1]]], 1),
        )

    def start_members(step_at, carry):
        for part in range(start_group):
            member = start_group * step_at + part
            rho[member] = own_splat(member, 0, part)
        return carry

    start_group = min(members, 4)
    lax.fori_loop(0, members // start_group, start_members, 0)

    def more_pair(unit, part):
        code = more_list[unit]
        member, block = split(code)
        rho[member] += own_splat(member, block, part)

    side_group = gy_side.shape[0]

    def side_units(step_at):
        for part in range(side_group):
            unit = side_group * step_at + part
            code = side_list[jnp.minimum(unit, side_count - 1)]
            place, block = split(code)
            is_near = place < members
            member = jnp.where(is_near, place, place - members)
            above = jnp.where(is_near, 1 - odd, odd)
            block = pl.ds(block, 1)
            keep = jnp.where(unit < side_count, 1.0, 0.0)
            lower = CX * above
            shift = (REACH - CX + 2 * CX * above).astype(jnp.float32)
            frac_x, frac_y, frac_z, q, power, weight = tables.fields(
                [sides[place, f, block, :] for f in range(FIELDS)]
            )
            gx, _ = tables.x(frac_x, power, shift, lower, LAP, False)
            gz, _ = tables.z(frac_z, power)
            tables.y(gy_side.at[part], None, frac_y, power, q)
            here = rows.at[rows.shape[0] - side_group + part]
            fill_left(left_side.at[part], weight * keep * gx, gz, LAP, here)
            at = pl.ds(pl.multiple_of(lower * zp, 16), LAP * zp)
            rho[member, at, :] += matmul_t(left_side[part], gy_side[part])

    def both(step_at, carry):
        more_pair(step_at, 0)
        side_units(step_at)
        return carry

    def more_alone(step_at, carry):
        more_pair(step_at, 0)
        return carry

    def side_alone(step_at, carry):
        side_units(step_at)
        return carry

    side_steps = (side_count + side_group - 1) // side_group
    shared = jnp.minimum(more_count, side_steps)
    lax.fori_loop(0, shared, both, 0)
    lax.fori_loop(shared, more_count, more_alone, 0)
    lax.fori_loop(shared, side_steps, side_alone, 0)
    fetch.wait()


def pull_kernel(members, zp, zs, stash, atoms_ref, near_target, far_target, rho, wanted, *rest):
    if stash:
        gy, slope, *rest = rest
        mean_ref, *outs, grad, mean_vmem, pulled, rows, forces, pull_list, sem = rest
    else:
        mean_ref, *outs, grad, mean_vmem, pulled, rows, forces, pull_list, sem, gy, slope = rest
    odd = lax.rem(lax.axis_index("sx"), 2)

    def list_member(member, count):
        return listed(pull_list, count, 0, 1, member * BLOCKS, live_of(atoms_ref, member))

    pull_count = lax.fori_loop(0, members, list_member, jnp.int32(0), unroll=members <= 4)
    forces[...] = jnp.zeros_like(forces)
    grad[:, :, NY - 96 :] = jnp.zeros((members, SPAN * zp, LANES - NY + 96), jnp.bfloat16)
    if not stash:
        zero_tails(gy, slope)
    tables = Tables(zp, zs, atoms_ref)

    group = max(1, 16 // zp)

    def gradient(first_plane, goal, means, t, carry):
        at = pl.ds(pl.multiple_of((first_plane + t * group) * zp, 16), group * zp)
        planes = pl.ds(t * group, group)
        here = [rho[m, at, 0:NY] for m in range(members)]
        first = functools.reduce(jnp.add, here)
        second = functools.reduce(jnp.add, [f * f for f in here])
        mean = first * (1.0 / members)
        spread = second * (1.0 / members) - mean * mean
        noise = noise_floor + spread * (1.0 / members)
        guess = pl.reciprocal(noise, approx=True)
        inv = guess * (2.0 - noise * guess)
        pull = (goal[planes].reshape(group * zp, NY) - mean) * inv
        gain = (inv - pull * pull) * (1.0 / (members * members))
        offset = pull * (-1.0 / members) - gain * mean
        for m in range(members):
            grad[m, at, 0:NY] = (offset + gain * here[m]).astype(jnp.bfloat16)
        if means is not None:
            means[planes] = mean.reshape(group, zp, NY)
        return carry

    for first_plane, goal, means in (
        (REACH, wanted, mean_vmem),
        ((REACH + CX) * (1 - odd), near_target, None),
        ((REACH + CX) * odd, far_target, None),
    ):
        steps = goal.shape[0] // group
        lax.fori_loop(0, steps, functools.partial(gradient, first_plane, goal, means), 0)
    give = pltpu.make_async_copy(mean_vmem, mean_ref, sem)
    give.start()

    pull_group = pulled.shape[0]

    def pull_units(first_unit, units):
        for part in range(units):
            code = pull_list[jnp.minimum(first_unit + part, pull_count - 1)]
            member, block = split(code)
            frac_x, frac_y, frac_z, q, power, weight = tables.own_fields(member, block)
            gx, off_x = tables.x(frac_x, power, REACH, 0, SPAN, True)
            gz, off_z = tables.z(frac_z, power)
            rows[part, 0:SPAN] = gx
            rows[part, SPAN : 2 * SPAN] = gx * off_x * q
            slot = code if stash else part
            if not stash:
                tables.y(gy.at[slot], slope.at[slot], frac_y, power, q)
            pulled[part] = jnp.dot(
                grad[member], jnp.concatenate([gy[slot], slope[slot]], 1),
                preferred_element_type=jnp.float32,
            )
            sum_x = jnp.zeros((zp, BLOCK), jnp.float32)
            sum_y = jnp.zeros((zp, BLOCK), jnp.float32)
            sum_z = jnp.zeros((zp, BLOCK), jnp.float32)
            for t in range(SPAN):
                plain = pulled[part, t * zp : (t + 1) * zp, 0:BLOCK]
                slanted = pulled[part, t * zp : (t + 1) * zp, BLOCK:]
                here = rows[part, t : t + 1]
                sum_x += rows[part, SPAN + t : SPAN + t + 1] * plain
                sum_y += here * slanted
                sum_z += here * plain
            at = pl.ds(block, 1)
            forces[member, 0, at] = weight * jnp.sum(sum_x * gz, 0, keepdims=True)
            forces[member, 1, at] = weight * jnp.sum(sum_y * gz, 0, keepdims=True)
            forces[member, 2, at] = weight * jnp.sum(sum_z * (gz * off_z * q), 0, keepdims=True)

    def pull_many(step_at, carry):
        pull_units(pull_group * step_at, pull_group)
        return carry

    def pull_two(step_at, carry):
        pull_units(2 * step_at, 2)
        return carry

    whole = pull_count // pull_group
    lax.fori_loop(0, whole, pull_many, 0)
    lax.fori_loop(whole * (pull_group // 2), (pull_count + 1) // 2, pull_two, 0)
    if len(outs) == 1:
        outs[0][...] = forces[...]
    else:
        for k, out in enumerate(outs):
            out[...] = forces[k]
    give.wait()


def shards(coords, widths, amplitudes, live_blocks, target_map):
    members = lax.axis_size("replica")
    bricks = lax.axis_size("sx")
    rank = lax.axis_index("replica")
    zs = NZ // members
    zp = max(zs, 8)
    sliced = zs % 8 == 0
    few = members <= 4 and members & (members - 1) == 0
    stash = members <= STASH_LIMIT
    blocks = (BLOCKS, BLOCK)
    vmem = pl.BlockSpec(memory_space=pltpu.VMEM)
    anywhere = pl.BlockSpec(memory_space=pl.ANY)

    target = target_map
    if not sliced:
        part = lax.dynamic_slice_in_dim(target_map, rank * zs, zs, 1)
        target = jnp.pad(part, ((0, 0), (0, zp - zs), (0, 0)))
    hbm = pl.BlockSpec(memory_space=pltpu.HBM)
    own = pl.pallas_call(
        pack_kernel,
        out_shape=jax.ShapeDtypeStruct((FIELDS,) + blocks, jnp.float32),
        in_specs=[hbm] * 3 + [pl.BlockSpec(memory_space=pltpu.SMEM)],
        out_specs=vmem,
        scratch_shapes=[pltpu.SemaphoreType.DMA((3,))],
        compiler_params=pltpu.CompilerParams(vmem_limit_bytes=4 * 1024 * 1024),
        name="pack",
    )(
        *(
            pltpu.with_memory_space_constraint(x, pltpu.HBM)
            for x in (coords.reshape((3,) + blocks), widths.reshape(blocks), amplitudes.reshape(blocks))
        ),
        live_blocks,
    )

    odd = lax.rem(lax.axis_index("sx"), 2)

    def edge(plane):
        z_first = rank * zs if sliced else 0
        return lax.dynamic_slice(target, (plane, z_first, 0), (REACH, zp, NY))

    near_edge, far_edge = edge((CX - REACH) * (1 - odd)), edge((CX - REACH) * odd)

    def swap(block, pairs):
        return lax.ppermute(block, "sx", pairs + [(b, a) for a, b in pairs])

    near_pairs = [(i, i + 1) for i in range(0, bricks - 1, 2)]
    far_pairs = [(i, i + 1) for i in range(1, bricks - 1, 2)]

    def across(block, k):
        return lax.ppermute(block, "replica", [(i, i ^ k) for i in range(members)])

    if few:
        got = {0: own}
        for k in (2, 3, 1):
            got[k] = across(own, k)
        everyone = jnp.stack([got[k] for k in range(members)])
        everyone, near_edge, far_edge = lax.optimization_barrier((everyone, near_edge, far_edge))
    else:
        everyone = lax.all_gather(own, "replica")
    far, near = swap(everyone, far_pairs), swap(everyone, near_pairs)
    near_edge, far_edge, _ = lax.optimization_barrier((near_edge, far_edge, everyone))
    far_target, near_target = swap(far_edge, far_pairs), swap(near_edge, near_pairs)

    force_shapes = (
        [jax.ShapeDtypeStruct((3,) + blocks, jnp.float32)] * members
        if few
        else [jax.ShapeDtypeStruct((members, 3) + blocks, jnp.float32)]
    )
    table = ((members * BLOCKS if stash else 8), LANES, BLOCK)
    tables = [jax.ShapeDtypeStruct(table, jnp.bfloat16)] * 2 if stash else []
    splat = pl.pallas_call(
        functools.partial(splat_kernel, members, zp, zs, sliced, stash),
        out_shape=[
            jax.ShapeDtypeStruct((members, SPAN * zp, LANES), jnp.float32),
            jax.ShapeDtypeStruct((CX, zp, NY), jnp.float32),
        ]
        + tables,
        in_specs=[vmem] * 3 + [hbm],
        out_specs=[vmem] * (2 + len(tables)),
        scratch_shapes=([] if stash else [pltpu.VMEM(table, jnp.bfloat16)])
        + [
            pltpu.VMEM((4, LANES, BLOCK), jnp.bfloat16),
            pltpu.VMEM((2 * members, FIELDS) + blocks, jnp.float32),
            pltpu.VMEM((8, SPAN * zp, BLOCK), jnp.bfloat16),
            pltpu.VMEM((4, LAP * zp, BLOCK), jnp.bfloat16),
            pltpu.VMEM((12, SPAN, BLOCK), jnp.float32),
            pltpu.SMEM((members * BLOCKS + 1,), jnp.int32),
            pltpu.SMEM((2 * members * BLOCKS + 1,), jnp.int32),
            pltpu.SemaphoreType.DMA,
        ],
        compiler_params=pltpu.CompilerParams(vmem_limit_bytes=24 * 1024 * 1024),
        cost_estimate=pl.CostEstimate(flops=6_000_000_000, bytes_accessed=14_000_000, transcendentals=0),
        name="splat",
    )(everyone, near, far, pltpu.with_memory_space_constraint(target, pltpu.HBM))
    mean, *partial = pl.pallas_call(
        functools.partial(pull_kernel, members, zp, zs, stash),
        out_shape=[jax.ShapeDtypeStruct((CX, zp, NY), jnp.float32)] + force_shapes,
        in_specs=[vmem] * (3 + len(splat)),
        out_specs=[anywhere] + [vmem] * len(force_shapes),
        scratch_shapes=[
            pltpu.VMEM((members, SPAN * zp, LANES), jnp.bfloat16),
            pltpu.VMEM((CX, zp, NY), jnp.float32),
            pltpu.VMEM((4, SPAN * zp, 2 * BLOCK), jnp.float32),
            pltpu.VMEM((4, 2 * SPAN, BLOCK), jnp.float32),
            pltpu.VMEM((members, 3) + blocks, jnp.float32),
            pltpu.SMEM((members * BLOCKS + 1,), jnp.int32),
            pltpu.SemaphoreType.DMA,
        ]
        + ([] if stash else [pltpu.VMEM(table, jnp.bfloat16)] * 2),
        compiler_params=pltpu.CompilerParams(vmem_limit_bytes=(24 if stash else 40) * 1024 * 1024),
        cost_estimate=pl.CostEstimate(flops=6_000_000_000, bytes_accessed=14_000_000, transcendentals=0),
        name="pull",
    )(everyone, near_target, far_target, *splat)

    if few:
        forces = partial[0]
        for k in (2, 3, 1):
            forces = forces + across(partial[k], k)
    else:
        forces = lax.psum_scatter(partial[0], "replica", scatter_dimension=0)
    return mean[:, :zs], forces.reshape(3, 1, ATOMS_DEV)


def solution(mesh):
    placed = (
        P(None, ("groups", "replica"), "sx"),
        P(("groups", "replica"), "sx"),
        P(("groups", "replica"), "sx"),
        P(("groups", "replica"), "sx"),
        P(("groups", "sx"), None, None),
    )
    return jax.shard_map(
        shards,
        mesh=mesh,
        in_specs=placed,
        out_specs=(P(("groups", "sx"), "replica", None), P(None, ("groups", "replica"), "sx")),
        check_vma=False,
    )
```

```python
import functools
import math

import jax
import jax.numpy as jnp
from jax import lax
from jax.experimental import pallas as pl
from jax.experimental.pallas import tpu as pltpu
from jax.sharding import PartitionSpec as P

CX = 24
NZ = 64
NY = 480
REACH = 6
BLOCK = 128
BLOCKS = 8
ATOMS_DEV = 1024
SPAN = CX + 2 * REACH
LAP = 2 * REACH
LANES = 512
FIELDS = 5
HALF_LOG2E = 0.5 * math.log2(math.e)
STASH_LIMIT = 4

noise_floor = 0.05


def pack_kernel(coords_ref, widths_ref, amplitudes_ref, live_ref, own_ref, sems):
    copies = [
        pltpu.make_async_copy(coords_ref, own_ref.at[pl.ds(0, 3)], sems.at[0]),
        pltpu.make_async_copy(widths_ref, own_ref.at[3], sems.at[1]),
        pltpu.make_async_copy(amplitudes_ref, own_ref.at[4], sems.at[2]),
    ]
    for copy in copies:
        copy.start()
    for copy in copies:
        copy.wait()
    block = lax.broadcasted_iota(jnp.int32, (BLOCKS, BLOCK), 0)
    own_ref[4] = jnp.where(block < live_ref[0, 0], own_ref[4], 0.0)


def live_of(ref, member):
    number = (lax.broadcasted_iota(jnp.int32, (BLOCKS, BLOCK), 0) + 1).astype(jnp.float32)
    return jnp.max(jnp.where(ref[member, 4] != 0.0, number, 0.0)).astype(jnp.int32)


def split(code):
    return lax.shift_right_logical(code, 3), code & 7


def listed(out, count, first, stride, base, live):
    for block in range(first, BLOCKS, stride):
        out[count] = base + block
        count = count + jnp.where(block < live, 1, 0)
    return count


class Tables:
    def __init__(self, zp, zs, atoms_ref):
        self.zp, self.zs, self.atoms_ref = zp, zs, atoms_ref
        self.brick = lax.axis_index("sx")
        self.last_plane = CX * lax.axis_size("sx")
        self.step = lax.broadcasted_iota(jnp.int32, (16, BLOCK), 0).astype(jnp.float32)
        step_z = lax.broadcasted_iota(jnp.int32, (zp, BLOCK), 0)
        self.own_z = (step_z < zs).astype(jnp.float32)
        self.cell_z = (step_z + lax.axis_index("replica") * zs).astype(jnp.float32)

    def fields(self, data):
        frac_x, frac_y, frac_z, width, weight = data
        inv = 1.0 / width
        q = inv * inv
        return frac_x, frac_y, frac_z, q, q * -HALF_LOG2E, weight

    def own_fields(self, member, block):
        return self.fields([self.atoms_ref[member, f, pl.ds(block, 1), :] for f in range(FIELDS)])

    def y(self, out, slopes, frac, power, q):
        base = self.step - NY * frac
        for k in range(NY // 16):
            off = base + float(16 * k)
            value = jnp.exp2(off * off * power)
            out[16 * k : 16 * k + 16, :] = value.astype(jnp.bfloat16)
            if slopes is not None:
                slopes[16 * k : 16 * k + 16, :] = (value * (off * q)).astype(jnp.bfloat16)

    def x(self, frac, power, shift, lower, count, edges):
        cell = lax.broadcasted_iota(jnp.int32, (count, BLOCK), 0) + lower
        off = cell.astype(jnp.float32) - (CX * frac + shift)
        value = jnp.exp2(off * off * power)
        if edges:
            plane = cell + (self.brick * CX - REACH)
            value = jnp.where((plane >= 0) & (plane < self.last_plane), value, 0.0)
        return value, off

    def z(self, frac, power):
        off = self.cell_z - NZ * frac
        value = jnp.exp2(off * off * power)
        return (value if self.zs == self.zp else value * self.own_z), off


def zero_tails(*tables):
    for table in tables:
        table[:, NY:, :] = jnp.zeros((table.shape[0], LANES - NY, BLOCK), jnp.bfloat16)


def splat_kernel(
    members, zp, zs, sliced, stash, atoms_ref, near_ref, far_ref, target_ref, rho, wanted, *rest
):
    if stash:
        gy, slope, gy_side, sides, more_list, side_list, sem = rest
    else:
        gy, gy_side, sides, more_list, side_list, sem = rest
        slope = None
    odd = lax.rem(lax.axis_index("sx"), 2)
    if sliced:
        z_first = pl.multiple_of(lax.axis_index("replica") * zs, 8)
        source = target_ref.at[:, pl.ds(z_first, zs), :]
    else:
        source = target_ref
    fetch = pltpu.make_async_copy(source, wanted, sem)
    fetch.start()

    brick = lax.axis_index("sx")
    inner = (brick > 0) & (brick < lax.axis_size("sx") - 1)

    def list_member(member, counts):
        own, near, far = (live_of(ref, member) for ref in (atoms_ref, near_ref, far_ref))
        far = jnp.where(inner, far, 0)
        base = member * BLOCKS
        sides[member] = near_ref[member]
        sides[members + member] = far_ref[member]
        side_count = listed(side_list, counts[1], 0, 1, base, near)
        return (
            listed(more_list, counts[0], 2, 2, base, own),
            listed(side_list, side_count, 0, 1, members * BLOCKS + base, far),
        )

    more_count, side_count = lax.fori_loop(
        0, members, list_member, (jnp.int32(0),) * 2, unroll=members <= 4
    )
    zero_tails(gy, gy_side)
    if stash:
        zero_tails(slope)
    tables = Tables(zp, zs, atoms_ref)

    def left_of(scaled, gz, count):
        group = max(1, 16 // zp)
        made = []
        for t in range(0, count, group):
            pieces = [scaled[t + i : t + i + 1] * gz for i in range(group)]
            piece = pieces[0] if group == 1 else jnp.concatenate(pieces, 0)
            made.append(piece.astype(jnp.bfloat16))
        return jnp.concatenate(made, 0)

    def matmul_t(a, b):
        return lax.dot_general(a, b, (((1,), (1,)), ((), ())), preferred_element_type=jnp.float32)

    def own_splat(member, block, part):
        at = [member * BLOCKS + block + half if stash else 2 * part + half for half in range(2)]
        lefts = []
        for half in range(2):
            frac_x, frac_y, frac_z, q, power, weight = tables.own_fields(member, block + half)
            gx, _ = tables.x(frac_x, power, REACH, 0, SPAN, True)
            gz, _ = tables.z(frac_z, power)
            tables.y(gy.at[at[half]], slope.at[at[half]] if stash else None, frac_y, power, q)
            lefts.append(left_of(weight * gx, gz, SPAN))
        return matmul_t(
            jnp.concatenate(lefts, 1),
            jnp.concatenate([gy[at[0]], gy[at[1]]], 1),
        )

    def start_members(step_at, carry):
        for part in range(start_group):
            member = start_group * step_at + part
            rho[member] = own_splat(member, 0, part)
        return carry

    start_group = min(members, 4)
    lax.fori_loop(0, members // start_group, start_members, 0)

    def more_pair(unit, part):
        code = more_list[unit]
        member, block = split(code)
        rho[member] += own_splat(member, block, part)

    side_group = gy_side.shape[0]

    def side_units(step_at):
        for part in range(side_group):
            unit = side_group * step_at + part
            code = side_list[jnp.minimum(unit, side_count - 1)]
            place, block = split(code)
            is_near = place < members
            member = jnp.where(is_near, place, place - members)
            above = jnp.where(is_near, 1 - odd, odd)
            block = pl.ds(block, 1)
            keep = jnp.where(unit < side_count, 1.0, 0.0)
            lower = CX * above
            shift = (REACH - CX + 2 * CX * above).astype(jnp.float32)
            frac_x, frac_y, frac_z, q, power, weight = tables.fields(
                [sides[place, f, block, :] for f in range(FIELDS)]
            )
            gx, _ = tables.x(frac_x, power, shift, lower, LAP, False)
            gz, _ = tables.z(frac_z, power)
            tables.y(gy_side.at[part], None, frac_y, power, q)
            side_left = left_of(weight * keep * gx, gz, LAP)
            at = pl.ds(pl.multiple_of(lower * zp, 16), LAP * zp)
            rho[member, at, :] += matmul_t(side_left, gy_side[part])

    def both(step_at, carry):
        more_pair(step_at, 0)
        side_units(step_at)
        return carry

    def more_alone(step_at, carry):
        more_pair(step_at, 0)
        return carry

    def side_alone(step_at, carry):
        side_units(step_at)
        return carry

    side_steps = (side_count + side_group - 1) // side_group
    shared = jnp.minimum(more_count, side_steps)
    lax.fori_loop(0, shared, both, 0)
    lax.fori_loop(shared, more_count, more_alone, 0)
    lax.fori_loop(shared, side_steps, side_alone, 0)
    fetch.wait()


def pull_kernel(members, zp, zs, stash, atoms_ref, near_target, far_target, rho, wanted, *rest):
    if stash:
        gy, slope, *rest = rest
        mean_ref, *outs, grad, mean_vmem, pulled, rows, forces, pull_list, sem = rest
    else:
        mean_ref, *outs, grad, mean_vmem, pulled, rows, forces, pull_list, sem, gy, slope = rest
    odd = lax.rem(lax.axis_index("sx"), 2)

    def list_member(member, count):
        return listed(pull_list, count, 0, 1, member * BLOCKS, live_of(atoms_ref, member))

    pull_count = lax.fori_loop(0, members, list_member, jnp.int32(0), unroll=members <= 4)
    forces[...] = jnp.zeros_like(forces)
    grad[:, :, NY - 96 :] = jnp.zeros((members, SPAN * zp, LANES - NY + 96), jnp.bfloat16)
    if not stash:
        zero_tails(gy, slope)
    tables = Tables(zp, zs, atoms_ref)

    group = max(1, 16 // zp)

    def gradient(first_plane, goal, means, t, carry):
        at = pl.ds(pl.multiple_of((first_plane + t * group) * zp, 16), group * zp)
        planes = pl.ds(t * group, group)
        here = [rho[m, at, 0:NY] for m in range(members)]
        first = functools.reduce(jnp.add, here)
        second = functools.reduce(jnp.add, [f * f for f in here])
        mean = first * (1.0 / members)
        spread = second * (1.0 / members) - mean * mean
        noise = noise_floor + spread * (1.0 / members)
        guess = pl.reciprocal(noise, approx=True)
        inv = guess * (2.0 - noise * guess)
        pull = (goal[planes].reshape(group * zp, NY) - mean) * inv
        gain = (inv - pull * pull) * (1.0 / (members * members))
        offset = pull * (-1.0 / members) - gain * mean
        for m in range(members):
            grad[m, at, 0:NY] = (offset + gain * here[m]).astype(jnp.bfloat16)
        if means is not None:
            means[planes] = mean.reshape(group, zp, NY)
        return carry

    for first_plane, goal, means in (
        (REACH, wanted, mean_vmem),
        ((REACH + CX) * (1 - odd), near_target, None),
        ((REACH + CX) * odd, far_target, None),
    ):
        steps = goal.shape[0] // group
        lax.fori_loop(0, steps, functools.partial(gradient, first_plane, goal, means), 0, unroll=3)
    give = pltpu.make_async_copy(mean_vmem, mean_ref, sem)
    give.start()

    pull_group = pulled.shape[0]

    def pull_units(first_unit, units):
        for part in range(units):
            code = pull_list[jnp.minimum(first_unit + part, pull_count - 1)]
            member, block = split(code)
            frac_x, frac_y, frac_z, q, power, weight = tables.own_fields(member, block)
            gx, off_x = tables.x(frac_x, power, REACH, 0, SPAN, True)
            gz, off_z = tables.z(frac_z, power)
            rows[part, 0:SPAN] = gx
            rows[part, SPAN : 2 * SPAN] = gx * off_x * q
            slot = code if stash else part
            if not stash:
                tables.y(gy.at[slot], slope.at[slot], frac_y, power, q)
            got = jnp.dot(
                grad[member], jnp.concatenate([gy[slot], slope[slot]], 1),
                preferred_element_type=jnp.float32,
            )
            sum_x = jnp.zeros((zp, BLOCK), jnp.float32)
            sum_y = jnp.zeros((zp, BLOCK), jnp.float32)
            sum_z = jnp.zeros((zp, BLOCK), jnp.float32)
            for t in range(SPAN):
                plain = got[t * zp : (t + 1) * zp, 0:BLOCK]
                slanted = got[t * zp : (t + 1) * zp, BLOCK:]
                here = rows[part, t : t + 1]
                sum_x += rows[part, SPAN + t : SPAN + t + 1] * plain
                sum_y += here * slanted
                sum_z += here * plain
            at = pl.ds(block, 1)
            forces[member, 0, at] = weight * jnp.sum(sum_x * gz, 0, keepdims=True)
            forces[member, 1, at] = weight * jnp.sum(sum_y * gz, 0, keepdims=True)
            forces[member, 2, at] = weight * jnp.sum(sum_z * (gz * off_z * q), 0, keepdims=True)

    def pull_many(step_at, carry):
        pull_units(pull_group * step_at, pull_group)
        return carry

    def pull_two(step_at, carry):
        pull_units(2 * step_at, 2)
        return carry

    def pull_four(step_at, carry):
        pull_units(4 * step_at, 4)
        return carry

    eights = lax.shift_right_logical(pull_count, 3)
    fours = lax.shift_right_logical(pull_count, 2)
    lax.fori_loop(0, eights, pull_many, 0)
    lax.fori_loop(2 * eights, fours, pull_four, 0)
    lax.fori_loop(2 * fours, lax.shift_right_logical(pull_count + 1, 1), pull_two, 0)
    if len(outs) == 1:
        outs[0][...] = forces[...]
    else:
        for k, out in enumerate(outs):
            out[...] = forces[k]
    give.wait()


def shards(coords, widths, amplitudes, live_blocks, target_map):
    members = lax.axis_size("replica")
    bricks = lax.axis_size("sx")
    rank = lax.axis_index("replica")
    zs = NZ // members
    zp = max(zs, 8)
    sliced = zs % 8 == 0
    few = members <= 4 and members & (members - 1) == 0
    stash = members <= STASH_LIMIT
    blocks = (BLOCKS, BLOCK)
    vmem = pl.BlockSpec(memory_space=pltpu.VMEM)
    anywhere = pl.BlockSpec(memory_space=pl.ANY)

    target = target_map
    if not sliced:
        part = lax.dynamic_slice_in_dim(target_map, rank * zs, zs, 1)
        target = jnp.pad(part, ((0, 0), (0, zp - zs), (0, 0)))
    hbm = pl.BlockSpec(memory_space=pltpu.HBM)
    own = pl.pallas_call(
        pack_kernel,
        out_shape=jax.ShapeDtypeStruct((FIELDS,) + blocks, jnp.float32),
        in_specs=[hbm] * 3 + [pl.BlockSpec(memory_space=pltpu.SMEM)],
        out_specs=vmem,
        scratch_shapes=[pltpu.SemaphoreType.DMA((3,))],
        compiler_params=pltpu.CompilerParams(vmem_limit_bytes=4 * 1024 * 1024),
        name="pack",
    )(
        *(
            pltpu.with_memory_space_constraint(x, pltpu.HBM)
            for x in (coords.reshape((3,) + blocks), widths.reshape(blocks), amplitudes.reshape(blocks))
        ),
        live_blocks,
    )

    odd = lax.rem(lax.axis_index("sx"), 2)

    def edge(plane):
        z_first = rank * zs if sliced else 0
        return lax.dynamic_slice(target, (plane, z_first, 0), (REACH, zp, NY))

    near_edge, far_edge = edge((CX - REACH) * (1 - odd)), edge((CX - REACH) * odd)

    def swap(block, pairs):
        return lax.ppermute(block, "sx", pairs + [(b, a) for a, b in pairs])

    near_pairs = [(i, i + 1) for i in range(0, bricks - 1, 2)]
    far_pairs = [(i, i + 1) for i in range(1, bricks - 1, 2)]
    if bricks % 2 == 0 and bricks > 2:
        far_pairs.append((bricks - 1, 0))

    def across(block, k):
        return lax.ppermute(block, "replica", [(i, i ^ k) for i in range(members)])

    if few:
        got = {0: own}
        for k in (2, 3, 1):
            got[k] = across(own, k)
        everyone = jnp.stack([got[k] for k in range(members)])
        everyone, near_edge, far_edge = lax.optimization_barrier((everyone, near_edge, far_edge))
    else:
        everyone = lax.all_gather(own, "replica")
    far, near = swap(everyone, far_pairs), swap(everyone, near_pairs)
    near_edge, far_edge, _ = lax.optimization_barrier((near_edge, far_edge, everyone))
    far_target, near_target = swap(far_edge, far_pairs), swap(near_edge, near_pairs)

    force_shapes = (
        [jax.ShapeDtypeStruct((3,) + blocks, jnp.float32)] * members
        if few
        else [jax.ShapeDtypeStruct((members, 3) + blocks, jnp.float32)]
    )
    table = ((members * BLOCKS if stash else 8), LANES, BLOCK)
    tables = [jax.ShapeDtypeStruct(table, jnp.bfloat16)] * 2 if stash else []
    splat = pl.pallas_call(
        functools.partial(splat_kernel, members, zp, zs, sliced, stash),
        out_shape=[
            jax.ShapeDtypeStruct((members, SPAN * zp, LANES), jnp.float32),
            jax.ShapeDtypeStruct((CX, zp, NY), jnp.float32),
        ]
        + tables,
        in_specs=[vmem] * 3 + [hbm],
        out_specs=[vmem] * (2 + len(tables)),
        scratch_shapes=([] if stash else [pltpu.VMEM(table, jnp.bfloat16)])
        + [
            pltpu.VMEM((4, LANES, BLOCK), jnp.bfloat16),
            pltpu.VMEM((2 * members, FIELDS) + blocks, jnp.float32),
            pltpu.SMEM((members * BLOCKS + 1,), jnp.int32),
            pltpu.SMEM((2 * members * BLOCKS + 1,), jnp.int32),
            pltpu.SemaphoreType.DMA,
        ],
        compiler_params=pltpu.CompilerParams(vmem_limit_bytes=24 * 1024 * 1024),
        cost_estimate=pl.CostEstimate(flops=6_000_000_000, bytes_accessed=14_000_000, transcendentals=0),
        name="splat",
    )(everyone, near, far, pltpu.with_memory_space_constraint(target, pltpu.HBM))
    mean, *partial = pl.pallas_call(
        functools.partial(pull_kernel, members, zp, zs, stash),
        out_shape=[jax.ShapeDtypeStruct((CX, zp, NY), jnp.float32)] + force_shapes,
        in_specs=[vmem] * (3 + len(splat)),
        out_specs=[anywhere] + [vmem] * len(force_shapes),
        scratch_shapes=[
            pltpu.VMEM((members, SPAN * zp, LANES), jnp.bfloat16),
            pltpu.VMEM((CX, zp, NY), jnp.float32),
            pltpu.VMEM((8, SPAN * zp, 2 * BLOCK), jnp.float32),
            pltpu.VMEM((8, 2 * SPAN, BLOCK), jnp.float32),
            pltpu.VMEM((members, 3) + blocks, jnp.float32),
            pltpu.SMEM((members * BLOCKS + 1,), jnp.int32),
            pltpu.SemaphoreType.DMA,
        ]
        + ([] if stash else [pltpu.VMEM(table, jnp.bfloat16)] * 2),
        compiler_params=pltpu.CompilerParams(vmem_limit_bytes=(24 if stash else 40) * 1024 * 1024),
        cost_estimate=pl.CostEstimate(flops=6_000_000_000, bytes_accessed=14_000_000, transcendentals=0),
        name="pull",
    )(everyone, near_target, far_target, *splat)

    if few:
        forces = partial[0]
        for k in (2, 3, 1):
            forces = forces + across(partial[k], k)
    else:
        forces = lax.psum_scatter(partial[0], "replica", scatter_dimension=0)
    return mean[:, :zs], forces.reshape(3, 1, ATOMS_DEV)


def solution(mesh):
    placed = (
        P(None, ("groups", "replica"), "sx"),
        P(("groups", "replica"), "sx"),
        P(("groups", "replica"), "sx"),
        P(("groups", "replica"), "sx"),
        P(("groups", "sx"), None, None),
    )
    return jax.shard_map(
        shards,
        mesh=mesh,
        in_specs=placed,
        out_specs=(P(("groups", "sx"), "replica", None), P(None, ("groups", "replica"), "sx")),
        check_vma=False,
    )
```

```python
import functools
import math

import jax
import jax.numpy as jnp
from jax import lax
from jax.experimental import pallas as pl
from jax.experimental.pallas import tpu as pltpu
from jax.sharding import PartitionSpec as P

CX = 24
NZ = 64
NY = 480
REACH = 6
BLOCK = 128
BLOCKS = 8
ATOMS_DEV = 1024
SPAN = CX + 2 * REACH
LAP = 2 * REACH
LANES = 512
FIELDS = 5
HALF_LOG2E = 0.5 * math.log2(math.e)

noise_floor = 0.05


def pack_kernel(coords_ref, widths_ref, amplitudes_ref, live_ref, own_ref, sems):
    copies = [
        pltpu.make_async_copy(coords_ref, own_ref.at[pl.ds(0, 3)], sems.at[0]),
        pltpu.make_async_copy(widths_ref, own_ref.at[3], sems.at[1]),
        pltpu.make_async_copy(amplitudes_ref, own_ref.at[4], sems.at[2]),
    ]
    for copy in copies:
        copy.start()
    for copy in copies:
        copy.wait()
    block = lax.broadcasted_iota(jnp.int32, (BLOCKS, BLOCK), 0)
    own_ref[4] = jnp.where(block < live_ref[0, 0], own_ref[4], 0.0)


def live_of(ref, member):
    number = (lax.broadcasted_iota(jnp.int32, (BLOCKS, BLOCK), 0) + 1).astype(jnp.float32)
    return jnp.max(jnp.where(ref[member, 4] != 0.0, number, 0.0)).astype(jnp.int32)


def split(code):
    return lax.shift_right_logical(code, 3), code & 7


def listed(out, count, first, stride, base, live):
    for block in range(first, BLOCKS, stride):
        out[count] = base + block
        count = count + jnp.where(block < live, 1, 0)
    return count


class Tables:
    def __init__(self, zp, zs, atoms_ref):
        self.zp, self.zs, self.atoms_ref = zp, zs, atoms_ref
        self.brick = lax.axis_index("sx")
        self.last_plane = CX * lax.axis_size("sx")
        self.step = lax.broadcasted_iota(jnp.int32, (16, BLOCK), 0).astype(jnp.float32)
        step_z = lax.broadcasted_iota(jnp.int32, (zp, BLOCK), 0)
        self.own_z = (step_z < zs).astype(jnp.float32)
        self.cell_z = (step_z + lax.axis_index("replica") * zs).astype(jnp.float32)

    def fields(self, data):
        frac_x, frac_y, frac_z, width, weight = data
        inv = 1.0 / width
        q = inv * inv
        return frac_x, frac_y, frac_z, q, q * -HALF_LOG2E, weight

    def own_fields(self, member, block):
        return self.fields([self.atoms_ref[member, f, pl.ds(block, 1), :] for f in range(FIELDS)])

    def y(self, out, slopes, frac, power, q):
        base = self.step - NY * frac
        for k in range(NY // 16):
            off = base + float(16 * k)
            value = jnp.exp2(off * off * power)
            out[16 * k : 16 * k + 16, :] = value.astype(jnp.bfloat16)
            if slopes is not None:
                slopes[16 * k : 16 * k + 16, :] = (value * (off * q)).astype(jnp.bfloat16)

    def x(self, frac, power, shift, lower, count, edges):
        cell = lax.broadcasted_iota(jnp.int32, (count, BLOCK), 0) + lower
        off = cell.astype(jnp.float32) - (CX * frac + shift)
        value = jnp.exp2(off * off * power)
        if edges:
            plane = cell + (self.brick * CX - REACH)
            value = jnp.where((plane >= 0) & (plane < self.last_plane), value, 0.0)
        return value, off

    def z(self, frac, power):
        off = self.cell_z - NZ * frac
        value = jnp.exp2(off * off * power)
        return (value if self.zs == self.zp else value * self.own_z), off


def zero_tails(*tables):
    for table in tables:
        table[:, NY:, :] = jnp.zeros((table.shape[0], LANES - NY, BLOCK), jnp.bfloat16)


def splat_kernel(members, zp, zs, sliced, stash, stage, *refs):
    slope = None
    if stage == "own":
        atoms_ref, rho, gy, slope, more_list = refs
    elif stage == "side":
        atoms_ref, near_ref, far_ref, target_ref, _, _, _, rho, gy, slope, *refs = refs
        wanted, gy_side, sides, more_list, side_list, sem = refs
    else:
        atoms_ref, near_ref, far_ref, target_ref, rho, *refs = refs
        wanted, gy, gy_side, sides, more_list, side_list, sem = refs
    brick = lax.axis_index("sx")
    odd = lax.rem(brick, 2)
    inner = (brick > 0) & (brick < lax.axis_size("sx") - 1)

    if stage != "own":
        if sliced:
            z_first = pl.multiple_of(lax.axis_index("replica") * zs, 8)
            source = target_ref.at[:, pl.ds(z_first, zs), :]
        else:
            source = target_ref
        fetch = pltpu.make_async_copy(source, wanted, sem)
        fetch.start()

    def list_own(member, count):
        return listed(more_list, count, 2, 2, member * BLOCKS, live_of(atoms_ref, member))

    def list_sides(member, count):
        base = member * BLOCKS
        sides[member] = near_ref[member]
        sides[members + member] = far_ref[member]
        count = listed(side_list, count, 0, 1, base, live_of(near_ref, member))
        far = jnp.where(inner, live_of(far_ref, member), 0)
        return listed(side_list, count, 0, 1, members * BLOCKS + base, far)

    unroll = members <= 4
    more_count = lax.fori_loop(0, members, list_own, jnp.int32(0), unroll=unroll)
    if stage != "own":
        side_count = lax.fori_loop(0, members, list_sides, jnp.int32(0), unroll=unroll)
        zero_tails(gy_side)
    if stage != "side":
        zero_tails(gy)
    if stage == "own":
        zero_tails(slope)
    tables = Tables(zp, zs, atoms_ref)

    def left_of(scaled, gz, count):
        group = max(1, 16 // zp)
        made = []
        for t in range(0, count, group):
            pieces = [scaled[t + i : t + i + 1] * gz for i in range(group)]
            piece = pieces[0] if group == 1 else jnp.concatenate(pieces, 0)
            made.append(piece.astype(jnp.bfloat16))
        return jnp.concatenate(made, 0)

    def matmul_t(a, b):
        return lax.dot_general(a, b, (((1,), (1,)), ((), ())), preferred_element_type=jnp.float32)

    def own_splat(member, block, part):
        at = [member * BLOCKS + block + half if stash else 2 * part + half for half in range(2)]
        lefts = []
        for half in range(2):
            frac_x, frac_y, frac_z, q, power, weight = tables.own_fields(member, block + half)
            gx, _ = tables.x(frac_x, power, REACH, 0, SPAN, True)
            gz, _ = tables.z(frac_z, power)
            tables.y(gy.at[at[half]], slope.at[at[half]] if stash else None, frac_y, power, q)
            lefts.append(left_of(weight * gx, gz, SPAN))
        return matmul_t(
            jnp.concatenate(lefts, 1),
            jnp.concatenate([gy[at[0]], gy[at[1]]], 1),
        )

    def start_members(step_at, carry):
        for part in range(start_group):
            member = start_group * step_at + part
            rho[member] = own_splat(member, 0, part)
        return carry

    start_group = min(members, 4)
    if stage != "side":
        lax.fori_loop(0, members // start_group, start_members, 0)

    def more_pair(unit, part):
        code = more_list[unit]
        member, block = split(code)
        rho[member] += own_splat(member, block, part)

    def two_pairs(step_at, carry):
        more_pair(2 * step_at, 0)
        more_pair(2 * step_at + 1, 1)
        return carry

    early = jnp.minimum(lax.shift_right_logical(more_count, 1), 1)
    if stage == "own":
        lax.fori_loop(0, early, two_pairs, 0)
        return
    past = 2 * early if stage == "side" else 0

    side_group = gy_side.shape[0]

    def side_units(step_at):
        for part in range(side_group):
            unit = side_group * step_at + part
            code = side_list[jnp.minimum(unit, side_count - 1)]
            place, block = split(code)
            is_near = place < members
            member = jnp.where(is_near, place, place - members)
            above = jnp.where(is_near, 1 - odd, odd)
            block = pl.ds(block, 1)
            keep = jnp.where(unit < side_count, 1.0, 0.0)
            lower = CX * above
            shift = (REACH - CX + 2 * CX * above).astype(jnp.float32)
            frac_x, frac_y, frac_z, q, power, weight = tables.fields(
                [sides[place, f, block, :] for f in range(FIELDS)]
            )
            gx, _ = tables.x(frac_x, power, shift, lower, LAP, False)
            gz, _ = tables.z(frac_z, power)
            tables.y(gy_side.at[part], None, frac_y, power, q)
            side_left = left_of(weight * keep * gx, gz, LAP)
            at = pl.ds(pl.multiple_of(lower * zp, 16), LAP * zp)
            rho[member, at, :] += matmul_t(side_left, gy_side[part])

    def both(step_at, carry):
        more_pair(past + step_at, 0)
        side_units(step_at)
        return carry

    def more_alone(step_at, carry):
        more_pair(past + step_at, 0)
        return carry

    def side_alone(step_at, carry):
        side_units(step_at)
        return carry

    side_steps = (side_count + side_group - 1) // side_group
    shared = jnp.minimum(more_count - past, side_steps)
    lax.fori_loop(0, shared, both, 0)
    lax.fori_loop(shared, more_count - past, more_alone, 0)
    lax.fori_loop(shared, side_steps, side_alone, 0)
    fetch.wait()


def pull_kernel(members, zp, zs, stash, atoms_ref, near_target, far_target, rho, wanted, *rest):
    if stash:
        gy, slope, *rest = rest
        mean_ref, *outs, grad, mean_vmem, pulled, rows, forces, pull_list, sem = rest
    else:
        mean_ref, *outs, grad, mean_vmem, pulled, rows, forces, pull_list, sem, gy, slope = rest
    odd = lax.rem(lax.axis_index("sx"), 2)

    def list_member(member, count):
        return listed(pull_list, count, 0, 1, member * BLOCKS, live_of(atoms_ref, member))

    pull_count = lax.fori_loop(0, members, list_member, jnp.int32(0), unroll=members <= 4)
    forces[...] = jnp.zeros_like(forces)
    grad[:, :, NY - 96 :] = jnp.zeros((members, SPAN * zp, LANES - NY + 96), jnp.bfloat16)
    if not stash:
        zero_tails(gy, slope)
    tables = Tables(zp, zs, atoms_ref)

    group = max(1, 16 // zp)

    def gradient(first_plane, goal, means, t, carry):
        at = pl.ds(pl.multiple_of((first_plane + t * group) * zp, 16), group * zp)
        planes = pl.ds(t * group, group)
        here = [rho[m, at, 0:NY] for m in range(members)]
        first = functools.reduce(jnp.add, here)
        second = functools.reduce(jnp.add, [f * f for f in here])
        mean = first * (1.0 / members)
        spread = second * (1.0 / members) - mean * mean
        noise = noise_floor + spread * (1.0 / members)
        guess = pl.reciprocal(noise, approx=True)
        inv = guess * (2.0 - noise * guess)
        pull = (goal[planes].reshape(group * zp, NY) - mean) * inv
        gain = (inv - pull * pull) * (1.0 / (members * members))
        offset = pull * (-1.0 / members) - gain * mean
        for m in range(members):
            grad[m, at, 0:NY] = (offset + gain * here[m]).astype(jnp.bfloat16)
        if means is not None:
            means[planes] = mean.reshape(group, zp, NY)
        return carry

    for first_plane, goal, means in (
        (REACH, wanted, mean_vmem),
        ((REACH + CX) * (1 - odd), near_target, None),
        ((REACH + CX) * odd, far_target, None),
    ):
        steps = goal.shape[0] // group
        lax.fori_loop(0, steps, functools.partial(gradient, first_plane, goal, means), 0, unroll=3)
    give = pltpu.make_async_copy(mean_vmem, mean_ref, sem)
    give.start()

    pull_group = pulled.shape[0]

    def pull_units(first_unit, units):
        for part in range(units):
            code = pull_list[jnp.minimum(first_unit + part, pull_count - 1)]
            member, block = split(code)
            frac_x, frac_y, frac_z, q, power, weight = tables.own_fields(member, block)
            gx, off_x = tables.x(frac_x, power, REACH, 0, SPAN, True)
            gz, off_z = tables.z(frac_z, power)
            rows[part, 0:SPAN] = gx
            rows[part, SPAN : 2 * SPAN] = gx * off_x * q
            slot = code if stash else part
            if not stash:
                tables.y(gy.at[slot], slope.at[slot], frac_y, power, q)
            got = jnp.dot(
                grad[member], jnp.concatenate([gy[slot], slope[slot]], 1),
                preferred_element_type=jnp.float32,
            )
            sum_x = jnp.zeros((zp, BLOCK), jnp.float32)
            sum_y = jnp.zeros((zp, BLOCK), jnp.float32)
            sum_z = jnp.zeros((zp, BLOCK), jnp.float32)
            for t in range(SPAN):
                plain = got[t * zp : (t + 1) * zp, 0:BLOCK]
                slanted = got[t * zp : (t + 1) * zp, BLOCK:]
                here = rows[part, t : t + 1]
                sum_x += rows[part, SPAN + t : SPAN + t + 1] * plain
                sum_y += here * slanted
                sum_z += here * plain
            at = pl.ds(block, 1)
            forces[member, 0, at] = weight * jnp.sum(sum_x * gz, 0, keepdims=True)
            forces[member, 1, at] = weight * jnp.sum(sum_y * gz, 0, keepdims=True)
            forces[member, 2, at] = weight * jnp.sum(sum_z * (gz * off_z * q), 0, keepdims=True)

    def pull_many(step_at, carry):
        pull_units(pull_group * step_at, pull_group)
        return carry

    def pull_two(step_at, carry):
        pull_units(2 * step_at, 2)
        return carry

    def pull_four(step_at, carry):
        pull_units(4 * step_at, 4)
        return carry

    eights = lax.shift_right_logical(pull_count, 3)
    fours = lax.shift_right_logical(pull_count, 2)
    lax.fori_loop(0, eights, pull_many, 0)
    lax.fori_loop(2 * eights, fours, pull_four, 0)
    lax.fori_loop(2 * fours, lax.shift_right_logical(pull_count + 1, 1), pull_two, 0)
    if len(outs) == 1:
        outs[0][...] = forces[...]
    else:
        for k, out in enumerate(outs):
            out[...] = forces[k]
    give.wait()


def shards(coords, widths, amplitudes, live_blocks, target_map):
    members = lax.axis_size("replica")
    bricks = lax.axis_size("sx")
    rank = lax.axis_index("replica")
    zs = NZ // members
    zp = max(zs, 8)
    sliced = zs % 8 == 0
    few = members <= 4 and members & (members - 1) == 0
    stash = few
    blocks = (BLOCKS, BLOCK)
    vmem = pl.BlockSpec(memory_space=pltpu.VMEM)
    anywhere = pl.BlockSpec(memory_space=pl.ANY)

    target = target_map
    if not sliced:
        part = lax.dynamic_slice_in_dim(target_map, rank * zs, zs, 1)
        target = jnp.pad(part, ((0, 0), (0, zp - zs), (0, 0)))
    hbm = pl.BlockSpec(memory_space=pltpu.HBM)
    own = pl.pallas_call(
        pack_kernel,
        out_shape=jax.ShapeDtypeStruct((FIELDS,) + blocks, jnp.float32),
        in_specs=[hbm] * 3 + [pl.BlockSpec(memory_space=pltpu.SMEM)],
        out_specs=vmem,
        scratch_shapes=[pltpu.SemaphoreType.DMA((3,))],
        compiler_params=pltpu.CompilerParams(vmem_limit_bytes=4 * 1024 * 1024),
        name="pack",
    )(
        *(
            pltpu.with_memory_space_constraint(x, pltpu.HBM)
            for x in (coords.reshape((3,) + blocks), widths.reshape(blocks), amplitudes.reshape(blocks))
        ),
        live_blocks,
    )

    odd = lax.rem(lax.axis_index("sx"), 2)

    def edge(plane):
        z_first = rank * zs if sliced else 0
        return lax.dynamic_slice(target, (plane, z_first, 0), (REACH, zp, NY))

    near_edge, far_edge = edge((CX - REACH) * (1 - odd)), edge((CX - REACH) * odd)

    def swap(block, pairs):
        return lax.ppermute(block, "sx", pairs + [(b, a) for a, b in pairs])

    near_pairs = [(i, i + 1) for i in range(0, bricks - 1, 2)]
    far_pairs = [(i, i + 1) for i in range(1, bricks - 1, 2)]
    if bricks % 2 == 0 and bricks > 2:
        far_pairs.append((bricks - 1, 0))

    def across(block, k):
        return lax.ppermute(block, "replica", [(i, i ^ k) for i in range(members)])

    if few:
        got = {0: own}
        for k in (2, 3, 1):
            got[k] = across(own, k)
        everyone = jnp.stack([got[k] for k in range(members)])
        everyone, near_edge, far_edge = lax.optimization_barrier((everyone, near_edge, far_edge))
    else:
        everyone = lax.all_gather(own, "replica")
    far, near = swap(everyone, far_pairs), swap(everyone, near_pairs)
    near_edge, far_edge, _ = lax.optimization_barrier((near_edge, far_edge, everyone))
    far_target, near_target = swap(far_edge, far_pairs), swap(near_edge, near_pairs)

    force_shapes = (
        [jax.ShapeDtypeStruct((3,) + blocks, jnp.float32)] * members
        if few
        else [jax.ShapeDtypeStruct((members, 3) + blocks, jnp.float32)]
    )
    table = ((members * BLOCKS if stash else 8), LANES, BLOCK)
    kept = [((members, SPAN * zp, LANES), jnp.float32)] + [(table, jnp.bfloat16)] * (2 if stash else 0)
    goal = jax.ShapeDtypeStruct((CX, zp, NY), jnp.float32)
    lists = [pltpu.SMEM((n * members * BLOCKS + 1,), jnp.int32) for n in (1, 2)]
    work = [
        pltpu.VMEM((4, LANES, BLOCK), jnp.bfloat16),
        pltpu.VMEM((2 * members, FIELDS) + blocks, jnp.float32),
        *lists,
        pltpu.SemaphoreType.DMA,
    ]
    params = pltpu.CompilerParams(vmem_limit_bytes=24 * 1024 * 1024)
    goal_source = pltpu.with_memory_space_constraint(target, pltpu.HBM)
    if few:
        kept = [pltpu.VMEM(*k) for k in kept]
        first = pl.pallas_call(
            functools.partial(splat_kernel, members, zp, zs, sliced, stash, "own"),
            out_shape=kept,
            in_specs=[vmem],
            out_specs=[vmem] * 3,
            scratch_shapes=lists[:1],
            compiler_params=params,
            cost_estimate=pl.CostEstimate(flops=2_000_000_000, bytes_accessed=1_000_000, transcendentals=0),
            name="splat_own",
        )(everyone)
        first = [pltpu.with_memory_space_constraint(x, pltpu.VMEM) for x in first]
        *splat, wanted = pl.pallas_call(
            functools.partial(splat_kernel, members, zp, zs, sliced, stash, "side"),
            out_shape=kept + [goal],
            in_specs=[vmem] * 3 + [hbm] + [vmem] * 3,
            out_specs=[vmem] * 4,
            scratch_shapes=work,
            input_output_aliases={4: 0, 5: 1, 6: 2},
            compiler_params=params,
            cost_estimate=pl.CostEstimate(flops=500_000_000, bytes_accessed=1_000_000, transcendentals=0),
            name="splat_side",
        )(everyone, near, far, goal_source, *first)
        splat.insert(1, wanted)
    else:
        splat = pl.pallas_call(
            functools.partial(splat_kernel, members, zp, zs, sliced, stash, "all"),
            out_shape=[jax.ShapeDtypeStruct(*kept[0]), goal],
            in_specs=[vmem] * 3 + [hbm],
            out_specs=[vmem] * 2,
            scratch_shapes=[pltpu.VMEM(table, jnp.bfloat16)] + work,
            compiler_params=params,
            cost_estimate=pl.CostEstimate(flops=6_000_000_000, bytes_accessed=14_000_000, transcendentals=0),
            name="splat",
        )(everyone, near, far, goal_source)
    mean, *partial = pl.pallas_call(
        functools.partial(pull_kernel, members, zp, zs, stash),
        out_shape=[jax.ShapeDtypeStruct((CX, zp, NY), jnp.float32)] + force_shapes,
        in_specs=[vmem] * (3 + len(splat)),
        out_specs=[anywhere] + [vmem] * len(force_shapes),
        scratch_shapes=[
            pltpu.VMEM((members, SPAN * zp, LANES), jnp.bfloat16),
            pltpu.VMEM((CX, zp, NY), jnp.float32),
            pltpu.VMEM((8, SPAN * zp, 2 * BLOCK), jnp.float32),
            pltpu.VMEM((8, 2 * SPAN, BLOCK), jnp.float32),
            pltpu.VMEM((members, 3) + blocks, jnp.float32),
            pltpu.SMEM((members * BLOCKS + 1,), jnp.int32),
            pltpu.SemaphoreType.DMA,
        ]
        + ([] if stash else [pltpu.VMEM(table, jnp.bfloat16)] * 2),
        compiler_params=pltpu.CompilerParams(vmem_limit_bytes=(24 if stash else 40) * 1024 * 1024),
        cost_estimate=pl.CostEstimate(flops=6_000_000_000, bytes_accessed=14_000_000, transcendentals=0),
        name="pull",
    )(everyone, near_target, far_target, *splat)

    if few:
        forces = partial[0]
        for k in (2, 3, 1):
            forces = forces + across(partial[k], k)
    else:
        forces = lax.psum_scatter(partial[0], "replica", scatter_dimension=0)
    return mean[:, :zs], forces.reshape(3, 1, ATOMS_DEV)


def solution(mesh):
    placed = (
        P(None, ("groups", "replica"), "sx"),
        P(("groups", "replica"), "sx"),
        P(("groups", "replica"), "sx"),
        P(("groups", "replica"), "sx"),
        P(("groups", "sx"), None, None),
    )
    return jax.shard_map(
        shards,
        mesh=mesh,
        in_specs=placed,
        out_specs=(P(("groups", "sx"), "replica", None), P(None, ("groups", "replica"), "sx")),
        check_vma=False,
    )
```

```python
import functools
import math

import jax
import jax.numpy as jnp
from jax import lax
from jax.experimental import pallas as pl
from jax.experimental.pallas import tpu as pltpu
from jax.sharding import PartitionSpec as P

CX = 24
NZ = 64
NY = 480
REACH = 6
BLOCK = 128
BLOCKS = 8
ATOMS_DEV = 1024
SPAN = CX + 2 * REACH
LAP = 2 * REACH
LANES = 512
FIELDS = 5
HALF_LOG2E = 0.5 * math.log2(math.e)

noise_floor = 0.05


def pack_kernel(coords_ref, widths_ref, amplitudes_ref, live_ref, own_ref, sems):
    copies = [
        pltpu.make_async_copy(coords_ref, own_ref.at[pl.ds(0, 3)], sems.at[0]),
        pltpu.make_async_copy(widths_ref, own_ref.at[3], sems.at[1]),
        pltpu.make_async_copy(amplitudes_ref, own_ref.at[4], sems.at[2]),
    ]
    for copy in copies:
        copy.start()
    for copy in copies:
        copy.wait()
    block = lax.broadcasted_iota(jnp.int32, (BLOCKS, BLOCK), 0)
    own_ref[4] = jnp.where(block < live_ref[0, 0], own_ref[4], 0.0)


def live_of(ref, member):
    number = (lax.broadcasted_iota(jnp.int32, (BLOCKS, BLOCK), 0) + 1).astype(jnp.float32)
    return jnp.max(jnp.where(ref[member, 4] != 0.0, number, 0.0)).astype(jnp.int32)


def split(code):
    return lax.shift_right_logical(code, 3), code & 7


def listed(out, count, first, stride, base, live):
    for block in range(first, BLOCKS, stride):
        out[count] = base + block
        count = count + jnp.where(block < live, 1, 0)
    return count


class Tables:
    def __init__(self, zp, zs, atoms_ref):
        self.zp, self.zs, self.atoms_ref = zp, zs, atoms_ref
        self.brick = lax.axis_index("sx")
        self.last_plane = CX * lax.axis_size("sx")
        self.step = lax.broadcasted_iota(jnp.int32, (16, BLOCK), 0).astype(jnp.float32)
        step_z = lax.broadcasted_iota(jnp.int32, (zp, BLOCK), 0)
        self.own_z = (step_z < zs).astype(jnp.float32)
        self.cell_z = (step_z + lax.axis_index("replica") * zs).astype(jnp.float32)

    def fields(self, data):
        frac_x, frac_y, frac_z, width, weight = data
        inv = 1.0 / width
        q = inv * inv
        return frac_x, frac_y, frac_z, q, q * -HALF_LOG2E, weight

    def own_fields(self, member, block):
        return self.fields([self.atoms_ref[member, f, pl.ds(block, 1), :] for f in range(FIELDS)])

    def y(self, out, slopes, frac, power, q):
        base = self.step - NY * frac
        for k in range(NY // 16):
            off = base + float(16 * k)
            value = jnp.exp2(off * off * power)
            out[16 * k : 16 * k + 16, :] = value.astype(jnp.bfloat16)
            if slopes is not None:
                slopes[16 * k : 16 * k + 16, :] = (value * (off * q)).astype(jnp.bfloat16)

    def x(self, frac, power, shift, lower, count, edges):
        cell = lax.broadcasted_iota(jnp.int32, (count, BLOCK), 0) + lower
        off = cell.astype(jnp.float32) - (CX * frac + shift)
        value = jnp.exp2(off * off * power)
        if edges:
            plane = cell + (self.brick * CX - REACH)
            value = jnp.where((plane >= 0) & (plane < self.last_plane), value, 0.0)
        return value, off

    def z(self, frac, power):
        off = self.cell_z - NZ * frac
        value = jnp.exp2(off * off * power)
        return (value if self.zs == self.zp else value * self.own_z), off


def zero_tails(*tables):
    for table in tables:
        table[:, NY:, :] = jnp.zeros((table.shape[0], LANES - NY, BLOCK), jnp.bfloat16)


def splat_kernel(members, zp, zs, sliced, stash, stage, *refs):
    slope = None
    if stage == "own":
        atoms_ref, rho, gy, slope, more_list = refs
    elif stage == "side":
        atoms_ref, near_ref, far_ref, target_ref, _, _, _, rho, gy, slope, *refs = refs
        wanted, gy_side, sides, more_list, side_list, sem = refs
    else:
        atoms_ref, near_ref, far_ref, target_ref, rho, *refs = refs
        wanted, gy, gy_side, sides, more_list, side_list, sem = refs
    brick = lax.axis_index("sx")
    odd = lax.rem(brick, 2)
    inner = (brick > 0) & (brick < lax.axis_size("sx") - 1)

    if stage != "own":
        if sliced:
            z_first = pl.multiple_of(lax.axis_index("replica") * zs, 8)
            source = target_ref.at[:, pl.ds(z_first, zs), :]
        else:
            source = target_ref
        fetch = pltpu.make_async_copy(source, wanted, sem)
        fetch.start()

    def list_own(member, count):
        return listed(more_list, count, 2, 2, member * BLOCKS, live_of(atoms_ref, member))

    def list_sides(member, count):
        base = member * BLOCKS
        sides[member] = near_ref[member]
        sides[members + member] = far_ref[member]
        count = listed(side_list, count, 0, 1, base, live_of(near_ref, member))
        far = jnp.where(inner, live_of(far_ref, member), 0)
        return listed(side_list, count, 0, 1, members * BLOCKS + base, far)

    unroll = members <= 4
    more_count = lax.fori_loop(0, members, list_own, jnp.int32(0), unroll=unroll)
    if stage != "own":
        side_count = lax.fori_loop(0, members, list_sides, jnp.int32(0), unroll=unroll)
        zero_tails(gy_side)
    if stage != "side":
        zero_tails(gy)
    if stage == "own":
        zero_tails(slope)
    tables = Tables(zp, zs, atoms_ref)

    def left_of(scaled, gz, count):
        group = max(1, 16 // zp)
        made = []
        for t in range(0, count, group):
            pieces = [scaled[t + i : t + i + 1] * gz for i in range(group)]
            piece = pieces[0] if group == 1 else jnp.concatenate(pieces, 0)
            made.append(piece.astype(jnp.bfloat16))
        return jnp.concatenate(made, 0)

    def matmul_t(a, b):
        return lax.dot_general(a, b, (((1,), (1,)), ((), ())), preferred_element_type=jnp.float32)

    def own_splat(member, block, part):
        at = [member * BLOCKS + block + half if stash else 2 * part + half for half in range(2)]
        lefts = []
        for half in range(2):
            frac_x, frac_y, frac_z, q, power, weight = tables.own_fields(member, block + half)
            gx, _ = tables.x(frac_x, power, REACH, 0, SPAN, True)
            gz, _ = tables.z(frac_z, power)
            tables.y(gy.at[at[half]], slope.at[at[half]] if stash else None, frac_y, power, q)
            lefts.append(left_of(weight * gx, gz, SPAN))
        return matmul_t(
            jnp.concatenate(lefts, 1),
            jnp.concatenate([gy[at[0]], gy[at[1]]], 1),
        )

    def start_members(step_at, carry):
        for part in range(start_group):
            member = start_group * step_at + part
            rho[member] = own_splat(member, 0, part)
        return carry

    start_group = min(members, 4)
    if stage != "side":
        lax.fori_loop(0, members // start_group, start_members, 0)

    def more_pair(unit, part):
        code = more_list[unit]
        member, block = split(code)
        rho[member] += own_splat(member, block, part)

    def two_pairs(step_at, carry):
        more_pair(2 * step_at, 0)
        more_pair(2 * step_at + 1, 1)
        return carry

    early = jnp.minimum(lax.shift_right_logical(more_count, 1), 1)
    if stage == "own":
        lax.fori_loop(0, early, two_pairs, 0)
        return
    past = 2 * early if stage == "side" else 0

    side_group = gy_side.shape[0]

    def side_units(step_at):
        for part in range(side_group):
            unit = side_group * step_at + part
            code = side_list[jnp.minimum(unit, side_count - 1)]
            place, block = split(code)
            is_near = place < members
            member = jnp.where(is_near, place, place - members)
            above = jnp.where(is_near, 1 - odd, odd)
            block = pl.ds(block, 1)
            keep = jnp.where(unit < side_count, 1.0, 0.0)
            lower = CX * above
            shift = (REACH - CX + 2 * CX * above).astype(jnp.float32)
            frac_x, frac_y, frac_z, q, power, weight = tables.fields(
                [sides[place, f, block, :] for f in range(FIELDS)]
            )
            gx, _ = tables.x(frac_x, power, shift, lower, LAP, False)
            gz, _ = tables.z(frac_z, power)
            tables.y(gy_side.at[part], None, frac_y, power, q)
            side_left = left_of(weight * keep * gx, gz, LAP)
            at = pl.ds(pl.multiple_of(lower * zp, 16), LAP * zp)
            rho[member, at, :] += matmul_t(side_left, gy_side[part])

    def both(step_at, carry):
        more_pair(past + step_at, 0)
        side_units(step_at)
        return carry

    def more_alone(step_at, carry):
        more_pair(past + step_at, 0)
        return carry

    def side_alone(step_at, carry):
        side_units(step_at)
        return carry

    side_steps = (side_count + side_group - 1) // side_group
    shared = jnp.minimum(more_count - past, side_steps)
    lax.fori_loop(0, shared, both, 0)
    lax.fori_loop(shared, more_count - past, more_alone, 0)
    lax.fori_loop(shared, side_steps, side_alone, 0)
    fetch.wait()


def pull_kernel(members, zp, zs, stash, atoms_ref, near_target, far_target, rho, wanted, *rest):
    if stash:
        gy, slope, *rest = rest
        mean_ref, *outs, grad, mean_vmem, pulled, rows, forces, pull_list, sem = rest
    else:
        mean_ref, *outs, grad, mean_vmem, pulled, rows, forces, pull_list, sem, gy, slope = rest
    odd = lax.rem(lax.axis_index("sx"), 2)

    def list_member(member, count):
        return listed(pull_list, count, 0, 1, member * BLOCKS, live_of(atoms_ref, member))

    pull_count = lax.fori_loop(0, members, list_member, jnp.int32(0), unroll=members <= 4)
    forces[...] = jnp.zeros_like(forces)
    grad[:, :, NY - 96 :] = jnp.zeros((members, SPAN * zp, LANES - NY + 96), jnp.bfloat16)
    if not stash:
        zero_tails(gy, slope)
    tables = Tables(zp, zs, atoms_ref)

    group = max(1, 16 // zp)

    def gradient(first_plane, goal, means, t, carry):
        at = pl.ds(pl.multiple_of((first_plane + t * group) * zp, 16), group * zp)
        planes = pl.ds(t * group, group)
        here = [rho[m, at, 0:NY] for m in range(members)]
        first = functools.reduce(jnp.add, here)
        second = functools.reduce(jnp.add, [f * f for f in here])
        mean = first * (1.0 / members)
        spread = second * (1.0 / members) - mean * mean
        noise = noise_floor + spread * (1.0 / members)
        guess = pl.reciprocal(noise, approx=True)
        inv = guess * (2.0 - noise * guess)
        pull = (goal[planes].astype(jnp.float32).reshape(group * zp, NY) - mean) * inv
        gain = (inv - pull * pull) * (1.0 / (members * members))
        offset = pull * (-1.0 / members) - gain * mean
        for m in range(members):
            grad[m, at, 0:NY] = (offset + gain * here[m]).astype(jnp.bfloat16)
        if means is not None:
            means[planes] = mean.reshape(group, zp, NY)
        return carry

    for first_plane, goal, means in (
        (REACH, wanted, mean_vmem),
        ((REACH + CX) * (1 - odd), near_target, None),
        ((REACH + CX) * odd, far_target, None),
    ):
        steps = goal.shape[0] // group
        lax.fori_loop(0, steps, functools.partial(gradient, first_plane, goal, means), 0, unroll=3)
    give = pltpu.make_async_copy(mean_vmem, mean_ref, sem)
    give.start()

    pull_group = pulled.shape[0]

    def pull_units(first_unit, units):
        for part in range(units):
            code = pull_list[jnp.minimum(first_unit + part, pull_count - 1)]
            member, block = split(code)
            frac_x, frac_y, frac_z, q, power, weight = tables.own_fields(member, block)
            gx, off_x = tables.x(frac_x, power, REACH, 0, SPAN, True)
            gz, off_z = tables.z(frac_z, power)
            rows[part, 0:SPAN] = gx
            rows[part, SPAN : 2 * SPAN] = gx * off_x * q
            slot = code if stash else part
            if not stash:
                tables.y(gy.at[slot], slope.at[slot], frac_y, power, q)
            got = jnp.dot(
                grad[member], jnp.concatenate([gy[slot], slope[slot]], 1),
                preferred_element_type=jnp.float32,
            )
            sum_x = jnp.zeros((zp, BLOCK), jnp.float32)
            sum_y = jnp.zeros((zp, BLOCK), jnp.float32)
            sum_z = jnp.zeros((zp, BLOCK), jnp.float32)
            for t in range(SPAN):
                plain = got[t * zp : (t + 1) * zp, 0:BLOCK]
                slanted = got[t * zp : (t + 1) * zp, BLOCK:]
                here = rows[part, t : t + 1]
                sum_x += rows[part, SPAN + t : SPAN + t + 1] * plain
                sum_y += here * slanted
                sum_z += here * plain
            at = pl.ds(block, 1)
            forces[member, 0, at] = weight * jnp.sum(sum_x * gz, 0, keepdims=True)
            forces[member, 1, at] = weight * jnp.sum(sum_y * gz, 0, keepdims=True)
            forces[member, 2, at] = weight * jnp.sum(sum_z * (gz * off_z * q), 0, keepdims=True)

    def pull_many(step_at, carry):
        pull_units(pull_group * step_at, pull_group)
        return carry

    def pull_two(step_at, carry):
        pull_units(2 * step_at, 2)
        return carry

    def pull_four(step_at, carry):
        pull_units(4 * step_at, 4)
        return carry

    eights = lax.shift_right_logical(pull_count, 3)
    fours = lax.shift_right_logical(pull_count, 2)
    lax.fori_loop(0, eights, pull_many, 0)
    lax.fori_loop(2 * eights, fours, pull_four, 0)
    lax.fori_loop(2 * fours, lax.shift_right_logical(pull_count + 1, 1), pull_two, 0)
    if len(outs) == 1:
        outs[0][...] = forces[...]
    else:
        for k, out in enumerate(outs):
            out[...] = forces[k]
    give.wait()


def shards(coords, widths, amplitudes, live_blocks, target_map):
    members = lax.axis_size("replica")
    bricks = lax.axis_size("sx")
    rank = lax.axis_index("replica")
    zs = NZ // members
    zp = max(zs, 8)
    sliced = zs % 8 == 0
    few = members <= 4 and members & (members - 1) == 0
    stash = few
    blocks = (BLOCKS, BLOCK)
    vmem = pl.BlockSpec(memory_space=pltpu.VMEM)
    anywhere = pl.BlockSpec(memory_space=pl.ANY)

    target = target_map
    if not sliced:
        part = lax.dynamic_slice_in_dim(target_map, rank * zs, zs, 1)
        target = jnp.pad(part, ((0, 0), (0, zp - zs), (0, 0)))
    hbm = pl.BlockSpec(memory_space=pltpu.HBM)
    own = pl.pallas_call(
        pack_kernel,
        out_shape=jax.ShapeDtypeStruct((FIELDS,) + blocks, jnp.float32),
        in_specs=[hbm] * 3 + [pl.BlockSpec(memory_space=pltpu.SMEM)],
        out_specs=vmem,
        scratch_shapes=[pltpu.SemaphoreType.DMA((3,))],
        compiler_params=pltpu.CompilerParams(vmem_limit_bytes=4 * 1024 * 1024),
        name="pack",
    )(
        *(
            pltpu.with_memory_space_constraint(x, pltpu.HBM)
            for x in (coords.reshape((3,) + blocks), widths.reshape(blocks), amplitudes.reshape(blocks))
        ),
        live_blocks,
    )

    odd = lax.rem(lax.axis_index("sx"), 2)

    def edge(plane):
        z_first = rank * zs if sliced else 0
        block = lax.dynamic_slice(target, (plane, z_first, 0), (REACH, zp, NY))
        return block.astype(jnp.bfloat16)

    near_edge, far_edge = edge((CX - REACH) * (1 - odd)), edge((CX - REACH) * odd)

    def swap(block, pairs):
        return lax.ppermute(block, "sx", pairs + [(b, a) for a, b in pairs])

    near_pairs = [(i, i + 1) for i in range(0, bricks - 1, 2)]
    far_pairs = [(i, i + 1) for i in range(1, bricks - 1, 2)]
    if bricks % 2 == 0 and bricks > 2:
        far_pairs.append((bricks - 1, 0))

    def across(block, k):
        return lax.ppermute(block, "replica", [(i, i ^ k) for i in range(members)])

    if few:
        got = {0: own}
        for k in (2, 3, 1):
            got[k] = across(own, k)
        everyone = jnp.stack([got[k] for k in range(members)])
        everyone, near_edge, far_edge = lax.optimization_barrier((everyone, near_edge, far_edge))
    else:
        everyone = lax.all_gather(own, "replica")
    far, near = swap(everyone, far_pairs), swap(everyone, near_pairs)
    near_edge, far_edge, _ = lax.optimization_barrier((near_edge, far_edge, everyone))
    far_target, near_target = swap(far_edge, far_pairs), swap(near_edge, near_pairs)

    force_shapes = (
        [jax.ShapeDtypeStruct((3,) + blocks, jnp.float32)] * members
        if few
        else [jax.ShapeDtypeStruct((members, 3) + blocks, jnp.float32)]
    )
    table = ((members * BLOCKS if stash else 8), LANES, BLOCK)
    kept = [((members, SPAN * zp, LANES), jnp.float32)] + [(table, jnp.bfloat16)] * (2 if stash else 0)
    goal = jax.ShapeDtypeStruct((CX, zp, NY), jnp.float32)
    lists = [pltpu.SMEM((n * members * BLOCKS + 1,), jnp.int32) for n in (1, 2)]
    work = [
        pltpu.VMEM((4, LANES, BLOCK), jnp.bfloat16),
        pltpu.VMEM((2 * members, FIELDS) + blocks, jnp.float32),
        *lists,
        pltpu.SemaphoreType.DMA,
    ]
    params = pltpu.CompilerParams(vmem_limit_bytes=24 * 1024 * 1024)
    goal_source = pltpu.with_memory_space_constraint(target, pltpu.HBM)
    if few:
        kept = [pltpu.VMEM(*k) for k in kept]
        first = pl.pallas_call(
            functools.partial(splat_kernel, members, zp, zs, sliced, stash, "own"),
            out_shape=kept,
            in_specs=[vmem],
            out_specs=[vmem] * 3,
            scratch_shapes=lists[:1],
            compiler_params=params,
            cost_estimate=pl.CostEstimate(flops=2_000_000_000, bytes_accessed=1_000_000, transcendentals=0),
            name="splat_own",
        )(everyone)
        first = [pltpu.with_memory_space_constraint(x, pltpu.VMEM) for x in first]
        *splat, wanted = pl.pallas_call(
            functools.partial(splat_kernel, members, zp, zs, sliced, stash, "side"),
            out_shape=kept + [goal],
            in_specs=[vmem] * 3 + [hbm] + [vmem] * 3,
            out_specs=[vmem] * 4,
            scratch_shapes=work,
            input_output_aliases={4: 0, 5: 1, 6: 2},
            compiler_params=params,
            cost_estimate=pl.CostEstimate(flops=500_000_000, bytes_accessed=1_000_000, transcendentals=0),
            name="splat_side",
        )(everyone, near, far, goal_source, *first)
        splat.insert(1, wanted)
    else:
        splat = pl.pallas_call(
            functools.partial(splat_kernel, members, zp, zs, sliced, stash, "all"),
            out_shape=[jax.ShapeDtypeStruct(*kept[0]), goal],
            in_specs=[vmem] * 3 + [hbm],
            out_specs=[vmem] * 2,
            scratch_shapes=[pltpu.VMEM(table, jnp.bfloat16)] + work,
            compiler_params=params,
            cost_estimate=pl.CostEstimate(flops=6_000_000_000, bytes_accessed=14_000_000, transcendentals=0),
            name="splat",
        )(everyone, near, far, goal_source)
    mean, *partial = pl.pallas_call(
        functools.partial(pull_kernel, members, zp, zs, stash),
        out_shape=[jax.ShapeDtypeStruct((CX, zp, NY), jnp.float32)] + force_shapes,
        in_specs=[vmem] * (3 + len(splat)),
        out_specs=[anywhere] + [vmem] * len(force_shapes),
        scratch_shapes=[
            pltpu.VMEM((members, SPAN * zp, LANES), jnp.bfloat16),
            pltpu.VMEM((CX, zp, NY), jnp.float32),
            pltpu.VMEM((8, SPAN * zp, 2 * BLOCK), jnp.float32),
            pltpu.VMEM((8, 2 * SPAN, BLOCK), jnp.float32),
            pltpu.VMEM((members, 3) + blocks, jnp.float32),
            pltpu.SMEM((members * BLOCKS + 1,), jnp.int32),
            pltpu.SemaphoreType.DMA,
        ]
        + ([] if stash else [pltpu.VMEM(table, jnp.bfloat16)] * 2),
        compiler_params=pltpu.CompilerParams(vmem_limit_bytes=(24 if stash else 40) * 1024 * 1024),
        cost_estimate=pl.CostEstimate(flops=6_000_000_000, bytes_accessed=14_000_000, transcendentals=0),
        name="pull",
    )(everyone, near_target, far_target, *splat)

    if few:
        forces = partial[0]
        for k in (2, 3, 1):
            forces = forces + across(partial[k], k)
    else:
        forces = lax.psum_scatter(partial[0], "replica", scatter_dimension=0)
    return mean[:, :zs], forces.reshape(3, 1, ATOMS_DEV)


def solution(mesh):
    placed = (
        P(None, ("groups", "replica"), "sx"),
        P(("groups", "replica"), "sx"),
        P(("groups", "replica"), "sx"),
        P(("groups", "replica"), "sx"),
        P(("groups", "sx"), None, None),
    )
    return jax.shard_map(
        shards,
        mesh=mesh,
        in_specs=placed,
        out_specs=(P(("groups", "sx"), "replica", None), P(None, ("groups", "replica"), "sx")),
        check_vma=False,
    )
```

```python
import functools
import math

import jax
import jax.numpy as jnp
from jax import lax
from jax.experimental import pallas as pl
from jax.experimental.pallas import tpu as pltpu
from jax.sharding import PartitionSpec as P

CX = 24
NZ = 64
NY = 480
REACH = 6
BLOCK = 128
BLOCKS = 8
ATOMS_DEV = 1024
SPAN = CX + 2 * REACH
LAP = 2 * REACH
LANES = 512
FIELDS = 5
HALF_LOG2E = 0.5 * math.log2(math.e)

noise_floor = 0.05


def pack_kernel(coords_ref, widths_ref, amplitudes_ref, live_ref, own_ref, sems):
    copies = [
        pltpu.make_async_copy(coords_ref, own_ref.at[pl.ds(0, 3)], sems.at[0]),
        pltpu.make_async_copy(widths_ref, own_ref.at[3], sems.at[1]),
        pltpu.make_async_copy(amplitudes_ref, own_ref.at[4], sems.at[2]),
    ]
    for copy in copies:
        copy.start()
    for copy in copies:
        copy.wait()
    block = lax.broadcasted_iota(jnp.int32, (BLOCKS, BLOCK), 0)
    own_ref[4] = jnp.where(block < live_ref[0, 0], own_ref[4], 0.0)


def live_of(ref, member):
    number = (lax.broadcasted_iota(jnp.int32, (BLOCKS, BLOCK), 0) + 1).astype(jnp.float32)
    return jnp.max(jnp.where(ref[member, 4] != 0.0, number, 0.0)).astype(jnp.int32)


def split(code):
    return lax.shift_right_logical(code, 3), code & 7


def listed(out, count, first, stride, base, live):
    for block in range(first, BLOCKS, stride):
        out[count] = base + block
        count = count + jnp.where(block < live, 1, 0)
    return count


class Tables:
    def __init__(self, zp, zs, atoms_ref):
        self.zp, self.zs, self.atoms_ref = zp, zs, atoms_ref
        self.brick = lax.axis_index("sx")
        self.last_plane = CX * lax.axis_size("sx")
        self.step = lax.broadcasted_iota(jnp.int32, (16, BLOCK), 0).astype(jnp.float32)
        step_z = lax.broadcasted_iota(jnp.int32, (zp, BLOCK), 0)
        self.own_z = (step_z < zs).astype(jnp.float32)
        self.cell_z = (step_z + lax.axis_index("replica") * zs).astype(jnp.float32)

    def fields(self, data):
        frac_x, frac_y, frac_z, width, weight = data
        inv = 1.0 / width
        q = inv * inv
        return frac_x, frac_y, frac_z, q, q * -HALF_LOG2E, weight

    def own_fields(self, member, block):
        return self.fields([self.atoms_ref[member, f, pl.ds(block, 1), :] for f in range(FIELDS)])

    def y(self, out, slopes, frac, power, q):
        base = self.step - NY * frac
        for k in range(NY // 16):
            off = base + float(16 * k)
            value = jnp.exp2(off * off * power)
            out[16 * k : 16 * k + 16, :] = value.astype(jnp.bfloat16)
            if slopes is not None:
                slopes[16 * k : 16 * k + 16, :] = (value * (off * q)).astype(jnp.bfloat16)

    def x(self, frac, power, shift, lower, count, edges):
        cell = lax.broadcasted_iota(jnp.int32, (count, BLOCK), 0) + lower
        off = cell.astype(jnp.float32) - (CX * frac + shift)
        value = jnp.exp2(off * off * power)
        if edges:
            plane = cell + (self.brick * CX - REACH)
            value = jnp.where((plane >= 0) & (plane < self.last_plane), value, 0.0)
        return value, off

    def z(self, frac, power):
        off = self.cell_z - NZ * frac
        value = jnp.exp2(off * off * power)
        return (value if self.zs == self.zp else value * self.own_z), off


def zero_tails(*tables):
    for table in tables:
        table[:, NY:, :] = jnp.zeros((table.shape[0], LANES - NY, BLOCK), jnp.bfloat16)


def splat_kernel(members, zp, zs, sliced, stash, stage, *refs):
    slope = None
    if stage == "own":
        atoms_ref, rho, gy, slope, more_list = refs
    elif stage == "side":
        atoms_ref, near_ref, far_ref, target_ref, _, _, _, rho, gy, slope, *refs = refs
        wanted, gy_side, sides, more_list, side_list, sem = refs
    else:
        atoms_ref, near_ref, far_ref, target_ref, rho, *refs = refs
        wanted, gy, gy_side, sides, more_list, side_list, sem = refs
    brick = lax.axis_index("sx")
    odd = lax.rem(brick, 2)
    inner = (brick > 0) & (brick < lax.axis_size("sx") - 1)

    if stage != "own":
        if sliced:
            z_first = pl.multiple_of(lax.axis_index("replica") * zs, 8)
            source = target_ref.at[:, pl.ds(z_first, zs), :]
        else:
            source = target_ref
        fetch = pltpu.make_async_copy(source, wanted, sem)
        fetch.start()

    def list_own(member, count):
        return listed(more_list, count, 2, 2, member * BLOCKS, live_of(atoms_ref, member))

    def list_sides(member, count):
        base = member * BLOCKS
        sides[member] = near_ref[member]
        sides[members + member] = far_ref[member]
        count = listed(side_list, count, 0, 1, base, live_of(near_ref, member))
        far = jnp.where(inner, live_of(far_ref, member), 0)
        return listed(side_list, count, 0, 1, members * BLOCKS + base, far)

    unroll = members <= 4
    more_count = lax.fori_loop(0, members, list_own, jnp.int32(0), unroll=unroll)
    if stage != "own":
        side_count = lax.fori_loop(0, members, list_sides, jnp.int32(0), unroll=unroll)
        zero_tails(gy_side)
    if stage != "side":
        zero_tails(gy)
    if stage == "own":
        zero_tails(slope)
    tables = Tables(zp, zs, atoms_ref)

    def left_of(scaled, gz, count):
        group = max(1, 16 // zp)
        made = []
        for t in range(0, count, group):
            pieces = [scaled[t + i : t + i + 1] * gz for i in range(group)]
            piece = pieces[0] if group == 1 else jnp.concatenate(pieces, 0)
            made.append(piece.astype(jnp.bfloat16))
        return jnp.concatenate(made, 0)

    def matmul_t(a, b):
        return lax.dot_general(a, b, (((1,), (1,)), ((), ())), preferred_element_type=jnp.float32)

    def own_splat(member, block, part):
        at = [member * BLOCKS + block + half if stash else 2 * part + half for half in range(2)]
        lefts = []
        for half in range(2):
            frac_x, frac_y, frac_z, q, power, weight = tables.own_fields(member, block + half)
            gx, _ = tables.x(frac_x, power, REACH, 0, SPAN, True)
            gz, _ = tables.z(frac_z, power)
            tables.y(gy.at[at[half]], slope.at[at[half]] if stash else None, frac_y, power, q)
            lefts.append(left_of(weight * gx, gz, SPAN))
        return matmul_t(
            jnp.concatenate(lefts, 1),
            jnp.concatenate([gy[at[0]], gy[at[1]]], 1),
        )

    def start_members(step_at, carry):
        for part in range(start_group):
            member = start_group * step_at + part
            rho[member] = own_splat(member, 0, part)
        return carry

    start_group = min(members, 4)
    if stage != "side":
        lax.fori_loop(0, members // start_group, start_members, 0)

    def more_pair(unit, part):
        code = more_list[unit]
        member, block = split(code)
        rho[member] += own_splat(member, block, part)

    def two_pairs(step_at, carry):
        more_pair(2 * step_at, 0)
        more_pair(2 * step_at + 1, 1)
        return carry

    early = jnp.minimum(lax.shift_right_logical(more_count, 1), 2)
    if stage == "own":
        lax.fori_loop(0, early, two_pairs, 0)
        return
    past = 2 * early if stage == "side" else 0

    side_group = gy_side.shape[0]

    def side_units(step_at):
        for part in range(side_group):
            unit = side_group * step_at + part
            code = side_list[jnp.minimum(unit, side_count - 1)]
            place, block = split(code)
            is_near = place < members
            member = jnp.where(is_near, place, place - members)
            above = jnp.where(is_near, 1 - odd, odd)
            block = pl.ds(block, 1)
            keep = jnp.where(unit < side_count, 1.0, 0.0)
            lower = CX * above
            shift = (REACH - CX + 2 * CX * above).astype(jnp.float32)
            frac_x, frac_y, frac_z, q, power, weight = tables.fields(
                [sides[place, f, block, :] for f in range(FIELDS)]
            )
            gx, _ = tables.x(frac_x, power, shift, lower, LAP, False)
            gz, _ = tables.z(frac_z, power)
            tables.y(gy_side.at[part], None, frac_y, power, q)
            side_left = left_of(weight * keep * gx, gz, LAP)
            at = pl.ds(pl.multiple_of(lower * zp, 16), LAP * zp)
            rho[member, at, :] += matmul_t(side_left, gy_side[part])

    def both(step_at, carry):
        more_pair(past + step_at, 0)
        side_units(step_at)
        return carry

    def more_alone(step_at, carry):
        more_pair(past + step_at, 0)
        return carry

    def side_alone(step_at, carry):
        side_units(step_at)
        return carry

    side_steps = (side_count + side_group - 1) // side_group
    shared = jnp.minimum(more_count - past, side_steps)
    lax.fori_loop(0, shared, both, 0)
    lax.fori_loop(shared, more_count - past, more_alone, 0)
    lax.fori_loop(shared, side_steps, side_alone, 0)
    fetch.wait()


def pull_kernel(members, zp, zs, stash, atoms_ref, near_target, far_target, rho, wanted, *rest):
    if stash:
        gy, slope, *rest = rest
        mean_ref, *outs, grad, mean_vmem, pulled, rows, forces, pull_list, sem = rest
    else:
        mean_ref, *outs, grad, mean_vmem, pulled, rows, forces, pull_list, sem, gy, slope = rest
    odd = lax.rem(lax.axis_index("sx"), 2)

    def list_member(member, count):
        return listed(pull_list, count, 0, 1, member * BLOCKS, live_of(atoms_ref, member))

    pull_count = lax.fori_loop(0, members, list_member, jnp.int32(0), unroll=members <= 4)
    forces[...] = jnp.zeros_like(forces)
    grad[:, :, NY - 96 :] = jnp.zeros((members, SPAN * zp, LANES - NY + 96), jnp.bfloat16)
    if not stash:
        zero_tails(gy, slope)
    tables = Tables(zp, zs, atoms_ref)

    group = max(1, 16 // zp)

    def gradient(first_plane, goal, means, t, carry):
        at = pl.ds(pl.multiple_of((first_plane + t * group) * zp, 16), group * zp)
        planes = pl.ds(t * group, group)
        here = [rho[m, at, 0:NY] for m in range(members)]
        first = functools.reduce(jnp.add, here)
        second = functools.reduce(jnp.add, [f * f for f in here])
        mean = first * (1.0 / members)
        spread = second * (1.0 / members) - mean * mean
        noise = noise_floor + spread * (1.0 / members)
        guess = pl.reciprocal(noise, approx=True)
        inv = guess * (2.0 - noise * guess)
        pull = (goal[planes].astype(jnp.float32).reshape(group * zp, NY) - mean) * inv
        gain = (inv - pull * pull) * (1.0 / (members * members))
        offset = pull * (-1.0 / members) - gain * mean
        for m in range(members):
            grad[m, at, 0:NY] = (offset + gain * here[m]).astype(jnp.bfloat16)
        if means is not None:
            means[planes] = mean.reshape(group, zp, NY)
        return carry

    for first_plane, goal, means in (
        (REACH, wanted, mean_vmem),
        ((REACH + CX) * (1 - odd), near_target, None),
        ((REACH + CX) * odd, far_target, None),
    ):
        steps = goal.shape[0] // group
        lax.fori_loop(0, steps, functools.partial(gradient, first_plane, goal, means), 0, unroll=3)
    give = pltpu.make_async_copy(mean_vmem, mean_ref, sem)
    give.start()

    pull_group = pulled.shape[0]

    def pull_units(first_unit, units):
        for part in range(units):
            code = pull_list[jnp.minimum(first_unit + part, pull_count - 1)]
            member, block = split(code)
            frac_x, frac_y, frac_z, q, power, weight = tables.own_fields(member, block)
            gx, off_x = tables.x(frac_x, power, REACH, 0, SPAN, True)
            gz, off_z = tables.z(frac_z, power)
            rows[part, 0:SPAN] = gx
            rows[part, SPAN : 2 * SPAN] = gx * off_x * q
            slot = code if stash else part
            if not stash:
                tables.y(gy.at[slot], slope.at[slot], frac_y, power, q)
            got = jnp.dot(
                grad[member], jnp.concatenate([gy[slot], slope[slot]], 1),
                preferred_element_type=jnp.float32,
            )
            sum_x = jnp.zeros((zp, BLOCK), jnp.float32)
            sum_y = jnp.zeros((zp, BLOCK), jnp.float32)
            sum_z = jnp.zeros((zp, BLOCK), jnp.float32)
            for t in range(SPAN):
                plain = got[t * zp : (t + 1) * zp, 0:BLOCK]
                slanted = got[t * zp : (t + 1) * zp, BLOCK:]
                here = rows[part, t : t + 1]
                sum_x += rows[part, SPAN + t : SPAN + t + 1] * plain
                sum_y += here * slanted
                sum_z += here * plain
            at = pl.ds(block, 1)
            forces[member, 0, at] = weight * jnp.sum(sum_x * gz, 0, keepdims=True)
            forces[member, 1, at] = weight * jnp.sum(sum_y * gz, 0, keepdims=True)
            forces[member, 2, at] = weight * jnp.sum(sum_z * (gz * off_z * q), 0, keepdims=True)

    def pull_many(step_at, carry):
        pull_units(pull_group * step_at, pull_group)
        return carry

    def pull_two(step_at, carry):
        pull_units(2 * step_at, 2)
        return carry

    def pull_four(step_at, carry):
        pull_units(4 * step_at, 4)
        return carry

    eights = lax.shift_right_logical(pull_count, 3)
    fours = lax.shift_right_logical(pull_count, 2)
    lax.fori_loop(0, eights, pull_many, 0)
    lax.fori_loop(2 * eights, fours, pull_four, 0)
    lax.fori_loop(2 * fours, lax.shift_right_logical(pull_count + 1, 1), pull_two, 0)
    if len(outs) == 1:
        outs[0][...] = forces[...]
    else:
        for k, out in enumerate(outs):
            out[...] = forces[k]
    give.wait()


def shards(coords, widths, amplitudes, live_blocks, target_map):
    members = lax.axis_size("replica")
    bricks = lax.axis_size("sx")
    rank = lax.axis_index("replica")
    zs = NZ // members
    zp = max(zs, 8)
    sliced = zs % 8 == 0
    few = members <= 4 and members & (members - 1) == 0
    stash = few
    blocks = (BLOCKS, BLOCK)
    vmem = pl.BlockSpec(memory_space=pltpu.VMEM)
    anywhere = pl.BlockSpec(memory_space=pl.ANY)

    target = target_map
    if not sliced:
        part = lax.dynamic_slice_in_dim(target_map, rank * zs, zs, 1)
        target = jnp.pad(part, ((0, 0), (0, zp - zs), (0, 0)))
    hbm = pl.BlockSpec(memory_space=pltpu.HBM)
    own = pl.pallas_call(
        pack_kernel,
        out_shape=jax.ShapeDtypeStruct((FIELDS,) + blocks, jnp.float32),
        in_specs=[hbm] * 3 + [pl.BlockSpec(memory_space=pltpu.SMEM)],
        out_specs=vmem,
        scratch_shapes=[pltpu.SemaphoreType.DMA((3,))],
        compiler_params=pltpu.CompilerParams(vmem_limit_bytes=4 * 1024 * 1024),
        name="pack",
    )(
        *(
            pltpu.with_memory_space_constraint(x, pltpu.HBM)
            for x in (coords.reshape((3,) + blocks), widths.reshape(blocks), amplitudes.reshape(blocks))
        ),
        live_blocks,
    )

    odd = lax.rem(lax.axis_index("sx"), 2)

    def edge(plane):
        z_first = rank * zs if sliced else 0
        block = lax.dynamic_slice(target, (plane, z_first, 0), (REACH, zp, NY))
        return block.astype(jnp.bfloat16)

    near_edge, far_edge = edge((CX - REACH) * (1 - odd)), edge((CX - REACH) * odd)

    def swap(block, pairs):
        return lax.ppermute(block, "sx", pairs + [(b, a) for a, b in pairs])

    near_pairs = [(i, i + 1) for i in range(0, bricks - 1, 2)]
    far_pairs = [(i, i + 1) for i in range(1, bricks - 1, 2)]
    if bricks % 2 == 0 and bricks > 2:
        far_pairs.append((bricks - 1, 0))

    def across(block, k):
        return lax.ppermute(block, "replica", [(i, i ^ k) for i in range(members)])

    if few:
        got = {0: own}
        for k in (2, 3, 1):
            got[k] = across(own, k)
        everyone = jnp.stack([got[k] for k in range(members)])
        everyone, near_edge, far_edge = lax.optimization_barrier((everyone, near_edge, far_edge))
    else:
        everyone = lax.all_gather(own, "replica")
    far, near = swap(everyone, far_pairs), swap(everyone, near_pairs)
    near_edge, far_edge, _ = lax.optimization_barrier((near_edge, far_edge, everyone))
    far_target, near_target = swap(far_edge, far_pairs), swap(near_edge, near_pairs)

    force_shapes = (
        [jax.ShapeDtypeStruct((3,) + blocks, jnp.float32)] * members
        if few
        else [jax.ShapeDtypeStruct((members, 3) + blocks, jnp.float32)]
    )
    table = ((members * BLOCKS if stash else 8), LANES, BLOCK)
    kept = [((members, SPAN * zp, LANES), jnp.float32)] + [(table, jnp.bfloat16)] * (2 if stash else 0)
    goal = jax.ShapeDtypeStruct((CX, zp, NY), jnp.float32)
    lists = [pltpu.SMEM((n * members * BLOCKS + 1,), jnp.int32) for n in (1, 2)]
    work = [
        pltpu.VMEM((4, LANES, BLOCK), jnp.bfloat16),
        pltpu.VMEM((2 * members, FIELDS) + blocks, jnp.float32),
        *lists,
        pltpu.SemaphoreType.DMA,
    ]
    params = pltpu.CompilerParams(vmem_limit_bytes=24 * 1024 * 1024)
    goal_source = pltpu.with_memory_space_constraint(target, pltpu.HBM)
    if few:
        kept = [pltpu.VMEM(*k) for k in kept]
        first = pl.pallas_call(
            functools.partial(splat_kernel, members, zp, zs, sliced, stash, "own"),
            out_shape=kept,
            in_specs=[vmem],
            out_specs=[vmem] * 3,
            scratch_shapes=lists[:1],
            compiler_params=params,
            cost_estimate=pl.CostEstimate(flops=2_000_000_000, bytes_accessed=1_000_000, transcendentals=0),
            name="splat_own",
        )(everyone)
        first = [pltpu.with_memory_space_constraint(x, pltpu.VMEM) for x in first]
        *splat, wanted = pl.pallas_call(
            functools.partial(splat_kernel, members, zp, zs, sliced, stash, "side"),
            out_shape=kept + [goal],
            in_specs=[vmem] * 3 + [hbm] + [vmem] * 3,
            out_specs=[vmem] * 4,
            scratch_shapes=work,
            input_output_aliases={4: 0, 5: 1, 6: 2},
            compiler_params=params,
            cost_estimate=pl.CostEstimate(flops=500_000_000, bytes_accessed=1_000_000, transcendentals=0),
            name="splat_side",
        )(everyone, near, far, goal_source, *first)
        splat.insert(1, wanted)
    else:
        splat = pl.pallas_call(
            functools.partial(splat_kernel, members, zp, zs, sliced, stash, "all"),
            out_shape=[jax.ShapeDtypeStruct(*kept[0]), goal],
            in_specs=[vmem] * 3 + [hbm],
            out_specs=[vmem] * 2,
            scratch_shapes=[pltpu.VMEM(table, jnp.bfloat16)] + work,
            compiler_params=params,
            cost_estimate=pl.CostEstimate(flops=6_000_000_000, bytes_accessed=14_000_000, transcendentals=0),
            name="splat",
        )(everyone, near, far, goal_source)
    mean, *partial = pl.pallas_call(
        functools.partial(pull_kernel, members, zp, zs, stash),
        out_shape=[jax.ShapeDtypeStruct((CX, zp, NY), jnp.float32)] + force_shapes,
        in_specs=[vmem] * (3 + len(splat)),
        out_specs=[anywhere] + [vmem] * len(force_shapes),
        scratch_shapes=[
            pltpu.VMEM((members, SPAN * zp, LANES), jnp.bfloat16),
            pltpu.VMEM((CX, zp, NY), jnp.float32),
            pltpu.VMEM((8, SPAN * zp, 2 * BLOCK), jnp.float32),
            pltpu.VMEM((8, 2 * SPAN, BLOCK), jnp.float32),
            pltpu.VMEM((members, 3) + blocks, jnp.float32),
            pltpu.SMEM((members * BLOCKS + 1,), jnp.int32),
            pltpu.SemaphoreType.DMA,
        ]
        + ([] if stash else [pltpu.VMEM(table, jnp.bfloat16)] * 2),
        compiler_params=pltpu.CompilerParams(vmem_limit_bytes=(24 if stash else 40) * 1024 * 1024),
        cost_estimate=pl.CostEstimate(flops=6_000_000_000, bytes_accessed=14_000_000, transcendentals=0),
        name="pull",
    )(everyone, near_target, far_target, *splat)

    if few:
        forces = partial[0]
        for k in (2, 3, 1):
            forces = forces + across(partial[k], k)
    else:
        forces = lax.psum_scatter(partial[0], "replica", scatter_dimension=0)
    return mean[:, :zs], forces.reshape(3, 1, ATOMS_DEV)


def solution(mesh):
    placed = (
        P(None, ("groups", "replica"), "sx"),
        P(("groups", "replica"), "sx"),
        P(("groups", "replica"), "sx"),
        P(("groups", "replica"), "sx"),
        P(("groups", "sx"), None, None),
    )
    return jax.shard_map(
        shards,
        mesh=mesh,
        in_specs=placed,
        out_specs=(P(("groups", "sx"), "replica", None), P(None, ("groups", "replica"), "sx")),
        check_vma=False,
    )
```

```python
import functools
import math

import jax
import jax.numpy as jnp
from jax import lax
from jax.experimental import pallas as pl
from jax.experimental.pallas import tpu as pltpu
from jax.sharding import PartitionSpec as P

CX = 24
NZ = 64
NY = 480
REACH = 6
BLOCK = 128
BLOCKS = 8
ATOMS_DEV = 1024
SPAN = CX + 2 * REACH
LAP = 2 * REACH
LANES = 512
FIELDS = 5
HALF_LOG2E = 0.5 * math.log2(math.e)

noise_floor = 0.05


def pack_kernel(coords_ref, widths_ref, amplitudes_ref, live_ref, own_ref, sems):
    copies = [
        pltpu.make_async_copy(coords_ref, own_ref.at[pl.ds(0, 3)], sems.at[0]),
        pltpu.make_async_copy(widths_ref, own_ref.at[3], sems.at[1]),
        pltpu.make_async_copy(amplitudes_ref, own_ref.at[4], sems.at[2]),
    ]
    for copy in copies:
        copy.start()
    for copy in copies:
        copy.wait()
    block = lax.broadcasted_iota(jnp.int32, (BLOCKS, BLOCK), 0)
    own_ref[4] = jnp.where(block < live_ref[0, 0], own_ref[4], 0.0)


def live_of(ref, member):
    number = (lax.broadcasted_iota(jnp.int32, (BLOCKS, BLOCK), 0) + 1).astype(jnp.float32)
    return jnp.max(jnp.where(ref[member, 4] != 0.0, number, 0.0)).astype(jnp.int32)


def split(code):
    return lax.shift_right_logical(code, 3), code & 7


def listed(out, count, first, stride, base, live):
    for block in range(first, BLOCKS, stride):
        out[count] = base + block
        count = count + jnp.where(block < live, 1, 0)
    return count


class Tables:
    def __init__(self, zp, zs, atoms_ref):
        self.zp, self.zs, self.atoms_ref = zp, zs, atoms_ref
        self.brick = lax.axis_index("sx")
        self.last_plane = CX * lax.axis_size("sx")
        self.step = lax.broadcasted_iota(jnp.int32, (16, BLOCK), 0).astype(jnp.float32)
        step_z = lax.broadcasted_iota(jnp.int32, (zp, BLOCK), 0)
        self.own_z = (step_z < zs).astype(jnp.float32)
        self.cell_z = (step_z + lax.axis_index("replica") * zs).astype(jnp.float32)

    def fields(self, data):
        frac_x, frac_y, frac_z, width, weight = data
        inv = 1.0 / width
        q = inv * inv
        return frac_x, frac_y, frac_z, q, q * -HALF_LOG2E, weight

    def own_fields(self, member, block):
        return self.fields([self.atoms_ref[member, f, pl.ds(block, 1), :] for f in range(FIELDS)])

    def y(self, out, slopes, frac, power, q):
        base = self.step - NY * frac
        for k in range(NY // 16):
            off = base + float(16 * k)
            value = jnp.exp2(off * off * power)
            out[16 * k : 16 * k + 16, :] = value.astype(jnp.bfloat16)
            if slopes is not None:
                slopes[16 * k : 16 * k + 16, :] = (value * (off * q)).astype(jnp.bfloat16)

    def x(self, frac, power, shift, lower, count, edges):
        cell = lax.broadcasted_iota(jnp.int32, (count, BLOCK), 0) + lower
        off = cell.astype(jnp.float32) - (CX * frac + shift)
        value = jnp.exp2(off * off * power)
        if edges:
            plane = cell + (self.brick * CX - REACH)
            value = jnp.where((plane >= 0) & (plane < self.last_plane), value, 0.0)
        return value, off

    def z(self, frac, power):
        off = self.cell_z - NZ * frac
        value = jnp.exp2(off * off * power)
        return (value if self.zs == self.zp else value * self.own_z), off


def zero_tails(*tables):
    for table in tables:
        table[:, NY:, :] = jnp.zeros((table.shape[0], LANES - NY, BLOCK), jnp.bfloat16)


def splat_kernel(members, zp, zs, sliced, stash, stage, *refs):
    slope = None
    if stage == "own":
        atoms_ref, rho, gy, slope, more_list = refs
    elif stage == "side":
        atoms_ref, near_ref, far_ref, target_ref, _, _, _, rho, gy, slope, *refs = refs
        wanted, gy_side, sides, more_list, side_list, sem = refs
    else:
        atoms_ref, near_ref, far_ref, target_ref, rho, *refs = refs
        wanted, gy, gy_side, sides, more_list, side_list, sem = refs
    brick = lax.axis_index("sx")
    odd = lax.rem(brick, 2)
    inner = (brick > 0) & (brick < lax.axis_size("sx") - 1)

    if stage != "own":
        if sliced:
            z_first = pl.multiple_of(lax.axis_index("replica") * zs, 8)
            source = target_ref.at[:, pl.ds(z_first, zs), :]
        else:
            source = target_ref
        fetch = pltpu.make_async_copy(source, wanted, sem)
        fetch.start()

    def list_own(member, count):
        return listed(more_list, count, 2, 2, member * BLOCKS, live_of(atoms_ref, member))

    def list_sides(member, count):
        base = member * BLOCKS
        sides[member] = near_ref[member]
        sides[members + member] = far_ref[member]
        count = listed(side_list, count, 0, 1, base, live_of(near_ref, member))
        far = jnp.where(inner, live_of(far_ref, member), 0)
        return listed(side_list, count, 0, 1, members * BLOCKS + base, far)

    unroll = members <= 4
    more_count = lax.fori_loop(0, members, list_own, jnp.int32(0), unroll=unroll)
    if stage != "own":
        side_count = lax.fori_loop(0, members, list_sides, jnp.int32(0), unroll=unroll)
        zero_tails(gy_side)
    if stage != "side":
        zero_tails(gy)
    if stage == "own":
        zero_tails(slope)
    tables = Tables(zp, zs, atoms_ref)

    def left_of(scaled, gz, count):
        group = max(1, 16 // zp)
        made = []
        for t in range(0, count, group):
            pieces = [scaled[t + i : t + i + 1] * gz for i in range(group)]
            piece = pieces[0] if group == 1 else jnp.concatenate(pieces, 0)
            made.append(piece.astype(jnp.bfloat16))
        return jnp.concatenate(made, 0)

    def matmul_t(a, b):
        return lax.dot_general(a, b, (((1,), (1,)), ((), ())), preferred_element_type=jnp.float32)

    def own_splat(member, block, part):
        at = [member * BLOCKS + block + half if stash else 2 * part + half for half in range(2)]
        lefts = []
        for half in range(2):
            frac_x, frac_y, frac_z, q, power, weight = tables.own_fields(member, block + half)
            gx, _ = tables.x(frac_x, power, REACH, 0, SPAN, True)
            gz, _ = tables.z(frac_z, power)
            tables.y(gy.at[at[half]], slope.at[at[half]] if stash else None, frac_y, power, q)
            lefts.append(left_of(weight * gx, gz, SPAN))
        return matmul_t(
            jnp.concatenate(lefts, 1),
            jnp.concatenate([gy[at[0]], gy[at[1]]], 1),
        )

    def start_members(step_at, carry):
        for part in range(start_group):
            member = start_group * step_at + part
            rho[member] = own_splat(member, 0, part)
        return carry

    start_group = min(members, 4)
    if stage != "side":
        lax.fori_loop(0, members // start_group, start_members, 0)

    def more_pair(unit, part):
        code = more_list[unit]
        member, block = split(code)
        rho[member] += own_splat(member, block, part)

    def two_pairs(step_at, carry):
        more_pair(2 * step_at, 0)
        more_pair(2 * step_at + 1, 1)
        return carry

    early = jnp.minimum(lax.shift_right_logical(more_count, 1), 2)
    if stage == "own":
        lax.fori_loop(0, early, two_pairs, 0)
        return
    past = 2 * early if stage == "side" else 0

    side_group = gy_side.shape[0]

    def side_units(step_at):
        for part in range(side_group):
            unit = side_group * step_at + part
            code = side_list[jnp.minimum(unit, side_count - 1)]
            place, block = split(code)
            is_near = place < members
            member = jnp.where(is_near, place, place - members)
            above = jnp.where(is_near, 1 - odd, odd)
            block = pl.ds(block, 1)
            keep = jnp.where(unit < side_count, 1.0, 0.0)
            lower = CX * above
            shift = (REACH - CX + 2 * CX * above).astype(jnp.float32)
            frac_x, frac_y, frac_z, q, power, weight = tables.fields(
                [sides[place, f, block, :] for f in range(FIELDS)]
            )
            gx, _ = tables.x(frac_x, power, shift, lower, LAP, False)
            gz, _ = tables.z(frac_z, power)
            tables.y(gy_side.at[part], None, frac_y, power, q)
            side_left = left_of(weight * keep * gx, gz, LAP)
            at = pl.ds(pl.multiple_of(lower * zp, 16), LAP * zp)
            rho[member, at, :] += matmul_t(side_left, gy_side[part])

    def both(step_at, carry):
        more_pair(past + step_at, 0)
        side_units(step_at)
        return carry

    def more_alone(step_at, carry):
        more_pair(past + step_at, 0)
        return carry

    def side_alone(step_at, carry):
        side_units(step_at)
        return carry

    side_steps = (side_count + side_group - 1) // side_group
    shared = jnp.minimum(more_count - past, side_steps)
    lax.fori_loop(0, shared, both, 0)
    lax.fori_loop(shared, more_count - past, more_alone, 0)
    lax.fori_loop(shared, side_steps, side_alone, 0)
    fetch.wait()


def pull_kernel(members, zp, zs, stash, atoms_ref, near_target, far_target, rho, wanted, *rest):
    if stash:
        gy, slope, *rest = rest
        mean_ref, *outs, grad, mean_vmem, pulled, rows, forces, pull_list, sem = rest
    else:
        mean_ref, *outs, grad, mean_vmem, pulled, rows, forces, pull_list, sem, gy, slope = rest
    odd = lax.rem(lax.axis_index("sx"), 2)

    def list_member(member, count):
        return listed(pull_list, count, 0, 1, member * BLOCKS, live_of(atoms_ref, member))

    pull_count = lax.fori_loop(0, members, list_member, jnp.int32(0), unroll=members <= 4)
    forces[...] = jnp.zeros_like(forces)
    grad[:, :, NY - 96 :] = jnp.zeros((members, SPAN * zp, LANES - NY + 96), jnp.bfloat16)
    if not stash:
        zero_tails(gy, slope)
    tables = Tables(zp, zs, atoms_ref)

    group = max(1, 16 // zp)

    def gradient(first_plane, goal, means, t, carry):
        at = pl.ds(pl.multiple_of((first_plane + t * group) * zp, 16), group * zp)
        planes = pl.ds(t * group, group)
        here = [rho[m, at, 0:NY] for m in range(members)]
        first = functools.reduce(jnp.add, here)
        second = functools.reduce(jnp.add, [f * f for f in here])
        mean = first * (1.0 / members)
        spread = second * (1.0 / members) - mean * mean
        noise = noise_floor + spread * (1.0 / members)
        guess = pl.reciprocal(noise, approx=True)
        inv = guess * (2.0 - noise * guess)
        pull = (goal[planes].astype(jnp.float32).reshape(group * zp, NY) - mean) * inv
        gain = (inv - pull * pull) * (1.0 / (members * members))
        offset = pull * (-1.0 / members) - gain * mean
        for m in range(members):
            grad[m, at, 0:NY] = (offset + gain * here[m]).astype(jnp.bfloat16)
        if means is not None:
            means[planes] = mean.reshape(group, zp, NY)
        return carry

    for first_plane, goal, means in (
        (REACH, wanted, mean_vmem),
        ((REACH + CX) * (1 - odd), near_target, None),
        ((REACH + CX) * odd, far_target, None),
    ):
        steps = goal.shape[0] // group
        lax.fori_loop(0, steps, functools.partial(gradient, first_plane, goal, means), 0, unroll=3)
    give = pltpu.make_async_copy(mean_vmem, mean_ref, sem)
    give.start()

    pull_group = pulled.shape[0]

    def pull_units(first_unit, units):
        for part in range(units):
            code = pull_list[jnp.minimum(first_unit + part, pull_count - 1)]
            member, block = split(code)
            frac_x, frac_y, frac_z, q, power, weight = tables.own_fields(member, block)
            gx, off_x = tables.x(frac_x, power, REACH, 0, SPAN, True)
            gz, off_z = tables.z(frac_z, power)
            rows[part, 0:SPAN] = gx
            rows[part, SPAN : 2 * SPAN] = gx * off_x * q
            slot = code if stash else part
            if not stash:
                tables.y(gy.at[slot], slope.at[slot], frac_y, power, q)
            got = jnp.dot(
                grad[member], jnp.concatenate([gy[slot], slope[slot]], 1),
                preferred_element_type=jnp.float32,
            )
            sum_x = jnp.zeros((zp, BLOCK), jnp.float32)
            sum_y = jnp.zeros((zp, BLOCK), jnp.float32)
            sum_z = jnp.zeros((zp, BLOCK), jnp.float32)
            for t in range(SPAN):
                plain = got[t * zp : (t + 1) * zp, 0:BLOCK]
                slanted = got[t * zp : (t + 1) * zp, BLOCK:]
                here = rows[part, t : t + 1]
                sum_x += rows[part, SPAN + t : SPAN + t + 1] * plain
                sum_y += here * slanted
                sum_z += here * plain
            at = pl.ds(block, 1)
            forces[member, 0, at] = weight * jnp.sum(sum_x * gz, 0, keepdims=True)
            forces[member, 1, at] = weight * jnp.sum(sum_y * gz, 0, keepdims=True)
            forces[member, 2, at] = weight * jnp.sum(sum_z * (gz * off_z * q), 0, keepdims=True)

    def pull_many(step_at, carry):
        pull_units(pull_group * step_at, pull_group)
        return carry

    def pull_two(step_at, carry):
        pull_units(2 * step_at, 2)
        return carry

    def pull_four(step_at, carry):
        pull_units(4 * step_at, 4)
        return carry

    eights = lax.shift_right_logical(pull_count, 3)
    fours = lax.shift_right_logical(pull_count, 2)
    lax.fori_loop(0, eights, pull_many, 0)
    lax.fori_loop(2 * eights, fours, pull_four, 0)
    lax.fori_loop(2 * fours, lax.shift_right_logical(pull_count + 1, 1), pull_two, 0)
    if len(outs) == 1:
        outs[0][...] = forces[...]
    else:
        for k, out in enumerate(outs):
            out[...] = forces[k]
    give.wait()


def shards(coords, widths, amplitudes, live_blocks, target_map):
    members = lax.axis_size("replica")
    bricks = lax.axis_size("sx")
    rank = lax.axis_index("replica")
    zs = NZ // members
    zp = max(zs, 8)
    sliced = zs % 8 == 0
    few = members <= 4 and members & (members - 1) == 0
    stash = few
    blocks = (BLOCKS, BLOCK)
    vmem = pl.BlockSpec(memory_space=pltpu.VMEM)
    anywhere = pl.BlockSpec(memory_space=pl.ANY)

    target = target_map
    if not sliced:
        part = lax.dynamic_slice_in_dim(target_map, rank * zs, zs, 1)
        target = jnp.pad(part, ((0, 0), (0, zp - zs), (0, 0)))
    hbm = pl.BlockSpec(memory_space=pltpu.HBM)
    own = pl.pallas_call(
        pack_kernel,
        out_shape=jax.ShapeDtypeStruct((FIELDS,) + blocks, jnp.float32),
        in_specs=[hbm] * 3 + [pl.BlockSpec(memory_space=pltpu.SMEM)],
        out_specs=vmem,
        scratch_shapes=[pltpu.SemaphoreType.DMA((3,))],
        compiler_params=pltpu.CompilerParams(vmem_limit_bytes=4 * 1024 * 1024),
        name="pack",
    )(
        *(
            pltpu.with_memory_space_constraint(x, pltpu.HBM)
            for x in (coords.reshape((3,) + blocks), widths.reshape(blocks), amplitudes.reshape(blocks))
        ),
        live_blocks,
    )

    odd = lax.rem(lax.axis_index("sx"), 2)

    def edge(plane):
        z_first = rank * zs if sliced else 0
        block = lax.dynamic_slice(target, (plane, z_first, 0), (REACH, zp, NY))
        return block.astype(jnp.bfloat16)

    near_edge, far_edge = edge((CX - REACH) * (1 - odd)), edge((CX - REACH) * odd)

    def swap(block, pairs):
        return lax.ppermute(block, "sx", pairs + [(b, a) for a, b in pairs])

    near_pairs = [(i, i + 1) for i in range(0, bricks - 1, 2)]
    far_pairs = [(i, i + 1) for i in range(1, bricks - 1, 2)]
    if bricks % 2 == 0 and bricks > 2:
        far_pairs.append((bricks - 1, 0))

    def across(block, k):
        return lax.ppermute(block, "replica", [(i, i ^ k) for i in range(members)])

    if few:
        got = {0: own}
        for k in (2, 3, 1):
            got[k] = across(own, k)
        everyone = jnp.stack([got[k] for k in range(members)])
        everyone, near_edge, far_edge = lax.optimization_barrier((everyone, near_edge, far_edge))
    else:
        everyone = lax.all_gather(own, "replica")
    far, near = swap(everyone, far_pairs), swap(everyone, near_pairs)
    near_edge, far_edge, _ = lax.optimization_barrier((near_edge, far_edge, everyone))
    far_target, near_target = swap(far_edge, far_pairs), swap(near_edge, near_pairs)

    force_shapes = (
        [jax.ShapeDtypeStruct((3,) + blocks, jnp.float32)] * members
        if few
        else [jax.ShapeDtypeStruct((members, 3) + blocks, jnp.float32)]
    )
    table = ((members * BLOCKS if stash else 8), LANES, BLOCK)
    kept = [((members, SPAN * zp, LANES), jnp.float32)] + [(table, jnp.bfloat16)] * (2 if stash else 0)
    goal = jax.ShapeDtypeStruct((CX, zp, NY), jnp.float32)
    lists = [pltpu.SMEM((n * members * BLOCKS + 1,), jnp.int32) for n in (1, 2)]
    work = [
        pltpu.VMEM((6, LANES, BLOCK), jnp.bfloat16),
        pltpu.VMEM((2 * members, FIELDS) + blocks, jnp.float32),
        *lists,
        pltpu.SemaphoreType.DMA,
    ]
    params = pltpu.CompilerParams(vmem_limit_bytes=24 * 1024 * 1024)
    goal_source = pltpu.with_memory_space_constraint(target, pltpu.HBM)
    if few:
        kept = [pltpu.VMEM(*k) for k in kept]
        first = pl.pallas_call(
            functools.partial(splat_kernel, members, zp, zs, sliced, stash, "own"),
            out_shape=kept,
            in_specs=[vmem],
            out_specs=[vmem] * 3,
            scratch_shapes=lists[:1],
            compiler_params=params,
            cost_estimate=pl.CostEstimate(flops=2_000_000_000, bytes_accessed=1_000_000, transcendentals=0),
            name="splat_own",
        )(everyone)
        first = [pltpu.with_memory_space_constraint(x, pltpu.VMEM) for x in first]
        *splat, wanted = pl.pallas_call(
            functools.partial(splat_kernel, members, zp, zs, sliced, stash, "side"),
            out_shape=kept + [goal],
            in_specs=[vmem] * 3 + [hbm] + [vmem] * 3,
            out_specs=[vmem] * 4,
            scratch_shapes=work,
            input_output_aliases={4: 0, 5: 1, 6: 2},
            compiler_params=params,
            cost_estimate=pl.CostEstimate(flops=500_000_000, bytes_accessed=1_000_000, transcendentals=0),
            name="splat_side",
        )(everyone, near, far, goal_source, *first)
        splat.insert(1, wanted)
    else:
        splat = pl.pallas_call(
            functools.partial(splat_kernel, members, zp, zs, sliced, stash, "all"),
            out_shape=[jax.ShapeDtypeStruct(*kept[0]), goal],
            in_specs=[vmem] * 3 + [hbm],
            out_specs=[vmem] * 2,
            scratch_shapes=[pltpu.VMEM(table, jnp.bfloat16)] + work,
            compiler_params=params,
            cost_estimate=pl.CostEstimate(flops=6_000_000_000, bytes_accessed=14_000_000, transcendentals=0),
            name="splat",
        )(everyone, near, far, goal_source)
    mean, *partial = pl.pallas_call(
        functools.partial(pull_kernel, members, zp, zs, stash),
        out_shape=[jax.ShapeDtypeStruct((CX, zp, NY), jnp.float32)] + force_shapes,
        in_specs=[vmem] * (3 + len(splat)),
        out_specs=[anywhere] + [vmem] * len(force_shapes),
        scratch_shapes=[
            pltpu.VMEM((members, SPAN * zp, LANES), jnp.bfloat16),
            pltpu.VMEM((CX, zp, NY), jnp.float32),
            pltpu.VMEM((8, SPAN * zp, 2 * BLOCK), jnp.float32),
            pltpu.VMEM((8, 2 * SPAN, BLOCK), jnp.float32),
            pltpu.VMEM((members, 3) + blocks, jnp.float32),
            pltpu.SMEM((members * BLOCKS + 1,), jnp.int32),
            pltpu.SemaphoreType.DMA,
        ]
        + ([] if stash else [pltpu.VMEM(table, jnp.bfloat16)] * 2),
        compiler_params=pltpu.CompilerParams(vmem_limit_bytes=(24 if stash else 40) * 1024 * 1024),
        cost_estimate=pl.CostEstimate(flops=6_000_000_000, bytes_accessed=14_000_000, transcendentals=0),
        name="pull",
    )(everyone, near_target, far_target, *splat)

    if few:
        forces = partial[0]
        for k in (2, 3, 1):
            forces = forces + across(partial[k], k)
    else:
        forces = lax.psum_scatter(partial[0], "replica", scatter_dimension=0)
    return mean[:, :zs], forces.reshape(3, 1, ATOMS_DEV)


def solution(mesh):
    placed = (
        P(None, ("groups", "replica"), "sx"),
        P(("groups", "replica"), "sx"),
        P(("groups", "replica"), "sx"),
        P(("groups", "replica"), "sx"),
        P(("groups", "sx"), None, None),
    )
    return jax.shard_map(
        shards,
        mesh=mesh,
        in_specs=placed,
        out_specs=(P(("groups", "sx"), "replica", None), P(None, ("groups", "replica"), "sx")),
        check_vma=False,
    )
```
